128 devices in a mesh: stn: 16 (over y, z), blk: 8 (over x, core).
Axes of the slice: x: 4, y: 4, z: 4, core: 2. Of those that a mesh axis runs over, the one named last changes fastest.
Arguments:
- voltages: bfloat16 [2, 512, 524288], P(None, 'stn', 'blk'), may hold values from -12 to 12
- taps: float32 [16, 4096], replicated, may hold values from -1.5 to 1.5
- model_phase: float32 [512], replicated, may hold values from -3.140625 to 3.140625
Outputs:
- gains: float32 [2, 4096, 512], P(None, ('stn', 'blk'))
The draws below stay inside these ranges and needn't reach their ends.
All inputs are finite; a program needn't handle non-finite values.
Results may differ from the reference program's by a relative error of at most 0.0041.
Values may be sent and summed in bfloat16 or wider, within the bound.
A program may use at most 192 MiB of HBM per device.

```python
import math
import jax
import jax.numpy as jnp
from jax import lax

NIN = 512
NCH = 4096
TAPS = 16
SPECTRA = 128
TIME = 524288
ITERS = 4


def draw_voltages(key, part):
    key = jax.random.fold_in(key, 11)
    keys = jax.random.split(key, 4)
    ramp = jnp.arange(TIME, dtype=jnp.float32) / TIME
    common = jax.random.normal(keys[0], (2, TIME), jnp.float32) * 0.3
    magnitude = jnp.exp(jax.random.uniform(keys[1], (NIN,), jnp.float32, math.log(0.5), math.log(2.0)))
    phase = jax.random.uniform(keys[2], (NIN,), jnp.float32, -math.pi, math.pi)
    true_re = (magnitude * jnp.cos(phase))[:, None]
    true_im = (magnitude * jnp.sin(phase))[:, None]
    signal = jnp.stack([true_re * common[0] - true_im * common[1], true_re * common[1] + true_im * common[0]])
    noise = jax.random.normal(keys[3], (2, NIN, TIME), jnp.float32) * 0.7
    envelope = jnp.sqrt(1.0 + 2.0 * ramp)
    return jnp.clip((signal + noise) * envelope, -12.0, 12.0).astype(jnp.bfloat16)


def scatter_about(key, extent, width, limit, held_as=jnp.bfloat16):
    return jnp.clip(width * jax.random.normal(key, extent, jnp.float32), -limit, limit).astype(held_as)


def setup_inputs(seed: int = 0) -> dict:
    splits = jax.random.split(jax.random.key(seed), 4)
    voltages = draw_voltages(jax.random.fold_in(splits[3], 71), 0)
    taps = scatter_about(splits[1], (TAPS, NCH), 0.25, 1.5, jnp.float32)
    model_phase = jnp.clip(jax.random.uniform(splits[2], (NIN,), jnp.float32, -3.140625, 3.140625), -3.140625, 3.140625)
    return {"voltages": voltages, "taps": taps, "model_phase": model_phase}


epsilon = 1e-06

def filter_bank(group, taps):
    wave = group.astype(jnp.float32)
    inputs_here = group.shape[1]
    padding = jnp.zeros((2, inputs_here, (TAPS - 1) * NCH), jnp.float32)
    extended = jnp.concatenate([padding, wave], axis=2).reshape(2, inputs_here, SPECTRA + TAPS - 1, NCH)
    filtered = jnp.zeros((2, inputs_here, SPECTRA, NCH), jnp.float32)
    for tap_index in range(TAPS):
        filtered = filtered + taps[tap_index] * extended[:, :, tap_index:tap_index + SPECTRA, :]
    spectrum = jnp.fft.fft(filtered[0] + 1j * filtered[1], axis=-1)
    spec_re = jnp.real(spectrum)
    spec_im = jnp.imag(spectrum)
    power = lax.optimization_barrier(jnp.sum(spec_re * spec_re + spec_im * spec_im, axis=(1, 2)))
    scale = 1.0 / jnp.sqrt(power / (SPECTRA * NCH) + epsilon)
    return jnp.stack([spec_re * scale[:, None, None], spec_im * scale[:, None, None]]).astype(jnp.bfloat16)

def calibrate(block, model_re, model_im):
    wave = block.astype(jnp.float32)
    wave_re = wave[:, 0]
    wave_im = wave[:, 1]

    def outer(left, right):
        return jnp.einsum('cit,cjt->cij', left, right, precision=lax.Precision.HIGHEST)
    count = wave_re.shape[1]
    offdiag = 1.0 - jnp.eye(count, dtype=jnp.float32)
    vis_re = (outer(wave_re, wave_re) + outer(wave_im, wave_im)) * offdiag
    vis_im = (outer(wave_im, wave_re) - outer(wave_re, wave_im)) * offdiag

    def apply(left, vector):
        return jnp.einsum('cij,cj->ci', left, vector, precision=lax.Precision.HIGHEST)
    gain_re = jnp.ones(wave_re.shape[:2], jnp.float32)
    gain_im = jnp.zeros(wave_re.shape[:2], jnp.float32)
    for iteration in range(1, ITERS + 1):
        weight_re = gain_re * model_re - gain_im * model_im
        weight_im = gain_re * model_im + gain_im * model_re
        prod_re = apply(vis_re, weight_re) - apply(vis_im, weight_im)
        prod_im = apply(vis_re, weight_im) + apply(vis_im, weight_re)
        numer_re = model_re * prod_re + model_im * prod_im
        numer_im = model_re * prod_im - model_im * prod_re
        own_power = weight_re * weight_re + weight_im * weight_im
        denom = lax.optimization_barrier(jnp.sum(own_power, axis=1, keepdims=True)) - own_power + epsilon
        new_re = numer_re / denom
        new_im = numer_im / denom
        if iteration % 2 == 0:
            gain_re = (new_re + gain_re) * 0.5
            gain_im = (new_im + gain_im) * 0.5
        else:
            gain_re = new_re
            gain_im = new_im
    return jnp.stack([gain_re, gain_im], axis=1)

def reference(voltages, taps, model_phase):
    group_size = min(32, NIN)
    groups = voltages.reshape(2, NIN // group_size, group_size, TIME).transpose(1, 0, 2, 3)
    quantized = lax.map(lambda group: filter_bank(group, taps), groups)
    by_channel = quantized.transpose(4, 1, 0, 2, 3).reshape(NCH, 2, NIN, SPECTRA)
    block_size = min(8, NCH)
    blocks = by_channel.reshape(NCH // block_size, block_size, 2, NIN, SPECTRA)
    model_re = jnp.cos(model_phase)
    model_im = jnp.sin(model_phase)
    solved = lax.map(lambda block: calibrate(block, model_re, model_im), blocks)
    return solved.reshape(NCH, 2, NIN).transpose(1, 0, 2)
```

```python
import functools

import jax
import jax.numpy as jnp
import ml_dtypes
import numpy as np
from jax import lax
from jax.experimental import pallas as pl
from jax.experimental.pallas import tpu as pltpu
from jax.sharding import PartitionSpec as P

ITERS = 4
EPS = 1e-06
TAPS = 16
BEFORE = 7
AFTER = 8
LANES = 128
RADIX = 32
F32 = jnp.float32
BF16 = jnp.bfloat16
MESH = pl.DeviceIdType.MESH


def dft_tables(channels):
    b = np.arange(LANES)
    k = np.arange(RADIX)
    turns = (b[None, :, None] * (k[:, None, None] + RADIX * b[None, None, :])) % channels
    angle = -2.0 * np.pi * turns / channels
    cos, sin = np.cos(angle), np.sin(angle)
    table = np.concatenate(
        [np.concatenate([cos, sin], axis=2), np.concatenate([-sin, cos], axis=2)], axis=1
    ).astype(np.float32)
    high = table.astype(ml_dtypes.bfloat16)
    low = (table - high.astype(np.float32)).astype(ml_dtypes.bfloat16)
    return high, low


def times(z, w):
    re, im = z
    c, s = float(w.real), float(w.imag)
    if abs(s) < 1e-12:
        return (re, im) if c > 0 else (-re, -im)
    if abs(c) < 1e-12:
        return (-im, re) if s > 0 else (im, -re)
    if abs(abs(c) - abs(s)) < 1e-12:
        if c > 0 and s < 0:
            return ((re + im) * c, (im - re) * c)
        if c < 0 and s < 0:
            return ((im - re) * -c, (re + im) * c)
    return (re * c - im * s, re * s + im * c)


def add(x, y):
    return (x[0] + y[0], x[1] + y[1])


def sub(x, y):
    return (x[0] - y[0], x[1] - y[1])


def fft(points):
    size = len(points)
    if size == 1:
        return points
    if size == 2:
        return [add(points[0], points[1]), sub(points[0], points[1])]
    if size == 4:
        even = [add(points[0], points[2]), sub(points[0], points[2])]
        odd = [add(points[1], points[3]), sub(points[1], points[3])]
        turned = (odd[1][1], -odd[1][0])
        return [add(even[0], odd[0]), add(even[1], turned), sub(even[0], odd[0]), sub(even[1], turned)]
    if size == 8:
        even, odd = fft(points[0::2]), fft(points[1::2])
        odd = [times(z, np.exp(-2j * np.pi * i / 8)) for i, z in enumerate(odd)]
        return [add(e, o) for e, o in zip(even, odd)] + [sub(e, o) for e, o in zip(even, odd)]
    outer = size // 4
    result = [None] * size
    firsts = []
    for j in range(outer):
        first = fft([points[j + outer * r] for r in range(4)])
        firsts.append([times(z, np.exp(-2j * np.pi * j * u / size)) for u, z in enumerate(first)])
    for u in range(4):
        second = fft([firsts[j][u] for j in range(outer)])
        for v in range(outer):
            result[u + 4 * v] = second[v]
    return result


def filter_kernel(here, keep_ref, prev_ref, own_ref, next_ref, taps_ref, high_ref, low_ref, spec_ref, power_ref, work):
    group = own_ref.shape[1]
    channels = taps_ref.shape[1]

    def fir(a, carry):
        start = pl.multiple_of(a * LANES, LANES)
        keep = keep_ref[0:1, :]
        for p in range(2):
            rows = [taps_ref[k : k + 1, pl.ds(start, LANES)] for k in range(TAPS)]
            sums = [None] * here
            for j in range(here + TAPS - 1):
                if j < BEFORE:
                    source, spot = prev_ref, j
                elif j < BEFORE + here:
                    source, spot = own_ref, j - BEFORE
                else:
                    source, spot = next_ref, j - BEFORE - here
                at = pl.multiple_of(start + spot * channels, LANES)
                sample = source[p, :, pl.ds(at, LANES)].astype(F32)
                for k in range(TAPS):
                    u = j - k
                    if 0 <= u < here:
                        term = sample * rows[k]
                        sums[u] = term if sums[u] is None else sums[u] + term
                if j == BEFORE + here - 1:
                    for u in range(here - AFTER, here):
                        sums[u] = sums[u] * keep
            for u in range(here):
                work[p, a, u] = sums[u]
        return carry

    lax.fori_loop(0, RADIX, fir, 0)

    def turn(s, carry):
        for half in range(group // 8):
            rows = pl.ds(8 * half, 8)
            points = [(work[0, a, s, rows, :], work[1, a, s, rows, :]) for a in range(RADIX)]
            for k, (re, im) in enumerate(fft(points)):
                work[0, k, s, rows, :] = re
                work[1, k, s, rows, :] = im
        return carry

    lax.fori_loop(0, here, turn, 0)
    power_ref[...] = jnp.zeros(power_ref.shape, F32)

    def second(k, carry):
        both = jnp.concatenate(
            [work[0, k].reshape(here * group, LANES), work[1, k].reshape(here * group, LANES)], axis=1
        )
        high = both.astype(BF16)
        low = (both - high.astype(F32)).astype(BF16)
        table = high_ref[k]
        out = jnp.dot(high, table, preferred_element_type=F32)
        out = out + jnp.dot(low, table, preferred_element_type=F32)
        out = out + jnp.dot(high, low_ref[k], preferred_element_type=F32)
        out = out.reshape(here, group, 2 * LANES)
        spec_ref[k] = out
        square = jnp.sum(out * out, axis=0)
        power_ref[...] += square[:, :LANES] + square[:, LANES:]
        return carry

    lax.fori_loop(0, RADIX, second, 0)


def filter_bank(keep, before, voltages, after, taps):
    inputs = voltages.shape[1]
    channels = taps.shape[1]
    here = voltages.shape[2] // channels
    group = 16
    high, low = dft_tables(channels)
    whole = lambda *shape: pl.BlockSpec(shape, lambda g: (0,) * len(shape), pipeline_mode=pl.Buffered(1))
    part = lambda count: pl.BlockSpec((2, group, count * channels), lambda g: (0, g, 0))
    return pl.pallas_call(
        functools.partial(filter_kernel, here),
        grid=(inputs // group,),
        in_specs=[
            whole(8, LANES),
            part(BEFORE),
            part(here),
            part(AFTER),
            whole(*taps.shape),
            whole(*high.shape),
            whole(*low.shape),
        ],
        out_specs=[
            pl.BlockSpec((RADIX, here, group, 2 * LANES), lambda g: (0, 0, g, 0)),
            pl.BlockSpec((group, LANES), lambda g: (g, 0)),
        ],
        out_shape=[
            jax.ShapeDtypeStruct((RADIX, here, inputs, 2 * LANES), F32),
            jax.ShapeDtypeStruct((inputs, LANES), F32),
        ],
        scratch_shapes=[pltpu.VMEM((2, RADIX, here, group, LANES), F32)],
        compiler_params=pltpu.CompilerParams(vmem_limit_bytes=60 * 2**20),
        name="filter_bank",
    )(keep, before, voltages, after, taps, jnp.asarray(high), jnp.asarray(low))


def solve_kernel(
    stations, blocks,
    spec_ref, scale_ref, model_ref, first_ref,
    out_ref,
    quant, stage, weights, self_power, back_wide, back_narrow, sum_out, sum_in, norm_out, norm_in, gain, rows_ref,
    stage_sem, back_s, back_r, total_s, total_r, sum_s, sum_r, weight_s, weight_r, norm_s, norm_r,
):
    stn, blk = lax.axis_index("stn"), lax.axis_index("blk")
    here, inputs = spec_ref.shape[1], spec_ref.shape[2]
    chunk = RADIX // stations
    quad = RADIX // blocks
    per = quad // chunk

    def peer_stn(offset):
        return lax.rem(stn + offset, stations)

    def peer_blk(offset):
        return lax.rem(blk + offset, blocks)

    barrier = pltpu.get_barrier_semaphore()
    for offset in range(1, stations):
        pl.semaphore_signal(barrier, inc=1, device_id=(peer_stn(offset), blk), device_id_type=MESH)
    for offset in range(1, blocks):
        pl.semaphore_signal(barrier, inc=1, device_id=(stn, peer_blk(offset)), device_id_type=MESH)

    def fetch(k, slot):
        return pltpu.make_async_copy(spec_ref.at[k], stage.at[slot], stage_sem.at[slot])

    fetch(0, 0).start()

    def quantize(k, carry):
        slot = lax.rem(k, 2)

        @pl.when(k + 1 < RADIX)
        def _():
            fetch(k + 1, 1 - slot).start()

        fetch(k, slot).wait()
        scale = scale_ref[...]
        total = jnp.zeros((inputs, LANES), F32)
        for s in range(here):
            for p in range(2):
                value = (stage[slot, s, :, p * LANES : (p + 1) * LANES] * scale).astype(BF16)
                quant[k, p, s] = value
                wide = value.astype(F32)
                total = total + wide * wide
        self_power[k] = total
        return carry

    lax.fori_loop(0, RADIX, quantize, 0)

    def begin(m, carry):
        gain[m, 0] = jnp.ones((inputs, LANES), F32)
        gain[m, 1] = jnp.zeros((inputs, LANES), F32)
        return carry

    lax.fori_loop(0, quad, begin, 0)

    pl.semaphore_wait(barrier, stations + blocks - 2)

    def back_parts(turn):
        return [(back_wide if turn == 0 else back_narrow).at[n] for n in range(3)]

    def back_copy(turn, c, sender):
        back_out, back_in, _ = back_parts(turn)
        return pltpu.make_async_remote_copy(
            src_ref=back_out.at[c], dst_ref=back_in.at[sender], send_sem=back_s.at[c], recv_sem=back_r.at[sender],
            device_id=(c, blk), device_id_type=MESH,
        )

    def total_copy(turn, c, owner):
        _, _, back_sum = back_parts(turn)
        return pltpu.make_async_remote_copy(
            src_ref=back_sum.at[owner], dst_ref=back_sum.at[owner], send_sem=total_s.at[c], recv_sem=total_r.at[owner],
            device_id=(c, blk), device_id_type=MESH,
        )

    def sum_copy(r, sender):
        return pltpu.make_async_remote_copy(
            src_ref=sum_out.at[r], dst_ref=sum_in.at[sender], send_sem=sum_s.at[r], recv_sem=sum_r.at[sender],
            device_id=(stn, r), device_id_type=MESH,
        )

    def weight_copy(r, owner):
        part = weights.at[pl.ds(owner * quad, quad)]
        return pltpu.make_async_remote_copy(
            src_ref=part, dst_ref=part, send_sem=weight_s.at[r], recv_sem=weight_r.at[owner],
            device_id=(stn, r), device_id_type=MESH,
        )

    def norm_copy(turn, c, sender):
        return pltpu.make_async_remote_copy(
            src_ref=norm_out.at[turn], dst_ref=norm_in.at[turn, sender],
            send_sem=norm_s.at[turn, c], recv_sem=norm_r.at[turn, sender],
            device_id=(c, blk), device_id_type=MESH,
        )

    def weight(turn, k, p):
        return model_ref[p] if turn == 0 else weights[k, p].astype(F32)

    def down(turn, k, c, j):
        w_re, w_im = weight(turn, k, 0), weight(turn, k, 1)
        for s in range(here):
            q_re, q_im = quant[k, 0, s].astype(F32), quant[k, 1, s].astype(F32)
            rows_ref[s : s + 1, :] = jnp.sum(q_re * w_re + q_im * w_im, axis=0, keepdims=True)
            rows_ref[here + s : here + s + 1, :] = jnp.sum(q_re * w_im - q_im * w_re, axis=0, keepdims=True)
        back_out = back_parts(turn)[0]
        back_out[c, j] = rows_ref[...].astype(back_out.dtype)

    def up(turn, k, r, j):
        c, jj = lax.div(k, chunk), lax.rem(k, chunk)
        rows_ref[...] = back_parts(turn)[2][c, jj].astype(F32)
        h_re = jnp.zeros((inputs, LANES), F32)
        h_im = jnp.zeros((inputs, LANES), F32)
        for s in range(here):
            q_re, q_im = quant[k, 0, s].astype(F32), quant[k, 1, s].astype(F32)
            b_re, b_im = rows_ref[s : s + 1, :], rows_ref[here + s : here + s + 1, :]
            h_re = h_re + (q_re * b_re - q_im * b_im)
            h_im = h_im + (q_re * b_im + q_im * b_re)
        own = self_power[k]
        sum_out[r, j, 0] = (h_re - own * weight(turn, k, 0)).astype(BF16)
        sum_out[r, j, 1] = (h_im - own * weight(turn, k, 1)).astype(BF16)

    for turn in range(ITERS):
        def down_part(o, carry):
            r = peer_blk(o)
            if turn > 0:

                @pl.when(o > 0)
                def _():
                    weight_copy(r, r).wait_recv()

            def one(n, carry):
                c = r * per + n

                def each(j, carry):
                    down(turn, c * chunk + j, c, j)
                    return carry

                lax.fori_loop(0, chunk, each, 0)

                @pl.when(c != stn)
                def _():
                    back_copy(turn, c, stn).start()

                return carry

            return lax.fori_loop(0, per, one, carry)

        lax.fori_loop(0, blocks, down_part, 0)

        def gather(j, carry):
            back_out, back_in, back_sum = back_parts(turn)
            total = back_out[stn, j].astype(F32)

            def more(o, total):
                return total + back_in[peer_stn(o), j].astype(F32)

            back_sum[stn, j] = lax.fori_loop(1, stations, more, total).astype(back_sum.dtype)
            return carry

        def await_back(o, carry):
            c = peer_stn(o)
            back_copy(turn, c, c).wait_recv()
            return carry

        lax.fori_loop(1, stations, await_back, 0)
        lax.fori_loop(0, chunk, gather, 0)

        def send_total(o, carry):
            total_copy(turn, peer_stn(o), stn).start()
            return carry

        lax.fori_loop(1, stations, send_total, 0)

        def up_part(o, carry):
            r = peer_blk(o)
            for n in range(per):
                c = r * per + n

                @pl.when(c != stn)
                def _():
                    total_copy(turn, c, c).wait_recv()

            def each(j, carry):
                up(turn, r * quad + j, r, j)
                return carry

            lax.fori_loop(0, quad, each, 0)

            @pl.when(o < blocks)
            def _():
                sum_copy(r, blk).start()

            return carry

        lax.fori_loop(1, blocks + 1, up_part, 0)

        def settle(o, carry):
            c = peer_stn(o)
            back_copy(turn, c, stn).wait_send()
            total_copy(turn, c, stn).wait_send()
            if turn > 0:
                norm_copy(turn - 1, c, c).wait_recv()
                norm_copy(turn - 1, c, stn).wait_send()
            return carry

        lax.fori_loop(1, stations, settle, 0)

        def await_sum(o, carry):
            r = peer_blk(o)
            sum_copy(r, r).wait_recv()
            if turn > 0:
                weight_copy(r, blk).wait_send()
            return carry

        lax.fori_loop(1, blocks, await_sum, 0)

        if turn > 0:

            def norms(o, total):
                return total + norm_in[turn - 1, peer_stn(o)]

            rows_ref[0:8, :] = lax.fori_loop(1, stations, norms, norm_out[turn - 1])
        else:
            rows_ref[0:8, :] = first_ref[...]

        for m in range(quad):
            total_re = sum_out[blk, m, 0].astype(F32)
            total_im = sum_out[blk, m, 1].astype(F32)

            def more(o, totals):
                r = peer_blk(o)
                return totals[0] + sum_in[r, m, 0].astype(F32), totals[1] + sum_in[r, m, 1].astype(F32)

            total_re, total_im = lax.fori_loop(1, blocks, more, (total_re, total_im))
            m_re, m_im = model_ref[0], model_ref[1]
            g_re, g_im = gain[m, 0], gain[m, 1]
            w_re = g_re * m_re - g_im * m_im
            w_im = g_re * m_im + g_im * m_re
            denom = rows_ref[m : m + 1, :] - (w_re * w_re + w_im * w_im) + EPS
            new_re = (m_re * total_re + m_im * total_im) / denom
            new_im = (m_re * total_im - m_im * total_re) / denom
            if turn % 2 == 1:
                new_re = (new_re + g_re) * 0.5
                new_im = (new_im + g_im) * 0.5
            if turn == ITERS - 1:
                out_ref[m, 0] = new_re
                out_ref[m, 1] = new_im
            else:
                gain[m, 0] = new_re
                gain[m, 1] = new_im
                w_re = new_re * m_re - new_im * m_im
                w_im = new_re * m_im + new_im * m_re
                weights[blk * quad + m, 0] = w_re.astype(BF16)
                weights[blk * quad + m, 1] = w_im.astype(BF16)
                norm_out[turn, m : m + 1, :] = jnp.sum(w_re * w_re + w_im * w_im, axis=0, keepdims=True)

        if turn < ITERS - 1:
            for m in range(quad, 8):
                norm_out[turn, m : m + 1, :] = jnp.zeros((1, LANES), F32)

            def send_weight(o, carry):
                weight_copy(peer_blk(o), blk).start()
                return carry

            lax.fori_loop(1, blocks, send_weight, 0)

            def send_norm(o, carry):
                norm_copy(turn, peer_stn(o), stn).start()
                return carry

            lax.fori_loop(1, stations, send_norm, 0)

        def sent(o, carry):
            sum_copy(peer_blk(o), blk).wait_send()
            return carry

        lax.fori_loop(1, blocks, sent, 0)


def solve(stations, blocks, spec, scale, model, first):
    here, inputs = spec.shape[1], spec.shape[2]
    chunk, quad = RADIX // stations, RADIX // blocks
    vmem = pl.BlockSpec(memory_space=pltpu.VMEM)
    dma = pltpu.SemaphoreType.DMA
    return pl.pallas_call(
        functools.partial(solve_kernel, stations, blocks),
        in_specs=[pl.BlockSpec(memory_space=pl.ANY), vmem, vmem, vmem],
        out_specs=vmem,
        out_shape=jax.ShapeDtypeStruct((quad, 2, inputs, LANES), F32),
        scratch_shapes=[
            pltpu.VMEM((RADIX, 2, here, inputs, LANES), BF16),
            pltpu.VMEM((2, here, inputs, 2 * LANES), F32),
            pltpu.VMEM((RADIX, 2, inputs, LANES), BF16),
            pltpu.VMEM((RADIX, inputs, LANES), F32),
            pltpu.VMEM((3, stations, chunk, 2 * here, LANES), F32),
            pltpu.VMEM((3, stations, chunk, 2 * here, LANES), BF16),
            pltpu.VMEM((blocks, quad, 2, inputs, LANES), BF16),
            pltpu.VMEM((blocks, quad, 2, inputs, LANES), BF16),
            pltpu.VMEM((ITERS - 1, 8, LANES), F32),
            pltpu.VMEM((ITERS - 1, stations, 8, LANES), F32),
            pltpu.VMEM((quad, 2, inputs, LANES), F32),
            pltpu.VMEM((2 * here, LANES), F32),
            dma((2,)),
            dma((stations,)),
            dma((stations,)),
            dma((stations,)),
            dma((stations,)),
            dma((blocks,)),
            dma((blocks,)),
            dma((blocks,)),
            dma((blocks,)),
            dma((ITERS - 1, stations)),
            dma((ITERS - 1, stations)),
        ],
        compiler_params=pltpu.CompilerParams(
            collective_id=0, has_side_effects=True, vmem_limit_bytes=40 * 2**20
        ),
        name="gain_solver",
    )(spec, scale, model, first)


def on_device(stations, blocks, voltages, taps, model_phase):
    inputs = voltages.shape[1]
    channels = taps.shape[1]
    here = voltages.shape[2] // channels
    stn, blk = lax.axis_index("stn"), lax.axis_index("blk")
    before = lax.ppermute(
        voltages[:, :, (here - BEFORE) * channels :], "blk", [(i, i + 1) for i in range(blocks - 1)]
    )
    after = lax.ppermute(
        voltages[:, :, : AFTER * channels], "blk", [(i, (i - 1) % blocks) for i in range(blocks)]
    )
    keep = jnp.where(blk == blocks - 1, 0.0, 1.0) * jnp.ones((8, LANES), F32)
    spec, power = filter_bank(keep, before, voltages, after, taps)
    total = lax.psum(jnp.sum(power, axis=1), "blk")
    scale = 1.0 / jnp.sqrt(total / (here * blocks * channels) + EPS)
    scale = jnp.broadcast_to(scale[:, None], (inputs, LANES))
    model_re, model_im = jnp.cos(model_phase), jnp.sin(model_phase)
    first = jnp.broadcast_to(jnp.sum(model_re * model_re + model_im * model_im), (8, LANES))
    model = lax.dynamic_slice_in_dim(jnp.stack([model_re, model_im]), stn * inputs, inputs, axis=1)
    model = jnp.broadcast_to(model[:, :, None], (2, inputs, LANES))
    gains = solve(stations, blocks, spec, scale, model, first)
    quad = RADIX // blocks
    moved = lax.all_to_all(
        gains.reshape(quad * 2 * inputs, LANES).T, ("stn", "blk"), split_axis=0, concat_axis=0, tiled=True
    )
    lanes = LANES // (stations * blocks)
    moved = moved.reshape(stations, blocks, lanes, quad, 2, inputs).transpose(4, 2, 1, 3, 0, 5)
    return moved.reshape(2, lanes * RADIX, stations * inputs)


def solution(mesh):
    stations, blocks = mesh.shape["stn"], mesh.shape["blk"]
    in_specs = (P(None, "stn", "blk"), P(), P())
    out_specs = P(None, ("stn", "blk"), None)
    return jax.shard_map(
        functools.partial(on_device, stations, blocks),
        mesh=mesh, in_specs=in_specs, out_specs=out_specs, check_vma=False,
    )
```

```python
import functools

import jax
import jax.numpy as jnp
import ml_dtypes
import numpy as np
from jax import lax
from jax.experimental import pallas as pl
from jax.experimental.pallas import tpu as pltpu
from jax.sharding import PartitionSpec as P

ITERS = 4
EPS = 1e-06
TAPS = 16
BEFORE = 7
AFTER = 8
LANES = 128
GROUP = 16
RADIX = 32
F32 = jnp.float32
BF16 = jnp.bfloat16
MESH = pl.DeviceIdType.MESH


def dft_tables(channels):
    b = np.arange(LANES)
    k = np.arange(RADIX)
    turns = (b[None, :, None] * (k[:, None, None] + RADIX * b[None, None, :])) % channels
    angle = -2.0 * np.pi * turns / channels
    cos, sin = np.cos(angle), np.sin(angle)
    table = np.concatenate(
        [np.concatenate([cos, sin], axis=2), np.concatenate([-sin, cos], axis=2)], axis=1
    ).astype(np.float32)
    high = table.astype(ml_dtypes.bfloat16)
    low = (table - high.astype(np.float32)).astype(ml_dtypes.bfloat16)
    return high, low


def times(z, w):
    re, im = z
    c, s = float(w.real), float(w.imag)
    if abs(s) < 1e-12:
        return (re, im) if c > 0 else (-re, -im)
    if abs(c) < 1e-12:
        return (-im, re) if s > 0 else (im, -re)
    if abs(abs(c) - abs(s)) < 1e-12:
        if c > 0 and s < 0:
            return ((re + im) * c, (im - re) * c)
        if c < 0 and s < 0:
            return ((im - re) * -c, (re + im) * c)
    return (re * c - im * s, re * s + im * c)


def add(x, y):
    return (x[0] + y[0], x[1] + y[1])


def sub(x, y):
    return (x[0] - y[0], x[1] - y[1])


def fft(points):
    size = len(points)
    if size == 1:
        return points
    if size == 2:
        return [add(points[0], points[1]), sub(points[0], points[1])]
    if size == 4:
        even = [add(points[0], points[2]), sub(points[0], points[2])]
        odd = [add(points[1], points[3]), sub(points[1], points[3])]
        turned = (odd[1][1], -odd[1][0])
        return [add(even[0], odd[0]), add(even[1], turned), sub(even[0], odd[0]), sub(even[1], turned)]
    if size == 8:
        even, odd = fft(points[0::2]), fft(points[1::2])
        odd = [times(z, np.exp(-2j * np.pi * i / 8)) for i, z in enumerate(odd)]
        return [add(e, o) for e, o in zip(even, odd)] + [sub(e, o) for e, o in zip(even, odd)]
    outer = size // 4
    result = [None] * size
    firsts = []
    for j in range(outer):
        first = fft([points[j + outer * r] for r in range(4)])
        firsts.append([times(z, np.exp(-2j * np.pi * j * u / size)) for u, z in enumerate(first)])
    for u in range(4):
        second = fft([firsts[j][u] for j in range(outer)])
        for v in range(outer):
            result[u + 4 * v] = second[v]
    return result


def correlator_kernel(
    stations, blocks,
    volt_ref, high_hbm, low_hbm, keep_ref, taps_ref, model_ref, first_ref,
    out_ref,
    own, prev, following, work, high_ref, low_ref, power_out, power_in, scale_ref,
    quant, weights, self_power, back_wide, back_narrow, sum_out, sum_in, norm_out, norm_in, gain, rows_ref,
    own_sem, table_sem, halo_s, halo_r, power_s, power_r, back_s, back_r, total_s, total_r, sum_s, sum_r, weight_s, weight_r, norm_s, norm_r,
):
    stn, blk = lax.axis_index("stn"), lax.axis_index("blk")
    channels = taps_ref.shape[1]
    inputs = volt_ref.shape[1]
    here = volt_ref.shape[2] // channels
    groups = inputs // GROUP
    chunk = RADIX // stations
    quad = RADIX // blocks
    per = quad // chunk

    def peer_stn(offset):
        return lax.rem(stn + offset, stations)

    def peer_blk(offset):
        return lax.rem(blk + offset, blocks)

    barrier = pltpu.get_barrier_semaphore()
    for offset in range(1, stations):
        pl.semaphore_signal(barrier, inc=1, device_id=(peer_stn(offset), blk), device_id_type=MESH)
    for offset in range(1, blocks):
        pl.semaphore_signal(barrier, inc=1, device_id=(stn, peer_blk(offset)), device_id_type=MESH)

    def rows_of(g):
        return pl.ds(pl.multiple_of(g * GROUP, GROUP), GROUP)

    def own_copy(g):
        return pltpu.make_async_copy(volt_ref.at[:, rows_of(g), :], own.at[:, rows_of(g), :], own_sem.at[g])

    def table_copy(n):
        pair = ((high_hbm, high_ref), (low_hbm, low_ref))[n]
        return pltpu.make_async_copy(*pair, table_sem.at[n])

    def forward(g):
        return pltpu.make_async_remote_copy(
            src_ref=volt_ref.at[:, rows_of(g), pl.ds((here - BEFORE) * channels, BEFORE * channels)],
            dst_ref=prev.at[:, rows_of(g), :], send_sem=halo_s.at[0, g], recv_sem=halo_r.at[0, g],
            device_id=(stn, peer_blk(1)), device_id_type=MESH,
        )

    def backward(g):
        return pltpu.make_async_remote_copy(
            src_ref=volt_ref.at[:, rows_of(g), pl.ds(0, AFTER * channels)],
            dst_ref=following.at[:, rows_of(g), :], send_sem=halo_s.at[1, g], recv_sem=halo_r.at[1, g],
            device_id=(stn, peer_blk(blocks - 1)), device_id_type=MESH,
        )

    for g in range(groups):
        own_copy(g).start()
    for n in range(2):
        table_copy(n).start()
    pl.semaphore_wait(barrier, stations + blocks - 2)
    for g in range(groups):

        @pl.when(blk < blocks - 1)
        def _():
            forward(g).start()

        backward(g).start()

    @pl.when(blk == 0)
    def _():
        def clear(j, carry):
            at = pl.ds(pl.multiple_of(j * channels, channels), channels)
            for p in range(2):
                prev[p, :, at] = jnp.zeros((inputs, channels), BF16)
            return carry

        lax.fori_loop(0, BEFORE, clear, 0)

    def tap_rows(start):
        return [taps_ref[k : k + 1, pl.ds(start, LANES)] for k in range(TAPS)]

    def accumulate(sums, source, g, p, start, first, count, rows):
        for j in range(first, first + count):
            at = pl.multiple_of(start + (j - first) * channels, LANES)
            sample = source[p, rows_of(g), pl.ds(at, LANES)].astype(F32)
            for k in range(TAPS):
                u = j - k
                if 0 <= u < here:
                    term = sample * rows[k]
                    sums[u] = term if sums[u] is None else sums[u] + term

    def filter_own(g, carry):
        own_copy(g).wait()

        def part(a, carry):
            start = pl.multiple_of(a * LANES, LANES)
            rows = tap_rows(start)
            for p in range(2):
                sums = [None] * here
                accumulate(sums, own, g, p, start, BEFORE, here, rows)
                for u in range(here):
                    work[p, a, u, rows_of(g), :] = sums[u] if u < here - AFTER else sums[u] * keep_ref[0:1, :]
            return carry

        return lax.fori_loop(0, RADIX, part, carry)

    lax.fori_loop(0, groups, filter_own, 0)
    for n in range(2):
        table_copy(n).wait()

    def transform(g, carry):
        @pl.when(blk > 0)
        def _():
            forward(g).wait_recv()

        backward(g).wait_recv()

        def part(a, carry):
            start = pl.multiple_of(a * LANES, LANES)
            rows = tap_rows(start)
            for p in range(2):
                sums = [work[p, a, u, rows_of(g), :] for u in range(here)]
                accumulate(sums, prev, g, p, start, 0, BEFORE, rows)
                accumulate(sums, following, g, p, start, BEFORE + here, AFTER, rows)
                for u in range(here):
                    work[p, a, u, rows_of(g), :] = sums[u]
            return carry

        lax.fori_loop(0, RADIX, part, 0)

        def turn(s, carry):
            for half in range(GROUP // 8):
                rows = pl.ds(pl.multiple_of(g * GROUP + 8 * half, 8), 8)
                points = [(work[0, a, s, rows, :], work[1, a, s, rows, :]) for a in range(RADIX)]
                for k, (re, im) in enumerate(fft(points)):
                    work[0, k, s, rows, :] = re
                    work[1, k, s, rows, :] = im
            return carry

        lax.fori_loop(0, here, turn, 0)

        def second(k, total):
            both = jnp.concatenate(
                [work[p, k, :, rows_of(g), :].reshape(here * GROUP, LANES) for p in range(2)], axis=1
            )
            high = both.astype(BF16)
            low = (both - high.astype(F32)).astype(BF16)
            table = high_ref[k]
            out = jnp.dot(high, table, preferred_element_type=F32)
            out = out + jnp.dot(low, table, preferred_element_type=F32)
            out = out + jnp.dot(high, low_ref[k], preferred_element_type=F32)
            out = out.reshape(here, GROUP, 2 * LANES)
            work[0, k, :, rows_of(g), :] = out[:, :, :LANES]
            work[1, k, :, rows_of(g), :] = out[:, :, LANES:]
            square = jnp.sum(out * out, axis=0)
            return total + square[:, :LANES] + square[:, LANES:]

        total = lax.fori_loop(0, RADIX, second, jnp.zeros((GROUP, LANES), F32))
        power_out[rows_of(g), :] = jnp.broadcast_to(jnp.sum(total, axis=1, keepdims=True), (GROUP, LANES))
        return carry

    lax.fori_loop(0, groups, transform, 0)

    def power_copy(r, sender):
        return pltpu.make_async_remote_copy(
            src_ref=power_out, dst_ref=power_in.at[sender], send_sem=power_s.at[r], recv_sem=power_r.at[sender],
            device_id=(stn, r), device_id_type=MESH,
        )

    for offset in range(1, blocks):
        power_copy(peer_blk(offset), blk).start()
    power = power_out[...]
    for offset in range(1, blocks):
        r = peer_blk(offset)
        power_copy(r, r).wait_recv()
        power = power + power_in[r]
    scale_ref[...] = 1.0 / jnp.sqrt(power / (here * blocks * channels) + EPS)
    for offset in range(1, blocks):
        power_copy(peer_blk(offset), blk).wait_send()
    for g in range(groups):

        @pl.when(blk < blocks - 1)
        def _():
            forward(g).wait_send()

        backward(g).wait_send()

    def quantize(k):
        scale = scale_ref[...]
        total = jnp.zeros((inputs, LANES), F32)
        for s in range(here):
            for p in range(2):
                value = (work[p, k, s] * scale).astype(BF16)
                quant[k, p, s] = value
                wide = value.astype(F32)
                total = total + wide * wide
        self_power[k] = total

    def begin(m, carry):
        gain[m, 0] = jnp.ones((inputs, LANES), F32)
        gain[m, 1] = jnp.zeros((inputs, LANES), F32)
        return carry

    lax.fori_loop(0, quad, begin, 0)

    def back_parts(turn):
        return [(back_wide if turn == 0 else back_narrow).at[n] for n in range(3)]

    def back_copy(turn, c, sender):
        back_out, back_in, _ = back_parts(turn)
        return pltpu.make_async_remote_copy(
            src_ref=back_out.at[c], dst_ref=back_in.at[sender], send_sem=back_s.at[c], recv_sem=back_r.at[sender],
            device_id=(c, blk), device_id_type=MESH,
        )

    def total_copy(turn, c, owner):
        _, _, back_sum = back_parts(turn)
        return pltpu.make_async_remote_copy(
            src_ref=back_sum.at[owner], dst_ref=back_sum.at[owner], send_sem=total_s.at[c], recv_sem=total_r.at[owner],
            device_id=(c, blk), device_id_type=MESH,
        )

    def sum_copy(r, sender):
        return pltpu.make_async_remote_copy(
            src_ref=sum_out.at[r], dst_ref=sum_in.at[sender], send_sem=sum_s.at[r], recv_sem=sum_r.at[sender],
            device_id=(stn, r), device_id_type=MESH,
        )

    def weight_copy(r, owner):
        part = weights.at[pl.ds(owner * quad, quad)]
        return pltpu.make_async_remote_copy(
            src_ref=part, dst_ref=part, send_sem=weight_s.at[r], recv_sem=weight_r.at[owner],
            device_id=(stn, r), device_id_type=MESH,
        )

    def norm_copy(turn, c, sender):
        return pltpu.make_async_remote_copy(
            src_ref=norm_out.at[turn], dst_ref=norm_in.at[turn, sender],
            send_sem=norm_s.at[turn, c], recv_sem=norm_r.at[turn, sender],
            device_id=(c, blk), device_id_type=MESH,
        )

    def weight(turn, k, p):
        return model_ref[p] if turn == 0 else weights[k, p].astype(F32)

    def down(turn, k, c, j):
        w_re, w_im = weight(turn, k, 0), weight(turn, k, 1)
        for s in range(here):
            q_re, q_im = quant[k, 0, s].astype(F32), quant[k, 1, s].astype(F32)
            rows_ref[s : s + 1, :] = jnp.sum(q_re * w_re + q_im * w_im, axis=0, keepdims=True)
            rows_ref[here + s : here + s + 1, :] = jnp.sum(q_re * w_im - q_im * w_re, axis=0, keepdims=True)
        back_out = back_parts(turn)[0]
        back_out[c, j] = rows_ref[...].astype(back_out.dtype)

    def up(turn, k, r, j):
        c, jj = lax.div(k, chunk), lax.rem(k, chunk)
        rows_ref[...] = back_parts(turn)[2][c, jj].astype(F32)
        h_re = jnp.zeros((inputs, LANES), F32)
        h_im = jnp.zeros((inputs, LANES), F32)
        for s in range(here):
            q_re, q_im = quant[k, 0, s].astype(F32), quant[k, 1, s].astype(F32)
            b_re, b_im = rows_ref[s : s + 1, :], rows_ref[here + s : here + s + 1, :]
            h_re = h_re + (q_re * b_re - q_im * b_im)
            h_im = h_im + (q_re * b_im + q_im * b_re)
        own = self_power[k]
        sum_out[r, j, 0] = (h_re - own * weight(turn, k, 0)).astype(BF16)
        sum_out[r, j, 1] = (h_im - own * weight(turn, k, 1)).astype(BF16)

    for turn in range(ITERS):
        def down_part(o, carry):
            r = peer_blk(o)
            if turn > 0:

                @pl.when(o > 0)
                def _():
                    weight_copy(r, r).wait_recv()

            def one(n, carry):
                c = r * per + n

                def each(j, carry):
                    if turn == 0:
                        quantize(c * chunk + j)
                    down(turn, c * chunk + j, c, j)
                    return carry

                lax.fori_loop(0, chunk, each, 0)

                @pl.when(c != stn)
                def _():
                    back_copy(turn, c, stn).start()

                return carry

            return lax.fori_loop(0, per, one, carry)

        lax.fori_loop(0, blocks, down_part, 0)

        def gather(j, carry):
            back_out, back_in, back_sum = back_parts(turn)
            total = back_out[stn, j].astype(F32)

            def more(o, total):
                return total + back_in[peer_stn(o), j].astype(F32)

            back_sum[stn, j] = lax.fori_loop(1, stations, more, total).astype(back_sum.dtype)
            return carry

        def await_back(o, carry):
            c = peer_stn(o)
            back_copy(turn, c, c).wait_recv()
            return carry

        lax.fori_loop(1, stations, await_back, 0)
        lax.fori_loop(0, chunk, gather, 0)

        def send_total(o, carry):
            total_copy(turn, peer_stn(o), stn).start()
            return carry

        lax.fori_loop(1, stations, send_total, 0)

        def up_part(o, carry):
            r = peer_blk(o)
            for n in range(per):
                c = r * per + n

                @pl.when(c != stn)
                def _():
                    total_copy(turn, c, c).wait_recv()

            def each(j, carry):
                up(turn, r * quad + j, r, j)
                return carry

            lax.fori_loop(0, quad, each, 0)

            @pl.when(o < blocks)
            def _():
                sum_copy(r, blk).start()

            return carry

        lax.fori_loop(1, blocks + 1, up_part, 0)

        def settle(o, carry):
            c = peer_stn(o)
            back_copy(turn, c, stn).wait_send()
            total_copy(turn, c, stn).wait_send()
            if turn > 0:
                norm_copy(turn - 1, c, c).wait_recv()
                norm_copy(turn - 1, c, stn).wait_send()
            return carry

        lax.fori_loop(1, stations, settle, 0)

        def await_sum(o, carry):
            r = peer_blk(o)
            sum_copy(r, r).wait_recv()
            if turn > 0:
                weight_copy(r, blk).wait_send()
            return carry

        lax.fori_loop(1, blocks, await_sum, 0)

        if turn > 0:

            def norms(o, total):
                return total + norm_in[turn - 1, peer_stn(o)]

            rows_ref[0:8, :] = lax.fori_loop(1, stations, norms, norm_out[turn - 1])
        else:
            rows_ref[0:8, :] = first_ref[...]

        for m in range(quad):
            total_re = sum_out[blk, m, 0].astype(F32)
            total_im = sum_out[blk, m, 1].astype(F32)

            def more(o, totals):
                r = peer_blk(o)
                return totals[0] + sum_in[r, m, 0].astype(F32), totals[1] + sum_in[r, m, 1].astype(F32)

            total_re, total_im = lax.fori_loop(1, blocks, more, (total_re, total_im))
            m_re, m_im = model_ref[0], model_ref[1]
            g_re, g_im = gain[m, 0], gain[m, 1]
            w_re = g_re * m_re - g_im * m_im
            w_im = g_re * m_im + g_im * m_re
            denom = rows_ref[m : m + 1, :] - (w_re * w_re + w_im * w_im) + EPS
            new_re = (m_re * total_re + m_im * total_im) / denom
            new_im = (m_re * total_im - m_im * total_re) / denom
            if turn % 2 == 1:
                new_re = (new_re + g_re) * 0.5
                new_im = (new_im + g_im) * 0.5
            if turn == ITERS - 1:
                out_ref[m, 0] = new_re
                out_ref[m, 1] = new_im
            else:
                gain[m, 0] = new_re
                gain[m, 1] = new_im
                w_re = new_re * m_re - new_im * m_im
                w_im = new_re * m_im + new_im * m_re
                weights[blk * quad + m, 0] = w_re.astype(BF16)
                weights[blk * quad + m, 1] = w_im.astype(BF16)
                norm_out[turn, m : m + 1, :] = jnp.sum(w_re * w_re + w_im * w_im, axis=0, keepdims=True)

        if turn < ITERS - 1:
            for m in range(quad, 8):
                norm_out[turn, m : m + 1, :] = jnp.zeros((1, LANES), F32)

            def send_weight(o, carry):
                weight_copy(peer_blk(o), blk).start()
                return carry

            lax.fori_loop(1, blocks, send_weight, 0)

            def send_norm(o, carry):
                norm_copy(turn, peer_stn(o), stn).start()
                return carry

            lax.fori_loop(1, stations, send_norm, 0)

        def sent(o, carry):
            sum_copy(peer_blk(o), blk).wait_send()
            return carry

        lax.fori_loop(1, blocks, sent, 0)


def correlate(stations, blocks, voltages, high, low, keep, taps, model, first):
    inputs, channels = voltages.shape[1], taps.shape[1]
    here = voltages.shape[2] // channels
    groups = inputs // GROUP
    chunk, quad = RADIX // stations, RADIX // blocks
    hbm = pl.BlockSpec(memory_space=pl.ANY)
    vmem = pl.BlockSpec(memory_space=pltpu.VMEM)
    dma = pltpu.SemaphoreType.DMA
    return pl.pallas_call(
        functools.partial(correlator_kernel, stations, blocks),
        in_specs=[hbm, hbm, hbm, vmem, vmem, vmem, vmem],
        out_specs=vmem,
        out_shape=jax.ShapeDtypeStruct((quad, 2, inputs, LANES), F32),
        scratch_shapes=[
            pltpu.VMEM((2, inputs, here * channels), BF16),
            pltpu.VMEM((2, inputs, BEFORE * channels), BF16),
            pltpu.VMEM((2, inputs, AFTER * channels), BF16),
            pltpu.VMEM((2, RADIX, here, inputs, LANES), F32),
            pltpu.VMEM(high.shape, BF16),
            pltpu.VMEM(low.shape, BF16),
            pltpu.VMEM((inputs, LANES), F32),
            pltpu.VMEM((blocks, inputs, LANES), F32),
            pltpu.VMEM((inputs, LANES), F32),
            pltpu.VMEM((RADIX, 2, here, inputs, LANES), BF16),
            pltpu.VMEM((RADIX, 2, inputs, LANES), BF16),
            pltpu.VMEM((RADIX, inputs, LANES), F32),
            pltpu.VMEM((3, stations, chunk, 2 * here, LANES), F32),
            pltpu.VMEM((3, stations, chunk, 2 * here, LANES), BF16),
            pltpu.VMEM((blocks, quad, 2, inputs, LANES), BF16),
            pltpu.VMEM((blocks, quad, 2, inputs, LANES), BF16),
            pltpu.VMEM((ITERS - 1, 8, LANES), F32),
            pltpu.VMEM((ITERS - 1, stations, 8, LANES), F32),
            pltpu.VMEM((quad, 2, inputs, LANES), F32),
            pltpu.VMEM((2 * here, LANES), F32),
            dma((groups,)),
            dma((2,)),
            dma((2, groups)),
            dma((2, groups)),
            dma((blocks,)),
            dma((blocks,)),
            dma((stations,)),
            dma((stations,)),
            dma((stations,)),
            dma((stations,)),
            dma((blocks,)),
            dma((blocks,)),
            dma((blocks,)),
            dma((blocks,)),
            dma((ITERS - 1, stations)),
            dma((ITERS - 1, stations)),
        ],
        compiler_params=pltpu.CompilerParams(
            collective_id=0, has_side_effects=True, vmem_limit_bytes=62 * 2**20
        ),
        name="correlator",
    )(voltages, high, low, keep, taps, model, first)


def on_device(stations, blocks, voltages, taps, model_phase):
    inputs = voltages.shape[1]
    channels = taps.shape[1]
    stn, blk = lax.axis_index("stn"), lax.axis_index("blk")
    keep = jnp.where(blk == blocks - 1, 0.0, 1.0) * jnp.ones((8, LANES), F32)
    high, low = dft_tables(channels)
    model_re, model_im = jnp.cos(model_phase), jnp.sin(model_phase)
    first = jnp.broadcast_to(jnp.sum(model_re * model_re + model_im * model_im), (8, LANES))
    model = lax.dynamic_slice_in_dim(jnp.stack([model_re, model_im]), stn * inputs, inputs, axis=1)
    model = jnp.broadcast_to(model[:, :, None], (2, inputs, LANES))
    gains = correlate(stations, blocks, voltages, jnp.asarray(high), jnp.asarray(low), keep, taps, model, first)
    quad = RADIX // blocks
    moved = lax.all_to_all(
        gains.reshape(quad * 2 * inputs, LANES).T, ("stn", "blk"), split_axis=0, concat_axis=0, tiled=True
    )
    lanes = LANES // (stations * blocks)
    moved = moved.reshape(stations, blocks, lanes, quad, 2, inputs).transpose(4, 2, 1, 3, 0, 5)
    return moved.reshape(2, lanes * RADIX, stations * inputs)


def solution(mesh):
    stations, blocks = mesh.shape["stn"], mesh.shape["blk"]
    in_specs = (P(None, "stn", "blk"), P(), P())
    out_specs = P(None, ("stn", "blk"), None)
    return jax.shard_map(
        functools.partial(on_device, stations, blocks),
        mesh=mesh, in_specs=in_specs, out_specs=out_specs, check_vma=False,
    )
```

```python
import functools

import jax
import jax.numpy as jnp
import ml_dtypes
import numpy as np
from jax import lax
from jax.experimental import pallas as pl
from jax.experimental.pallas import tpu as pltpu
from jax.sharding import PartitionSpec as P

ITERS = 4
EPS = 1e-06
TAPS = 16
BEFORE = 7
AFTER = 8
LANES = 128
GROUP = 16
RADIX = 32
F32 = jnp.float32
BF16 = jnp.bfloat16
MESH = pl.DeviceIdType.MESH


def dft_tables(channels):
    b = np.arange(LANES)
    k = np.arange(RADIX)
    turns = (b[None, :, None] * (k[:, None, None] + RADIX * b[None, None, :])) % channels
    angle = -2.0 * np.pi * turns / channels
    cos, sin = np.cos(angle), np.sin(angle)
    table = np.concatenate(
        [np.concatenate([cos, sin], axis=2), np.concatenate([-sin, cos], axis=2)], axis=1
    ).astype(np.float32)
    high = table.astype(ml_dtypes.bfloat16)
    low = (table - high.astype(np.float32)).astype(ml_dtypes.bfloat16)
    return high, low


def times(z, w):
    re, im = z
    c, s = float(w.real), float(w.imag)
    if abs(s) < 1e-12:
        return (re, im) if c > 0 else (-re, -im)
    if abs(c) < 1e-12:
        return (-im, re) if s > 0 else (im, -re)
    if abs(abs(c) - abs(s)) < 1e-12:
        if c > 0 and s < 0:
            return ((re + im) * c, (im - re) * c)
        if c < 0 and s < 0:
            return ((im - re) * -c, (re + im) * c)
    return (re * c - im * s, re * s + im * c)


def add(x, y):
    return (x[0] + y[0], x[1] + y[1])


def sub(x, y):
    return (x[0] - y[0], x[1] - y[1])


def fft(points):
    size = len(points)
    if size == 1:
        return points
    if size == 2:
        return [add(points[0], points[1]), sub(points[0], points[1])]
    if size == 4:
        even = [add(points[0], points[2]), sub(points[0], points[2])]
        odd = [add(points[1], points[3]), sub(points[1], points[3])]
        turned = (odd[1][1], -odd[1][0])
        return [add(even[0], odd[0]), add(even[1], turned), sub(even[0], odd[0]), sub(even[1], turned)]
    if size == 8:
        even, odd = fft(points[0::2]), fft(points[1::2])
        odd = [times(z, np.exp(-2j * np.pi * i / 8)) for i, z in enumerate(odd)]
        return [add(e, o) for e, o in zip(even, odd)] + [sub(e, o) for e, o in zip(even, odd)]
    outer = size // 4
    result = [None] * size
    firsts = []
    for j in range(outer):
        first = fft([points[j + outer * r] for r in range(4)])
        firsts.append([times(z, np.exp(-2j * np.pi * j * u / size)) for u, z in enumerate(first)])
    for u in range(4):
        second = fft([firsts[j][u] for j in range(outer)])
        for v in range(outer):
            result[u + 4 * v] = second[v]
    return result


def correlator_kernel(
    stations, blocks,
    volt_ref, high_hbm, low_hbm, taps_ref, phase_ref, phases_ref,
    out_ref,
    own, prev, following, work, high_ref, low_ref, power_out, power_in, scale_ref, model_ref,
    near, weights, self_power, back_wide, back_narrow, sum_out, sum_in, gain, rows_ref,
    turned, final_out, final_in, last_out, last_in,
    own_sem, table_sem, halo_s, halo_r, power_s, power_r, far_s, far_r, back_s, back_r, total_s, total_r,
    sum_s, sum_r, weight_s, weight_r, final_s, final_r, last_s, last_r,
):
    stn, blk = lax.axis_index("stn"), lax.axis_index("blk")
    channels = taps_ref.shape[1]
    inputs = volt_ref.shape[1]
    here = volt_ref.shape[2] // channels
    groups = inputs // GROUP
    core, place = lax.rem(blk, 2), lax.div(blk, 2)
    partner = blk + 1 - 2 * core
    places = blocks // 2
    half = RADIX // 2
    chunk = half // stations
    quad = half // places
    per = quad // chunk
    spectra = 2 * here
    keep = jnp.where(blk == blocks - 1, 0.0, 1.0)

    def peer_stn(offset):
        return lax.rem(stn + offset, stations)

    def peer_blk(offset):
        return lax.rem(blk + offset, blocks)

    def peer_place(offset):
        return lax.rem(place + offset, places)

    barrier = pltpu.get_barrier_semaphore()
    for offset in range(1, stations):
        pl.semaphore_signal(barrier, inc=1, device_id=(peer_stn(offset), blk), device_id_type=MESH)
    for offset in range(1, blocks):
        pl.semaphore_signal(barrier, inc=1, device_id=(stn, peer_blk(offset)), device_id_type=MESH)

    def rows_of(g):
        return pl.ds(pl.multiple_of(g * GROUP, GROUP), GROUP)

    def own_copy(g):
        return pltpu.make_async_copy(volt_ref.at[:, rows_of(g), :], own.at[:, rows_of(g), :], own_sem.at[g])

    def table_copy(n):
        pair = ((high_hbm, high_ref), (low_hbm, low_ref))[n]
        return pltpu.make_async_copy(*pair, table_sem.at[n])

    def forward(g):
        return pltpu.make_async_remote_copy(
            src_ref=volt_ref.at[:, rows_of(g), pl.ds((here - BEFORE) * channels, BEFORE * channels)],
            dst_ref=prev.at[:, rows_of(g), :], send_sem=halo_s.at[0, g], recv_sem=halo_r.at[0, g],
            device_id=(stn, peer_blk(1)), device_id_type=MESH,
        )

    def backward(g):
        return pltpu.make_async_remote_copy(
            src_ref=volt_ref.at[:, rows_of(g), pl.ds(0, AFTER * channels)],
            dst_ref=following.at[:, rows_of(g), :], send_sem=halo_s.at[1, g], recv_sem=halo_r.at[1, g],
            device_id=(stn, peer_blk(blocks - 1)), device_id_type=MESH,
        )

    for g in range(groups):
        own_copy(g).start()
    for n in range(2):
        table_copy(n).start()
    pl.semaphore_wait(barrier, stations + blocks - 2)
    for g in range(groups):

        @pl.when(blk < blocks - 1)
        def _():
            forward(g).start()

        backward(g).start()

    @pl.when(blk == 0)
    def _():
        def clear(j, carry):
            at = pl.ds(pl.multiple_of(j * channels, channels), channels)
            for p in range(2):
                prev[p, :, at] = jnp.zeros((inputs, channels), BF16)
            return carry

        lax.fori_loop(0, BEFORE, clear, 0)

    def tap_rows(start):
        return [taps_ref[k : k + 1, pl.ds(start, LANES)] for k in range(TAPS)]

    def accumulate(sums, source, g, p, start, first, count, rows):
        for j in range(first, first + count):
            at = pl.multiple_of(start + (j - first) * channels, LANES)
            sample = source[p, rows_of(g), pl.ds(at, LANES)].astype(F32)
            for k in range(TAPS):
                u = j - k
                if 0 <= u < here:
                    term = sample * rows[k]
                    sums[u] = term if sums[u] is None else sums[u] + term

    def filter_own(g, carry):
        own_copy(g).wait()

        def part(a, carry):
            start = pl.multiple_of(a * LANES, LANES)
            rows = tap_rows(start)
            for p in range(2):
                sums = [None] * here
                accumulate(sums, own, g, p, start, BEFORE, here, rows)
                for u in range(here):
                    work[p, a, u, rows_of(g), :] = sums[u] if u < here - AFTER else sums[u] * keep
            return carry

        return lax.fori_loop(0, RADIX, part, carry)

    lax.fori_loop(0, groups, filter_own, 0)
    model_ref[0] = jnp.cos(phase_ref[...])
    model_ref[1] = jnp.sin(phase_ref[...])
    all_re, all_im = jnp.cos(phases_ref[...]), jnp.sin(phases_ref[...])
    first = jnp.sum(all_re * all_re + all_im * all_im)
    rows_ref[...] = jnp.zeros(rows_ref.shape, F32)
    for n in range(2):
        table_copy(n).wait()

    def transform(g, carry):
        @pl.when(blk > 0)
        def _():
            forward(g).wait_recv()

        backward(g).wait_recv()

        def part(a, carry):
            start = pl.multiple_of(a * LANES, LANES)
            rows = tap_rows(start)
            for p in range(2):
                sums = [work[p, a, u, rows_of(g), :] for u in range(here)]
                accumulate(sums, prev, g, p, start, 0, BEFORE, rows)
                accumulate(sums, following, g, p, start, BEFORE + here, AFTER, rows)
                for u in range(here):
                    work[p, a, u, rows_of(g), :] = sums[u]
            return carry

        lax.fori_loop(0, RADIX, part, 0)

        def turn(s, carry):
            for half in range(GROUP // 8):
                rows = pl.ds(pl.multiple_of(g * GROUP + 8 * half, 8), 8)
                points = [(work[0, a, s, rows, :], work[1, a, s, rows, :]) for a in range(RADIX)]
                for k, (re, im) in enumerate(fft(points)):
                    work[0, k, s, rows, :] = re
                    work[1, k, s, rows, :] = im
            return carry

        lax.fori_loop(0, here, turn, 0)

        def second(k, total):
            both = jnp.concatenate(
                [work[p, k, :, rows_of(g), :].reshape(here * GROUP, LANES) for p in range(2)], axis=1
            )
            high = both.astype(BF16)
            low = (both - high.astype(F32)).astype(BF16)
            table = high_ref[k]
            out = jnp.dot(
                jnp.concatenate([high, low, high], axis=1),
                jnp.concatenate([table, table, low_ref[k]], axis=0),
                preferred_element_type=F32,
            )
            out = out.reshape(here, GROUP, 2 * LANES)
            work[0, k, :, rows_of(g), :] = out[:, :, :LANES]
            work[1, k, :, rows_of(g), :] = out[:, :, LANES:]
            square = jnp.sum(out * out, axis=0)
            return total + square[:, :LANES] + square[:, LANES:]

        total = lax.fori_loop(0, RADIX, second, jnp.zeros((GROUP, LANES), F32), unroll=4)
        power_out[rows_of(g), :] = jnp.broadcast_to(jnp.sum(total, axis=1, keepdims=True), (GROUP, LANES))
        return carry

    lax.fori_loop(0, groups, transform, 0)

    def power_copy(r, sender):
        return pltpu.make_async_remote_copy(
            src_ref=power_out, dst_ref=power_in.at[sender], send_sem=power_s.at[r], recv_sem=power_r.at[sender],
            device_id=(stn, r), device_id_type=MESH,
        )

    for offset in range(1, blocks):
        power_copy(peer_blk(offset), blk).start()
    power = power_out[...]
    for offset in range(1, blocks):
        r = peer_blk(offset)
        power_copy(r, r).wait_recv()
        power = power + power_in[r]
    scale_ref[...] = 1.0 / jnp.sqrt(power / (here * blocks * channels) + EPS)
    for offset in range(1, blocks):
        power_copy(peer_blk(offset), blk).wait_send()
    for g in range(groups):

        @pl.when(blk < blocks - 1)
        def _():
            forward(g).wait_send()

        backward(g).wait_send()

    def far_rows(k, s):
        return pl.ds(pl.multiple_of((k * here + s) * LANES, LANES), LANES)

    def far_copy(k):
        part = pl.ds(pl.multiple_of(k * here * LANES, here * LANES), here * LANES)
        return pltpu.make_async_remote_copy(
            src_ref=own.at[:, :, part], dst_ref=following.at[:, :, part], send_sem=far_s.at[k], recv_sem=far_r.at[k],
            device_id=(stn, partner), device_id_type=MESH,
        )

    def hand_over(k, carry):
        scale = scale_ref[...]
        for s in range(here):
            for p in range(2):
                own[p, :, far_rows(k, s)] = (work[p, (1 - core) * half + k, s] * scale).astype(BF16)
        far_copy(k).start()
        return carry

    lax.fori_loop(0, half, hand_over, 0)

    def quantize(k):
        far_copy(k).wait_recv()
        scale = scale_ref[...]
        total = jnp.zeros((inputs, LANES), F32)
        for s in range(here):
            for p in range(2):
                value = (work[p, core * half + k, s] * scale).astype(BF16)
                near[k, p, s] = value
                wide = value.astype(F32)
                wider = following[p, :, far_rows(k, s)].astype(F32)
                total = total + (wide * wide + wider * wider)
        self_power[k] = total

    def sample(k, p, t):
        return (near[k, p, t] if t < here else following[p, :, far_rows(k, t - here)]).astype(F32)

    def begin(m, carry):
        gain[m, 0] = jnp.ones((inputs, LANES), F32)
        gain[m, 1] = jnp.zeros((inputs, LANES), F32)
        return carry

    lax.fori_loop(0, quad, begin, 0)

    def back_parts(turn):
        return [(back_wide if turn == 0 else back_narrow).at[n] for n in range(3)]

    def back_copy(turn, c, sender):
        back_out, back_in, _ = back_parts(turn)
        return pltpu.make_async_remote_copy(
            src_ref=back_out.at[c], dst_ref=back_in.at[sender], send_sem=back_s.at[c], recv_sem=back_r.at[sender],
            device_id=(c, blk), device_id_type=MESH,
        )

    def total_copy(turn, c, owner):
        _, _, back_sum = back_parts(turn)
        return pltpu.make_async_remote_copy(
            src_ref=back_sum.at[owner], dst_ref=back_sum.at[owner], send_sem=total_s.at[c], recv_sem=total_r.at[owner],
            device_id=(c, blk), device_id_type=MESH,
        )

    def sum_copy(r, sender):
        return pltpu.make_async_remote_copy(
            src_ref=sum_out.at[r], dst_ref=sum_in.at[sender], send_sem=sum_s.at[r], recv_sem=sum_r.at[sender],
            device_id=(stn, 2 * r + core), device_id_type=MESH,
        )

    def weight_copy(r, owner):
        part = weights.at[pl.ds(owner * quad, quad)]
        return pltpu.make_async_remote_copy(
            src_ref=part, dst_ref=part, send_sem=weight_s.at[r], recv_sem=weight_r.at[owner],
            device_id=(stn, 2 * r + core), device_id_type=MESH,
        )

    def split_norm(norm):
        high = norm.astype(BF16).astype(F32)
        rows_ref[2 * spectra : 2 * spectra + 1, :] = high
        rows_ref[2 * spectra + 1 : 2 * spectra + 2, :] = norm - high

    def weight(turn, k, p):
        return model_ref[p] if turn == 0 else weights[k, p].astype(F32)

    def down(turn, k, c, j):
        w_re, w_im = weight(turn, k, 0), weight(turn, k, 1)
        for t in range(spectra):
            q_re, q_im = sample(k, 0, t), sample(k, 1, t)
            rows_ref[t : t + 1, :] = jnp.sum(q_re * w_re + q_im * w_im, axis=0, keepdims=True)
            rows_ref[spectra + t : spectra + t + 1, :] = jnp.sum(q_re * w_im - q_im * w_re, axis=0, keepdims=True)
        back_out = back_parts(turn)[0]
        if turn == 0:
            back_out[c, j] = rows_ref[: 2 * spectra, :]
        else:
            split_norm(jnp.sum(w_re * w_re + w_im * w_im, axis=0, keepdims=True))
            back_out[c, j] = rows_ref[...].astype(BF16)

    def up(turn, k, r, j):
        c, jj = lax.div(k, chunk), lax.rem(k, chunk)
        back = back_parts(turn)[2]
        rows_ref[: back.shape[2], :] = back[c, jj].astype(F32)
        h_re = jnp.zeros((inputs, LANES), F32)
        h_im = jnp.zeros((inputs, LANES), F32)
        for t in range(spectra):
            q_re, q_im = sample(k, 0, t), sample(k, 1, t)
            b_re, b_im = rows_ref[t : t + 1, :], rows_ref[spectra + t : spectra + t + 1, :]
            h_re = h_re + (q_re * b_re - q_im * b_im)
            h_im = h_im + (q_re * b_im + q_im * b_re)
        own_power = self_power[k]
        sum_out[r, j, 0] = (h_re - own_power * weight(turn, k, 0)).astype(BF16)
        sum_out[r, j, 1] = (h_im - own_power * weight(turn, k, 1)).astype(BF16)

    for turn in range(ITERS):
        def down_part(o, carry):
            r = peer_place(o)
            if turn > 0:

                @pl.when(o > 0)
                def _():
                    weight_copy(r, r).wait_recv()

            def one(n, carry):
                c = r * per + n

                def each(j, carry):
                    if turn == 0:
                        quantize(c * chunk + j)
                    down(turn, c * chunk + j, c, j)
                    return carry

                lax.fori_loop(0, chunk, each, 0)

                @pl.when(c != stn)
                def _():
                    back_copy(turn, c, stn).start()

                return carry

            return lax.fori_loop(0, per, one, carry)

        lax.fori_loop(0, places, down_part, 0)

        def gather(j, carry):
            back_out, back_in, back_sum = back_parts(turn)
            total = back_out[stn, j].astype(F32)

            def more(o, total):
                return total + back_in[peer_stn(o), j].astype(F32)

            total = lax.fori_loop(1, stations, more, total)
            if turn > 0:
                rows_ref[...] = total
                split_norm(jnp.sum(rows_ref[2 * spectra : 2 * spectra + 2, :], axis=0, keepdims=True))
                total = rows_ref[...]
            back_sum[stn, j] = total.astype(back_sum.dtype)
            return carry

        def await_back(o, carry):
            c = peer_stn(o)
            back_copy(turn, c, c).wait_recv()
            return carry

        lax.fori_loop(1, stations, await_back, 0)
        lax.fori_loop(0, chunk, gather, 0)

        def send_total(o, carry):
            total_copy(turn, peer_stn(o), stn).start()
            return carry

        lax.fori_loop(1, stations, send_total, 0)

        def up_part(o, carry):
            r = peer_place(o)
            for n in range(per):
                c = r * per + n

                @pl.when(c != stn)
                def _():
                    total_copy(turn, c, c).wait_recv()

            def each(j, carry):
                up(turn, r * quad + j, r, j)
                return carry

            lax.fori_loop(0, quad, each, 0)

            @pl.when(o < places)
            def _():
                sum_copy(r, place).start()

            return carry

        lax.fori_loop(1, places + 1, up_part, 0)

        def settle(o, carry):
            c = peer_stn(o)
            back_copy(turn, c, stn).wait_send()
            total_copy(turn, c, stn).wait_send()
            return carry

        lax.fori_loop(1, stations, settle, 0)

        def await_sum(o, carry):
            r = peer_place(o)
            sum_copy(r, r).wait_recv()
            if turn > 0:
                weight_copy(r, place).wait_send()
            return carry

        lax.fori_loop(1, places, await_sum, 0)

        for m in range(quad):
            k = place * quad + m
            total_re = sum_out[place, m, 0].astype(F32)
            total_im = sum_out[place, m, 1].astype(F32)

            def more(o, totals):
                r = peer_place(o)
                return totals[0] + sum_in[r, m, 0].astype(F32), totals[1] + sum_in[r, m, 1].astype(F32)

            total_re, total_im = lax.fori_loop(1, places, more, (total_re, total_im))
            m_re, m_im = model_ref[0], model_ref[1]
            g_re, g_im = gain[m, 0], gain[m, 1]
            w_re = g_re * m_re - g_im * m_im
            w_im = g_re * m_im + g_im * m_re
            if turn == 0:
                norm = first
            else:
                tail = back_narrow[2, lax.div(k, chunk), lax.rem(k, chunk), 2 * spectra :, :].astype(F32)
                norm = tail[0:1, :] + tail[1:2, :]
            denom = norm - (w_re * w_re + w_im * w_im) + EPS
            new_re = (m_re * total_re + m_im * total_im) / denom
            new_im = (m_re * total_im - m_im * total_re) / denom
            if turn % 2 == 1:
                new_re = (new_re + g_re) * 0.5
                new_im = (new_im + g_im) * 0.5
            gain[m, 0] = new_re
            gain[m, 1] = new_im
            if turn < ITERS - 1:
                w_re = new_re * m_re - new_im * m_im
                w_im = new_re * m_im + new_im * m_re
                weights[k, 0] = w_re.astype(BF16)
                weights[k, 1] = w_im.astype(BF16)

        if turn < ITERS - 1:
            def send_weight(o, carry):
                weight_copy(peer_place(o), place).start()
                return carry

            lax.fori_loop(1, places, send_weight, 0)

        def sent(o, carry):
            sum_copy(peer_place(o), place).wait_send()
            return carry

        lax.fori_loop(1, places, sent, 0)

    def handed(k, carry):
        far_copy(k).wait_send()
        return carry

    lax.fori_loop(0, half, handed, 0)

    def final_copy(r, sender):
        return pltpu.make_async_remote_copy(
            src_ref=final_out.at[r], dst_ref=final_in.at[sender], send_sem=final_s.at[r], recv_sem=final_r.at[sender],
            device_id=(stn, r), device_id_type=MESH,
        )

    def last_copy(c, sender):
        return pltpu.make_async_remote_copy(
            src_ref=last_out.at[c], dst_ref=last_in.at[sender], send_sem=last_s.at[c], recv_sem=last_r.at[sender],
            device_id=(c, blk), device_id_type=MESH,
        )

    width = quad * 2 * inputs
    turned[...] = gain[...].reshape(width, LANES).T.reshape(stations, blocks, width)
    for r in range(blocks):
        final_out[r] = turned[:, r, :]
    for offset in range(1, blocks):
        final_copy(peer_blk(offset), blk).start()
    final_in[blk] = final_out[blk]
    for offset in range(1, blocks):
        r = peer_blk(offset)
        final_copy(r, r).wait_recv()
    for c in range(stations):
        last_out[c] = final_in[:, c, :]

    def send_last(o, carry):
        last_copy(peer_stn(o), stn).start()
        return carry

    lax.fori_loop(1, stations, send_last, 0)
    last_in[stn] = last_out[stn]

    def await_last(o, carry):
        c = peer_stn(o)
        last_copy(c, c).wait_recv()
        return carry

    lax.fori_loop(1, stations, await_last, 0)
    span = LANES // inputs
    for m in range(quad):
        for p in range(2):
            at = (2 * m + p) * inputs
            for n in range(stations // span):
                block = jnp.concatenate(
                    [last_in[n * span + i, :, at : at + inputs] for i in range(span)], axis=1
                )
                for r in range(blocks):
                    k = (r % 2) * half + (r // 2) * quad + m
                    out_ref[p, k : k + 1, n * LANES : (n + 1) * LANES] = block[r : r + 1, :]

    for offset in range(1, blocks):
        final_copy(peer_blk(offset), blk).wait_send()

    def sent_last(o, carry):
        last_copy(peer_stn(o), stn).wait_send()
        return carry

    lax.fori_loop(1, stations, sent_last, 0)


def correlate(stations, blocks, voltages, high, low, taps, phase, phases):
    inputs, channels = voltages.shape[1], taps.shape[1]
    here = voltages.shape[2] // channels
    groups = inputs // GROUP
    places, half = blocks // 2, RADIX // 2
    chunk, quad = half // stations, half // places
    rows = 4 * here + 16
    width = quad * 2 * inputs
    hbm = pl.BlockSpec(memory_space=pl.ANY)
    vmem = pl.BlockSpec(memory_space=pltpu.VMEM)
    dma = pltpu.SemaphoreType.DMA
    return pl.pallas_call(
        functools.partial(correlator_kernel, stations, blocks),
        in_specs=[hbm, hbm, hbm, vmem, vmem, vmem],
        out_specs=vmem,
        out_shape=jax.ShapeDtypeStruct((2, RADIX, stations * inputs), F32),
        scratch_shapes=[
            pltpu.VMEM((2, inputs, here * channels), BF16),
            pltpu.VMEM((2, inputs, BEFORE * channels), BF16),
            pltpu.VMEM((2, inputs, AFTER * channels), BF16),
            pltpu.VMEM((2, RADIX, here, inputs, LANES), F32),
            pltpu.VMEM(high.shape, BF16),
            pltpu.VMEM(low.shape, BF16),
            pltpu.VMEM((inputs, LANES), F32),
            pltpu.VMEM((blocks, inputs, LANES), F32),
            pltpu.VMEM((inputs, LANES), F32),
            pltpu.VMEM((2, inputs, LANES), F32),
            pltpu.VMEM((half, 2, here, inputs, LANES), BF16),
            pltpu.VMEM((half, 2, inputs, LANES), BF16),
            pltpu.VMEM((half, inputs, LANES), F32),
            pltpu.VMEM((3, stations, chunk, 4 * here, LANES), F32),
            pltpu.VMEM((3, stations, chunk, rows, LANES), BF16),
            pltpu.VMEM((places, quad, 2, inputs, LANES), BF16),
            pltpu.VMEM((places, quad, 2, inputs, LANES), BF16),
            pltpu.VMEM((quad, 2, inputs, LANES), F32),
            pltpu.VMEM((rows, LANES), F32),
            pltpu.VMEM((stations, blocks, width), F32),
            pltpu.VMEM((blocks, stations, width), F32),
            pltpu.VMEM((blocks, stations, width), F32),
            pltpu.VMEM((stations, blocks, width), F32),
            pltpu.VMEM((stations, blocks, width), F32),
            dma((groups,)),
            dma((2,)),
            dma((2, groups)),
            dma((2, groups)),
            dma((blocks,)),
            dma((blocks,)),
            dma((half,)),
            dma((half,)),
            dma((stations,)),
            dma((stations,)),
            dma((stations,)),
            dma((stations,)),
            dma((places,)),
            dma((places,)),
            dma((places,)),
            dma((places,)),
            dma((blocks,)),
            dma((blocks,)),
            dma((stations,)),
            dma((stations,)),
        ],
        compiler_params=pltpu.CompilerParams(
            collective_id=0, has_side_effects=True, vmem_limit_bytes=62 * 2**20
        ),
        name="correlator",
    )(voltages, high, low, taps, phase, phases)


def on_device(stations, blocks, voltages, taps, model_phase):
    inputs = voltages.shape[1]
    high, low = dft_tables(taps.shape[1])
    phase = lax.dynamic_slice_in_dim(model_phase, lax.axis_index("stn") * inputs, inputs)
    phase = jnp.broadcast_to(phase[:, None], (inputs, LANES))
    phases = model_phase.reshape(-1, LANES)
    return correlate(stations, blocks, voltages, jnp.asarray(high), jnp.asarray(low), taps, phase, phases)


def solution(mesh):
    stations, blocks = mesh.shape["stn"], mesh.shape["blk"]
    in_specs = (P(None, "stn", "blk"), P(), P())
    out_specs = P(None, ("stn", "blk"), None)
    return jax.shard_map(
        functools.partial(on_device, stations, blocks),
        mesh=mesh, in_specs=in_specs, out_specs=out_specs, check_vma=False,
    )
```

```python
import functools

import jax
import jax.numpy as jnp
import ml_dtypes
import numpy as np
from jax import lax
from jax.experimental import pallas as pl
from jax.experimental.pallas import tpu as pltpu
from jax.sharding import PartitionSpec as P

ITERS = 4
EPS = 1e-06
TAPS = 16
BEFORE = 7
AFTER = 8
LANES = 128
GROUP = 16
RADIX = 32
F32 = jnp.float32
BF16 = jnp.bfloat16
MESH = pl.DeviceIdType.MESH


def dft_tables(channels):
    b = np.arange(LANES)
    k = np.arange(RADIX)
    turns = (b[None, :, None] * (k[:, None, None] + RADIX * b[None, None, :])) % channels
    angle = -2.0 * np.pi * turns / channels
    cos, sin = np.cos(angle), np.sin(angle)
    table = np.concatenate(
        [np.concatenate([cos, sin], axis=2), np.concatenate([-sin, cos], axis=2)], axis=1
    ).astype(np.float32)
    high = table.astype(ml_dtypes.bfloat16)
    low = (table - high.astype(np.float32)).astype(ml_dtypes.bfloat16)
    return high, low


def times(z, w):
    re, im = z
    c, s = float(w.real), float(w.imag)
    if abs(s) < 1e-12:
        return (re, im) if c > 0 else (-re, -im)
    if abs(c) < 1e-12:
        return (-im, re) if s > 0 else (im, -re)
    if abs(abs(c) - abs(s)) < 1e-12:
        if c > 0 and s < 0:
            return ((re + im) * c, (im - re) * c)
        if c < 0 and s < 0:
            return ((im - re) * -c, (re + im) * c)
    return (re * c - im * s, re * s + im * c)


def add(x, y):
    return (x[0] + y[0], x[1] + y[1])


def sub(x, y):
    return (x[0] - y[0], x[1] - y[1])


def fft(points):
    size = len(points)
    if size == 1:
        return points
    if size == 2:
        return [add(points[0], points[1]), sub(points[0], points[1])]
    if size == 4:
        even = [add(points[0], points[2]), sub(points[0], points[2])]
        odd = [add(points[1], points[3]), sub(points[1], points[3])]
        turned = (odd[1][1], -odd[1][0])
        return [add(even[0], odd[0]), add(even[1], turned), sub(even[0], odd[0]), sub(even[1], turned)]
    if size == 8:
        even, odd = fft(points[0::2]), fft(points[1::2])
        odd = [times(z, np.exp(-2j * np.pi * i / 8)) for i, z in enumerate(odd)]
        return [add(e, o) for e, o in zip(even, odd)] + [sub(e, o) for e, o in zip(even, odd)]
    outer = size // 4
    result = [None] * size
    firsts = []
    for j in range(outer):
        first = fft([points[j + outer * r] for r in range(4)])
        firsts.append([times(z, np.exp(-2j * np.pi * j * u / size)) for u, z in enumerate(first)])
    for u in range(4):
        second = fft([firsts[j][u] for j in range(outer)])
        for v in range(outer):
            result[u + 4 * v] = second[v]
    return result


def correlator_kernel(
    stations, blocks,
    volt_ref, high_hbm, low_hbm, taps_ref, phases_ref,
    out_ref,
    own, prev, following, work, high_ref, low_ref, power_out, power_in, scale_ref, model_ref,
    near, weights, self_power, back_wide, back_narrow, sum_out, sum_in, gain, rows_ref,
    turned, final_out, final_in, last_out, last_in,
    own_sem, table_sem, halo_s, halo_r, power_s, power_r, far_s, far_r, back_s, back_r, total_s, total_r,
    sum_s, sum_r, weight_s, weight_r, final_s, final_r, last_s, last_r,
):
    stn, blk = lax.axis_index("stn"), lax.axis_index("blk")
    channels = taps_ref.shape[1]
    inputs = volt_ref.shape[1]
    here = volt_ref.shape[2] // channels
    groups = inputs // GROUP
    core, place = lax.rem(blk, 2), lax.div(blk, 2)
    partner = blk + 1 - 2 * core
    places = blocks // 2
    half = RADIX // 2
    chunk = half // stations
    quad = half // places
    per = quad // chunk
    spectra = 2 * here
    keep = jnp.where(blk == blocks - 1, 0.0, 1.0)

    def peer_stn(offset):
        return lax.rem(stn + offset, stations)

    def peer_blk(offset):
        return lax.rem(blk + offset, blocks)

    def peer_place(offset):
        return lax.rem(place + offset, places)

    barrier = pltpu.get_barrier_semaphore()
    for offset in range(1, stations):
        pl.semaphore_signal(barrier, inc=1, device_id=(peer_stn(offset), blk), device_id_type=MESH)
    for offset in range(1, blocks):
        pl.semaphore_signal(barrier, inc=1, device_id=(stn, peer_blk(offset)), device_id_type=MESH)

    def rows_of(g):
        return pl.ds(pl.multiple_of(g * GROUP, GROUP), GROUP)

    def own_copy(g):
        return pltpu.make_async_copy(volt_ref.at[:, rows_of(g), :], own.at[:, rows_of(g), :], own_sem.at[g])

    def table_copy(n):
        pair = ((high_hbm, high_ref), (low_hbm, low_ref))[n]
        return pltpu.make_async_copy(*pair, table_sem.at[n])

    def forward(g):
        return pltpu.make_async_remote_copy(
            src_ref=volt_ref.at[:, rows_of(g), pl.ds((here - BEFORE) * channels, BEFORE * channels)],
            dst_ref=prev.at[:, rows_of(g), :], send_sem=halo_s.at[0, g], recv_sem=halo_r.at[0, g],
            device_id=(stn, peer_blk(1)), device_id_type=MESH,
        )

    def backward(g):
        return pltpu.make_async_remote_copy(
            src_ref=volt_ref.at[:, rows_of(g), pl.ds(0, AFTER * channels)],
            dst_ref=following.at[:, rows_of(g), :], send_sem=halo_s.at[1, g], recv_sem=halo_r.at[1, g],
            device_id=(stn, peer_blk(blocks - 1)), device_id_type=MESH,
        )

    for g in range(groups):
        own_copy(g).start()
    for n in range(2):
        table_copy(n).start()
    pl.semaphore_wait(barrier, stations + blocks - 2)
    for g in range(groups):

        @pl.when(blk < blocks - 1)
        def _():
            forward(g).start()

        backward(g).start()

    @pl.when(blk == 0)
    def _():
        def clear(j, carry):
            at = pl.ds(pl.multiple_of(j * channels, channels), channels)
            for p in range(2):
                prev[p, :, at] = jnp.zeros((inputs, channels), BF16)
            return carry

        lax.fori_loop(0, BEFORE, clear, 0)

    def tap_rows(start):
        return [taps_ref[k : k + 1, pl.ds(start, LANES)] for k in range(TAPS)]

    def accumulate(sums, source, g, p, start, first, count, rows):
        for j in range(first, first + count):
            at = pl.multiple_of(start + (j - first) * channels, LANES)
            sample = source[p, rows_of(g), pl.ds(at, LANES)].astype(F32)
            for k in range(TAPS):
                u = j - k
                if 0 <= u < here:
                    term = sample * rows[k]
                    sums[u] = term if sums[u] is None else sums[u] + term

    def filter_own(g, carry):
        own_copy(g).wait()

        def part(a, carry):
            start = pl.multiple_of(a * LANES, LANES)
            rows = tap_rows(start)
            for p in range(2):
                sums = [None] * here
                accumulate(sums, own, g, p, start, BEFORE, here, rows)
                for u in range(here):
                    work[p, a, u, rows_of(g), :] = sums[u] if u < here - AFTER else sums[u] * keep
            return carry

        return lax.fori_loop(0, RADIX, part, carry)

    lax.fori_loop(0, groups, filter_own, 0)
    span = LANES // inputs
    row = phases_ref[pl.ds(lax.div(stn, span), 1), :]
    lane = lax.broadcasted_iota(jnp.int32, (inputs, LANES), 1)
    wanted = lax.broadcasted_iota(jnp.int32, (inputs, LANES), 0) + lax.rem(stn, span) * inputs
    phase = jnp.sum(jnp.where(lane == wanted, row, 0.0), axis=1, keepdims=True)
    phase = jnp.broadcast_to(phase, (inputs, LANES))
    model_ref[0] = jnp.cos(phase)
    model_ref[1] = jnp.sin(phase)
    all_re, all_im = jnp.cos(phases_ref[...]), jnp.sin(phases_ref[...])
    first = jnp.sum(all_re * all_re + all_im * all_im)
    rows_ref[...] = jnp.zeros(rows_ref.shape, F32)
    for n in range(2):
        table_copy(n).wait()

    def filter_rest(g, low_half, high_half):
        spots = [u for u in range(here) if (u < AFTER and low_half) or (u >= AFTER and high_half)]

        def part(a, total):
            start = pl.multiple_of(a * LANES, LANES)
            rows = tap_rows(start)
            for p in range(2):
                sums = [work[p, a, u, rows_of(g), :] if u in spots else None for u in range(here)]
                if low_half:
                    accumulate(sums, prev, g, p, start, 0, BEFORE, rows)
                if high_half:
                    accumulate(sums, following, g, p, start, BEFORE + here, AFTER, rows)
                for u in spots:
                    work[p, a, u, rows_of(g), :] = sums[u]
                    total = total + sums[u] * sums[u]
            return total

        return lax.fori_loop(0, RADIX, part, jnp.zeros((GROUP, LANES), F32))

    def transform(g, first_spot, count):
        def turn(s, carry):
            for part in range(GROUP // 8):
                rows = pl.ds(g * GROUP + 8 * part, 8)
                points = [(work[0, a, s, rows, :], work[1, a, s, rows, :]) for a in range(RADIX)]
                for k, (re, im) in enumerate(fft(points)):
                    work[0, k, s, rows, :] = re
                    work[1, k, s, rows, :] = im
            return carry

        lax.fori_loop(first_spot, first_spot + count, turn, 0)

        def second(k, carry):
            spots = pl.ds(first_spot, count)
            both = jnp.concatenate(
                [work[p, k, spots, rows_of(g), :].reshape(count * GROUP, LANES) for p in range(2)], axis=1
            )
            high = both.astype(BF16)
            low = (both - high.astype(F32)).astype(BF16)
            table = high_ref[k]
            out = jnp.dot(
                jnp.concatenate([high, low, high], axis=1),
                jnp.concatenate([table, table, low_ref[k]], axis=0),
                preferred_element_type=F32,
            )
            out = out.reshape(count, GROUP, 2 * LANES)
            work[0, k, spots, rows_of(g), :] = out[:, :, :LANES]
            work[1, k, spots, rows_of(g), :] = out[:, :, LANES:]
            return carry

        lax.fori_loop(0, RADIX, second, 0, unroll=4)

    def await_prev(g):
        @pl.when(blk > 0)
        def _():
            forward(g).wait_recv()

    def power_copy(r, sender):
        return pltpu.make_async_remote_copy(
            src_ref=power_out, dst_ref=power_in.at[sender], send_sem=power_s.at[r], recv_sem=power_r.at[sender],
            device_id=(stn, r), device_id_type=MESH,
        )

    for g in range(groups):
        await_prev(g)
        if g < groups - 1:
            backward(g).wait_recv()
            total = filter_rest(g, True, True)
        else:
            total = filter_rest(g, True, False)
            transform(g, 0, AFTER)
            backward(g).wait_recv()
            total = total + filter_rest(g, False, True)
        total = jnp.sum(total, axis=1, keepdims=True) * channels
        power_out[g * GROUP : (g + 1) * GROUP, :] = jnp.broadcast_to(total, (GROUP, LANES))
        if g < groups - 1:
            transform(g, 0, here)
        else:
            for offset in range(1, blocks):
                power_copy(peer_blk(offset), blk).start()
            transform(g, AFTER, here - AFTER)

    power = power_out[...]
    for offset in range(1, blocks):
        r = peer_blk(offset)
        power_copy(r, r).wait_recv()
        power = power + power_in[r]
    scale_ref[...] = 1.0 / jnp.sqrt(power / (here * blocks * channels) + EPS)
    for offset in range(1, blocks):
        power_copy(peer_blk(offset), blk).wait_send()
    for g in range(groups):

        @pl.when(blk < blocks - 1)
        def _():
            forward(g).wait_send()

        backward(g).wait_send()

    def far_rows(k, s):
        return pl.ds(pl.multiple_of((k * here + s) * LANES, LANES), LANES)

    def far_copy(k):
        part = pl.ds(pl.multiple_of(k * here * LANES, here * LANES), here * LANES)
        return pltpu.make_async_remote_copy(
            src_ref=own.at[:, :, part], dst_ref=following.at[:, :, part], send_sem=far_s.at[k], recv_sem=far_r.at[k],
            device_id=(stn, partner), device_id_type=MESH,
        )

    def hand_over(k, carry):
        scale = scale_ref[...]
        for s in range(here):
            for p in range(2):
                own[p, :, far_rows(k, s)] = (work[p, (1 - core) * half + k, s] * scale).astype(BF16)
        far_copy(k).start()
        return carry

    lax.fori_loop(0, half, hand_over, 0)

    def quantize(k):
        far_copy(k).wait_recv()
        scale = scale_ref[...]
        total = jnp.zeros((inputs, LANES), F32)
        for s in range(here):
            for p in range(2):
                value = (work[p, core * half + k, s] * scale).astype(BF16)
                near[k, p, s] = value
                wide = value.astype(F32)
                wider = following[p, :, far_rows(k, s)].astype(F32)
                total = total + (wide * wide + wider * wider)
        self_power[k] = total

    def sample(k, p, t):
        return (near[k, p, t] if t < here else following[p, :, far_rows(k, t - here)]).astype(F32)

    def begin(m, carry):
        gain[m, 0] = jnp.ones((inputs, LANES), F32)
        gain[m, 1] = jnp.zeros((inputs, LANES), F32)
        return carry

    lax.fori_loop(0, quad, begin, 0)

    def back_parts(turn):
        return [(back_wide if turn == 0 else back_narrow).at[n] for n in range(3)]

    def back_copy(turn, c, sender):
        back_out, back_in, _ = back_parts(turn)
        return pltpu.make_async_remote_copy(
            src_ref=back_out.at[c], dst_ref=back_in.at[sender], send_sem=back_s.at[c], recv_sem=back_r.at[sender],
            device_id=(c, blk), device_id_type=MESH,
        )

    def total_copy(turn, c, owner):
        _, _, back_sum = back_parts(turn)
        return pltpu.make_async_remote_copy(
            src_ref=back_sum.at[owner], dst_ref=back_sum.at[owner], send_sem=total_s.at[c], recv_sem=total_r.at[owner],
            device_id=(c, blk), device_id_type=MESH,
        )

    def sum_copy(r, sender):
        return pltpu.make_async_remote_copy(
            src_ref=sum_out.at[r], dst_ref=sum_in.at[sender], send_sem=sum_s.at[r], recv_sem=sum_r.at[sender],
            device_id=(stn, 2 * r + core), device_id_type=MESH,
        )

    def weight_copy(r, owner):
        part = weights.at[pl.ds(owner * quad, quad)]
        return pltpu.make_async_remote_copy(
            src_ref=part, dst_ref=part, send_sem=weight_s.at[r], recv_sem=weight_r.at[owner],
            device_id=(stn, 2 * r + core), device_id_type=MESH,
        )

    def split_norm(norm):
        high = norm.astype(BF16).astype(F32)
        rows_ref[2 * spectra : 2 * spectra + 1, :] = high
        rows_ref[2 * spectra + 1 : 2 * spectra + 2, :] = norm - high

    def weight(turn, k, p):
        return model_ref[p] if turn == 0 else weights[k, p].astype(F32)

    def down(turn, k, c, j):
        w_re, w_im = weight(turn, k, 0), weight(turn, k, 1)
        for t in range(spectra):
            q_re, q_im = sample(k, 0, t), sample(k, 1, t)
            rows_ref[t : t + 1, :] = jnp.sum(q_re * w_re + q_im * w_im, axis=0, keepdims=True)
            rows_ref[spectra + t : spectra + t + 1, :] = jnp.sum(q_re * w_im - q_im * w_re, axis=0, keepdims=True)
        back_out = back_parts(turn)[0]
        if turn == 0:
            back_out[c, j] = rows_ref[: 2 * spectra, :]
        else:
            split_norm(jnp.sum(w_re * w_re + w_im * w_im, axis=0, keepdims=True))
            back_out[c, j] = rows_ref[...].astype(BF16)

    def up(turn, k, r, j):
        c, jj = lax.div(k, chunk), lax.rem(k, chunk)
        back = back_parts(turn)[2]
        rows_ref[: back.shape[2], :] = back[c, jj].astype(F32)
        h_re = jnp.zeros((inputs, LANES), F32)
        h_im = jnp.zeros((inputs, LANES), F32)
        for t in range(spectra):
            q_re, q_im = sample(k, 0, t), sample(k, 1, t)
            b_re, b_im = rows_ref[t : t + 1, :], rows_ref[spectra + t : spectra + t + 1, :]
            h_re = h_re + (q_re * b_re - q_im * b_im)
            h_im = h_im + (q_re * b_im + q_im * b_re)
        own_power = self_power[k]
        sum_out[r, j, 0] = (h_re - own_power * weight(turn, k, 0)).astype(BF16)
        sum_out[r, j, 1] = (h_im - own_power * weight(turn, k, 1)).astype(BF16)

    for turn in range(ITERS):
        def down_part(o, carry):
            r = peer_place(o)
            if turn > 0:

                @pl.when(o > 0)
                def _():
                    weight_copy(r, r).wait_recv()

            def one(n, carry):
                c = r * per + n

                def each(j, carry):
                    if turn == 0:
                        quantize(c * chunk + j)
                    down(turn, c * chunk + j, c, j)
                    return carry

                lax.fori_loop(0, chunk, each, 0)

                @pl.when(c != stn)
                def _():
                    back_copy(turn, c, stn).start()

                return carry

            return lax.fori_loop(0, per, one, carry)

        lax.fori_loop(0, places, down_part, 0)

        def gather(j, carry):
            back_out, back_in, back_sum = back_parts(turn)
            total = back_out[stn, j].astype(F32)

            def more(o, total):
                return total + back_in[peer_stn(o), j].astype(F32)

            total = lax.fori_loop(1, stations, more, total)
            if turn > 0:
                rows_ref[...] = total
                split_norm(jnp.sum(rows_ref[2 * spectra : 2 * spectra + 2, :], axis=0, keepdims=True))
                total = rows_ref[...]
            back_sum[stn, j] = total.astype(back_sum.dtype)
            return carry

        def await_back(o, carry):
            c = peer_stn(o)
            back_copy(turn, c, c).wait_recv()
            return carry

        lax.fori_loop(1, stations, await_back, 0)
        lax.fori_loop(0, chunk, gather, 0)

        def send_total(o, carry):
            total_copy(turn, peer_stn(o), stn).start()
            return carry

        lax.fori_loop(1, stations, send_total, 0)

        def up_part(o, carry):
            r = peer_place(o)
            for n in range(per):
                c = r * per + n

                @pl.when(c != stn)
                def _():
                    total_copy(turn, c, c).wait_recv()

            def each(j, carry):
                up(turn, r * quad + j, r, j)
                return carry

            lax.fori_loop(0, quad, each, 0)

            @pl.when(o < places)
            def _():
                sum_copy(r, place).start()

            return carry

        lax.fori_loop(1, places + 1, up_part, 0)

        def settle(o, carry):
            c = peer_stn(o)
            back_copy(turn, c, stn).wait_send()
            total_copy(turn, c, stn).wait_send()
            return carry

        lax.fori_loop(1, stations, settle, 0)

        def await_sum(o, carry):
            r = peer_place(o)
            sum_copy(r, r).wait_recv()
            if turn > 0:
                weight_copy(r, place).wait_send()
            return carry

        lax.fori_loop(1, places, await_sum, 0)

        for m in range(quad):
            k = place * quad + m
            total_re = sum_out[place, m, 0].astype(F32)
            total_im = sum_out[place, m, 1].astype(F32)

            def more(o, totals):
                r = peer_place(o)
                return totals[0] + sum_in[r, m, 0].astype(F32), totals[1] + sum_in[r, m, 1].astype(F32)

            total_re, total_im = lax.fori_loop(1, places, more, (total_re, total_im))
            m_re, m_im = model_ref[0], model_ref[1]
            g_re, g_im = gain[m, 0], gain[m, 1]
            w_re = g_re * m_re - g_im * m_im
            w_im = g_re * m_im + g_im * m_re
            if turn == 0:
                norm = first
            else:
                tail = back_narrow[2, lax.div(k, chunk), lax.rem(k, chunk), 2 * spectra :, :].astype(F32)
                norm = tail[0:1, :] + tail[1:2, :]
            denom = norm - (w_re * w_re + w_im * w_im) + EPS
            new_re = (m_re * total_re + m_im * total_im) / denom
            new_im = (m_re * total_im - m_im * total_re) / denom
            if turn % 2 == 1:
                new_re = (new_re + g_re) * 0.5
                new_im = (new_im + g_im) * 0.5
            gain[m, 0] = new_re
            gain[m, 1] = new_im
            if turn < ITERS - 1:
                w_re = new_re * m_re - new_im * m_im
                w_im = new_re * m_im + new_im * m_re
                weights[k, 0] = w_re.astype(BF16)
                weights[k, 1] = w_im.astype(BF16)

        if turn < ITERS - 1:
            def send_weight(o, carry):
                weight_copy(peer_place(o), place).start()
                return carry

            lax.fori_loop(1, places, send_weight, 0)

        def sent(o, carry):
            sum_copy(peer_place(o), place).wait_send()
            return carry

        lax.fori_loop(1, places, sent, 0)

    def handed(k, carry):
        far_copy(k).wait_send()
        return carry

    lax.fori_loop(0, half, handed, 0)

    def final_copy(r, sender):
        return pltpu.make_async_remote_copy(
            src_ref=final_out.at[r], dst_ref=final_in.at[sender], send_sem=final_s.at[r], recv_sem=final_r.at[sender],
            device_id=(stn, r), device_id_type=MESH,
        )

    def last_copy(c, sender):
        return pltpu.make_async_remote_copy(
            src_ref=last_out.at[c], dst_ref=last_in.at[sender], send_sem=last_s.at[c], recv_sem=last_r.at[sender],
            device_id=(c, blk), device_id_type=MESH,
        )

    width = quad * 2 * inputs
    turned[...] = gain[...].reshape(width, LANES).T.reshape(stations, blocks, width)
    for r in range(blocks):
        final_out[r] = turned[:, r, :]
    for offset in range(1, blocks):
        final_copy(peer_blk(offset), blk).start()
    final_in[blk] = final_out[blk]
    for offset in range(1, blocks):
        r = peer_blk(offset)
        final_copy(r, r).wait_recv()
    for c in range(stations):
        last_out[c] = final_in[:, c, :]

    def send_last(o, carry):
        last_copy(peer_stn(o), stn).start()
        return carry

    lax.fori_loop(1, stations, send_last, 0)
    last_in[stn] = last_out[stn]

    def await_last(o, carry):
        c = peer_stn(o)
        last_copy(c, c).wait_recv()
        return carry

    lax.fori_loop(1, stations, await_last, 0)
    for m in range(quad):
        for p in range(2):
            at = (2 * m + p) * inputs
            for n in range(stations // span):
                block = jnp.concatenate(
                    [last_in[n * span + i, :, at : at + inputs] for i in range(span)], axis=1
                )
                for r in range(blocks):
                    k = (r % 2) * half + (r // 2) * quad + m
                    out_ref[p, k : k + 1, n * LANES : (n + 1) * LANES] = block[r : r + 1, :]

    for offset in range(1, blocks):
        final_copy(peer_blk(offset), blk).wait_send()

    def sent_last(o, carry):
        last_copy(peer_stn(o), stn).wait_send()
        return carry

    lax.fori_loop(1, stations, sent_last, 0)


def correlate(stations, blocks, voltages, high, low, taps, phases):
    inputs, channels = voltages.shape[1], taps.shape[1]
    here = voltages.shape[2] // channels
    groups = inputs // GROUP
    places, half = blocks // 2, RADIX // 2
    chunk, quad = half // stations, half // places
    rows = 4 * here + 16
    width = quad * 2 * inputs
    hbm = pl.BlockSpec(memory_space=pl.ANY)
    vmem = pl.BlockSpec(memory_space=pltpu.VMEM)
    dma = pltpu.SemaphoreType.DMA
    return pl.pallas_call(
        functools.partial(correlator_kernel, stations, blocks),
        in_specs=[hbm, hbm, hbm, vmem, vmem],
        out_specs=vmem,
        out_shape=jax.ShapeDtypeStruct((2, RADIX, stations * inputs), F32),
        scratch_shapes=[
            pltpu.VMEM((2, inputs, here * channels), BF16),
            pltpu.VMEM((2, inputs, BEFORE * channels), BF16),
            pltpu.VMEM((2, inputs, AFTER * channels), BF16),
            pltpu.VMEM((2, RADIX, here, inputs, LANES), F32),
            pltpu.VMEM(high.shape, BF16),
            pltpu.VMEM(low.shape, BF16),
            pltpu.VMEM((inputs, LANES), F32),
            pltpu.VMEM((blocks, inputs, LANES), F32),
            pltpu.VMEM((inputs, LANES), F32),
            pltpu.VMEM((2, inputs, LANES), F32),
            pltpu.VMEM((half, 2, here, inputs, LANES), BF16),
            pltpu.VMEM((half, 2, inputs, LANES), BF16),
            pltpu.VMEM((half, inputs, LANES), F32),
            pltpu.VMEM((3, stations, chunk, 4 * here, LANES), F32),
            pltpu.VMEM((3, stations, chunk, rows, LANES), BF16),
            pltpu.VMEM((places, quad, 2, inputs, LANES), BF16),
            pltpu.VMEM((places, quad, 2, inputs, LANES), BF16),
            pltpu.VMEM((quad, 2, inputs, LANES), F32),
            pltpu.VMEM((rows, LANES), F32),
            pltpu.VMEM((stations, blocks, width), F32),
            pltpu.VMEM((blocks, stations, width), F32),
            pltpu.VMEM((blocks, stations, width), F32),
            pltpu.VMEM((stations, blocks, width), F32),
            pltpu.VMEM((stations, blocks, width), F32),
            dma((groups,)),
            dma((2,)),
            dma((2, groups)),
            dma((2, groups)),
            dma((blocks,)),
            dma((blocks,)),
            dma((half,)),
            dma((half,)),
            dma((stations,)),
            dma((stations,)),
            dma((stations,)),
            dma((stations,)),
            dma((places,)),
            dma((places,)),
            dma((places,)),
            dma((places,)),
            dma((blocks,)),
            dma((blocks,)),
            dma((stations,)),
            dma((stations,)),
        ],
        compiler_params=pltpu.CompilerParams(
            collective_id=0, has_side_effects=True, vmem_limit_bytes=62 * 2**20
        ),
        name="correlator",
    )(voltages, high, low, taps, phases)


def on_device(stations, blocks, voltages, taps, model_phase):
    high, low = dft_tables(taps.shape[1])
    phases = model_phase.reshape(-1, LANES)
    return correlate(stations, blocks, voltages, jnp.asarray(high), jnp.asarray(low), taps, phases)


def solution(mesh):
    stations, blocks = mesh.shape["stn"], mesh.shape["blk"]
    in_specs = (P(None, "stn", "blk"), P(), P())
    out_specs = P(None, ("stn", "blk"), None)
    return jax.shard_map(
        functools.partial(on_device, stations, blocks),
        mesh=mesh, in_specs=in_specs, out_specs=out_specs, check_vma=False,
    )
```

```python
import functools
import math

import jax
import jax.numpy as jnp
import ml_dtypes
import numpy as np
from jax import lax
from jax.experimental import pallas as pl
from jax.experimental.pallas import tpu as pltpu
from jax.sharding import PartitionSpec as P

ITERS = 4
EPS = 1e-06
TAPS = 16
BEFORE = 7
AFTER = 8
LANES = 128
GROUP = 16
RADIX = 32
F32 = jnp.float32
BF16 = jnp.bfloat16
MESH = pl.DeviceIdType.MESH


def dft_tables(channels):
    b = np.arange(LANES)
    k = np.arange(RADIX)
    turns = (b[None, :, None] * (k[:, None, None] + RADIX * b[None, None, :])) % channels
    angle = -2.0 * np.pi * turns / channels
    cos, sin = np.cos(angle), np.sin(angle)
    table = np.concatenate(
        [np.concatenate([cos, sin], axis=2), np.concatenate([-sin, cos], axis=2)], axis=1
    ).astype(np.float32)
    high = table.astype(ml_dtypes.bfloat16)
    low = (table - high.astype(np.float32)).astype(ml_dtypes.bfloat16)
    return high, low


def times(z, w):
    re, im = z
    c, s = float(w.real), float(w.imag)
    if abs(s) < 1e-12:
        return (re, im) if c > 0 else (-re, -im)
    if abs(c) < 1e-12:
        return (-im, re) if s > 0 else (im, -re)
    if abs(abs(c) - abs(s)) < 1e-12:
        if c > 0 and s < 0:
            return ((re + im) * c, (im - re) * c)
        if c < 0 and s < 0:
            return ((im - re) * -c, (re + im) * c)
    return (re * c - im * s, re * s + im * c)


def add(x, y):
    return (x[0] + y[0], x[1] + y[1])


def sub(x, y):
    return (x[0] - y[0], x[1] - y[1])


def fft(points):
    size = len(points)
    if size == 1:
        return points
    if size == 2:
        return [add(points[0], points[1]), sub(points[0], points[1])]
    if size == 4:
        even = [add(points[0], points[2]), sub(points[0], points[2])]
        odd = [add(points[1], points[3]), sub(points[1], points[3])]
        turned = (odd[1][1], -odd[1][0])
        return [add(even[0], odd[0]), add(even[1], turned), sub(even[0], odd[0]), sub(even[1], turned)]
    if size == 8:
        even, odd = fft(points[0::2]), fft(points[1::2])
        odd = [times(z, np.exp(-2j * np.pi * i / 8)) for i, z in enumerate(odd)]
        return [add(e, o) for e, o in zip(even, odd)] + [sub(e, o) for e, o in zip(even, odd)]
    outer = size // 4
    result = [None] * size
    firsts = []
    for j in range(outer):
        first = fft([points[j + outer * r] for r in range(4)])
        firsts.append([times(z, np.exp(-2j * np.pi * j * u / size)) for u, z in enumerate(first)])
    for u in range(4):
        second = fft([firsts[j][u] for j in range(outer)])
        for v in range(outer):
            result[u + 4 * v] = second[v]
    return result


def correlator_kernel(
    stations, blocks,
    volt_ref, high_hbm, low_hbm, taps_ref, phases_ref,
    out_ref,
    own, prev, following, work, high_ref, low_ref, power_out, power_in, scale_ref, model_ref,
    near, weights, self_power, back_wide, back_narrow, sum_out, sum_in, gain, rows_ref,
    turned, final_out, final_in, last_out, last_in,
    own_sem, table_sem, halo_s, halo_r, power_s, power_r, far_s, far_r, back_s, back_r, total_s, total_r,
    sum_s, sum_r, weight_s, weight_r, final_s, final_r, last_s, last_r,
):
    stn, blk = lax.axis_index("stn"), lax.axis_index("blk")
    channels = taps_ref.shape[1]
    inputs = volt_ref.shape[1]
    here = volt_ref.shape[2] // channels
    groups = inputs // GROUP
    core, place = lax.rem(blk, 2), lax.div(blk, 2)
    partner = blk + 1 - 2 * core
    places = blocks // 2
    half = RADIX // 2
    chunk = half // stations
    quad = half // places
    per = quad // chunk
    spectra = 2 * here
    keep = jnp.where(blk == blocks - 1, 0.0, 1.0)

    def peer_stn(offset):
        return lax.rem(stn + offset, stations)

    def peer_blk(offset):
        return lax.rem(blk + offset, blocks)

    def peer_place(offset):
        return lax.rem(place + offset, places)

    side = math.isqrt(stations)
    row_at, column_at = lax.div(stn, side), lax.rem(stn, side)
    ring = [min(d, side - d) for d in range(side)]
    others = sorted(
        ((dy, dz) for dy in range(side) for dz in range(side) if dy or dz), key=lambda d: -ring[d[0]] - ring[d[1]]
    )

    def far_first():
        for dy, dz in others:
            yield lax.rem(row_at + dy, side) * side + lax.rem(column_at + dz, side)

    def order(turn, q, n):
        offset = q + lax.div(q, 2) * (1 - 2 * lax.rem(q, 2)) if places == 4 else q
        if turn == 0:
            offset = offset + row_at
        r = lax.rem(place + offset, places)
        return r, r * per + lax.rem(n + column_at, per)

    barrier = pltpu.get_barrier_semaphore()
    for offset in range(1, stations):
        pl.semaphore_signal(barrier, inc=1, device_id=(peer_stn(offset), blk), device_id_type=MESH)
    for offset in range(1, blocks):
        pl.semaphore_signal(barrier, inc=1, device_id=(stn, peer_blk(offset)), device_id_type=MESH)

    def rows_of(g):
        return pl.ds(pl.multiple_of(g * GROUP, GROUP), GROUP)

    def own_copy(g):
        return pltpu.make_async_copy(volt_ref.at[:, rows_of(g), :], own.at[:, rows_of(g), :], own_sem.at[g])

    def table_copy(n):
        pair = ((high_hbm, high_ref), (low_hbm, low_ref))[n]
        return pltpu.make_async_copy(*pair, table_sem.at[n])

    def forward(g):
        return pltpu.make_async_remote_copy(
            src_ref=volt_ref.at[:, rows_of(g), pl.ds((here - BEFORE) * channels, BEFORE * channels)],
            dst_ref=prev.at[:, rows_of(g), :], send_sem=halo_s.at[0, g], recv_sem=halo_r.at[0, g],
            device_id=(stn, peer_blk(1)), device_id_type=MESH,
        )

    def backward(g):
        return pltpu.make_async_remote_copy(
            src_ref=volt_ref.at[:, rows_of(g), pl.ds(0, AFTER * channels)],
            dst_ref=following.at[:, rows_of(g), :], send_sem=halo_s.at[1, g], recv_sem=halo_r.at[1, g],
            device_id=(stn, peer_blk(blocks - 1)), device_id_type=MESH,
        )

    for g in range(groups):
        own_copy(g).start()
    for n in range(2):
        table_copy(n).start()
    pl.semaphore_wait(barrier, stations + blocks - 2)
    for g in range(groups):

        @pl.when(blk < blocks - 1)
        def _():
            forward(g).start()

        backward(g).start()

    @pl.when(blk == 0)
    def _():
        def clear(j, carry):
            at = pl.ds(pl.multiple_of(j * channels, channels), channels)
            for p in range(2):
                prev[p, :, at] = jnp.zeros((inputs, channels), BF16)
            return carry

        lax.fori_loop(0, BEFORE, clear, 0)

    def tap_rows(start):
        return [taps_ref[k : k + 1, pl.ds(start, LANES)] for k in range(TAPS)]

    def accumulate(sums, source, g, p, start, first, count, rows):
        for j in range(first, first + count):
            at = pl.multiple_of(start + (j - first) * channels, LANES)
            sample = source[p, rows_of(g), pl.ds(at, LANES)].astype(F32)
            for k in range(TAPS):
                u = j - k
                if 0 <= u < here:
                    term = sample * rows[k]
                    sums[u] = term if sums[u] is None else sums[u] + term

    def filter_own(g, carry):
        own_copy(g).wait()

        def part(a, carry):
            start = pl.multiple_of(a * LANES, LANES)
            rows = tap_rows(start)
            for p in range(2):
                sums = [None] * here
                accumulate(sums, own, g, p, start, BEFORE, here, rows)
                for u in range(here):
                    work[p, a, u, rows_of(g), :] = sums[u] if u < here - AFTER else sums[u] * keep
            return carry

        return lax.fori_loop(0, RADIX, part, carry)

    lax.fori_loop(0, groups, filter_own, 0)
    span = LANES // inputs
    row = phases_ref[pl.ds(lax.div(stn, span), 1), :]
    lane = lax.broadcasted_iota(jnp.int32, (inputs, LANES), 1)
    wanted = lax.broadcasted_iota(jnp.int32, (inputs, LANES), 0) + lax.rem(stn, span) * inputs
    phase = jnp.sum(jnp.where(lane == wanted, row, 0.0), axis=1, keepdims=True)
    phase = jnp.broadcast_to(phase, (inputs, LANES))
    model_ref[0] = jnp.cos(phase)
    model_ref[1] = jnp.sin(phase)
    all_re, all_im = jnp.cos(phases_ref[...]), jnp.sin(phases_ref[...])
    first = jnp.sum(all_re * all_re + all_im * all_im)
    rows_ref[...] = jnp.zeros(rows_ref.shape, F32)
    for n in range(2):
        table_copy(n).wait()

    def filter_rest(g, low_half, high_half):
        spots = [u for u in range(here) if (u < AFTER and low_half) or (u >= AFTER and high_half)]

        def part(a, total):
            start = pl.multiple_of(a * LANES, LANES)
            rows = tap_rows(start)
            for p in range(2):
                sums = [work[p, a, u, rows_of(g), :] if u in spots else None for u in range(here)]
                if low_half:
                    accumulate(sums, prev, g, p, start, 0, BEFORE, rows)
                if high_half:
                    accumulate(sums, following, g, p, start, BEFORE + here, AFTER, rows)
                for u in spots:
                    work[p, a, u, rows_of(g), :] = sums[u]
                    total = total + sums[u] * sums[u]
            return total

        return lax.fori_loop(0, RADIX, part, jnp.zeros((GROUP, LANES), F32))

    def transform(g, first_spot, count):
        def turn(s, carry):
            for part in range(GROUP // 8):
                rows = pl.ds(g * GROUP + 8 * part, 8)
                points = [(work[0, a, s, rows, :], work[1, a, s, rows, :]) for a in range(RADIX)]
                for k, (re, im) in enumerate(fft(points)):
                    work[0, k, s, rows, :] = re
                    work[1, k, s, rows, :] = im
            return carry

        lax.fori_loop(first_spot, first_spot + count, turn, 0)

        def second(k, carry):
            spots = pl.ds(first_spot, count)
            both = jnp.concatenate(
                [work[p, k, spots, rows_of(g), :].reshape(count * GROUP, LANES) for p in range(2)], axis=1
            )
            high = both.astype(BF16)
            low = (both - high.astype(F32)).astype(BF16)
            table = high_ref[k]
            out = jnp.dot(
                jnp.concatenate([high, low, high], axis=1),
                jnp.concatenate([table, table, low_ref[k]], axis=0),
                preferred_element_type=F32,
            )
            out = out.reshape(count, GROUP, 2 * LANES)
            work[0, k, spots, rows_of(g), :] = out[:, :, :LANES]
            work[1, k, spots, rows_of(g), :] = out[:, :, LANES:]
            return carry

        lax.fori_loop(0, RADIX, second, 0, unroll=4)

    def await_prev(g):
        @pl.when(blk > 0)
        def _():
            forward(g).wait_recv()

    def power_copy(r, sender):
        return pltpu.make_async_remote_copy(
            src_ref=power_out, dst_ref=power_in.at[sender], send_sem=power_s.at[r], recv_sem=power_r.at[sender],
            device_id=(stn, r), device_id_type=MESH,
        )

    for g in range(groups):
        await_prev(g)
        if g < groups - 1:
            backward(g).wait_recv()
            total = filter_rest(g, True, True)
        else:
            total = filter_rest(g, True, False)
            transform(g, 0, AFTER)
            backward(g).wait_recv()
            total = total + filter_rest(g, False, True)
        total = jnp.sum(total, axis=1, keepdims=True) * channels
        power_out[g * GROUP : (g + 1) * GROUP, :] = jnp.broadcast_to(total, (GROUP, LANES))
        if g < groups - 1:
            transform(g, 0, here)
        else:
            for offset in range(1, blocks):
                power_copy(peer_blk(offset), blk).start()
            transform(g, AFTER, here - AFTER)

    power = power_out[...]
    for offset in range(1, blocks):
        r = peer_blk(offset)
        power_copy(r, r).wait_recv()
        power = power + power_in[r]
    scale_ref[...] = 1.0 / jnp.sqrt(power / (here * blocks * channels) + EPS)
    for offset in range(1, blocks):
        power_copy(peer_blk(offset), blk).wait_send()
    for g in range(groups):

        @pl.when(blk < blocks - 1)
        def _():
            forward(g).wait_send()

        backward(g).wait_send()

    def far_rows(k, s):
        return pl.ds(pl.multiple_of((k * here + s) * LANES, LANES), LANES)

    def far_copy(k):
        part = pl.ds(pl.multiple_of(k * here * LANES, here * LANES), here * LANES)
        return pltpu.make_async_remote_copy(
            src_ref=own.at[:, :, part], dst_ref=following.at[:, :, part], send_sem=far_s.at[k], recv_sem=far_r.at[k],
            device_id=(stn, partner), device_id_type=MESH,
        )

    def hand_over(i, carry):
        c = order(0, lax.div(i, quad), lax.div(lax.rem(i, quad), chunk))[1]
        k = c * chunk + lax.rem(i, chunk)
        scale = scale_ref[...]
        for s in range(here):
            for p in range(2):
                own[p, :, far_rows(k, s)] = (work[p, (1 - core) * half + k, s] * scale).astype(BF16)
        far_copy(k).start()
        return carry

    lax.fori_loop(0, half, hand_over, 0)

    def quantize(k):
        far_copy(k).wait_recv()
        scale = scale_ref[...]
        total = jnp.zeros((inputs, LANES), F32)
        for s in range(here):
            for p in range(2):
                value = (work[p, core * half + k, s] * scale).astype(BF16)
                near[k, p, s] = value
                wide = value.astype(F32)
                wider = following[p, :, far_rows(k, s)].astype(F32)
                total = total + (wide * wide + wider * wider)
        self_power[k] = total

    def sample(k, p, t):
        return (near[k, p, t] if t < here else following[p, :, far_rows(k, t - here)]).astype(F32)

    def begin(m, carry):
        gain[m, 0] = jnp.ones((inputs, LANES), F32)
        gain[m, 1] = jnp.zeros((inputs, LANES), F32)
        return carry

    lax.fori_loop(0, quad, begin, 0)

    def back_parts(turn):
        return [(back_wide if turn == 0 else back_narrow).at[n] for n in range(3)]

    def back_copy(turn, c, sender):
        back_out, back_in, _ = back_parts(turn)
        return pltpu.make_async_remote_copy(
            src_ref=back_out.at[c], dst_ref=back_in.at[sender], send_sem=back_s.at[c], recv_sem=back_r.at[sender],
            device_id=(c, blk), device_id_type=MESH,
        )

    def total_copy(turn, c, owner):
        _, _, back_sum = back_parts(turn)
        return pltpu.make_async_remote_copy(
            src_ref=back_sum.at[owner], dst_ref=back_sum.at[owner], send_sem=total_s.at[c], recv_sem=total_r.at[owner],
            device_id=(c, blk), device_id_type=MESH,
        )

    def sum_copy(r, sender):
        return pltpu.make_async_remote_copy(
            src_ref=sum_out.at[r], dst_ref=sum_in.at[sender], send_sem=sum_s.at[r], recv_sem=sum_r.at[sender],
            device_id=(stn, 2 * r + core), device_id_type=MESH,
        )

    def weight_copy(r, owner):
        part = weights.at[pl.ds(owner * quad, quad)]
        return pltpu.make_async_remote_copy(
            src_ref=part, dst_ref=part, send_sem=weight_s.at[r], recv_sem=weight_r.at[owner],
            device_id=(stn, 2 * r + core), device_id_type=MESH,
        )

    def split_norm(norm):
        high = norm.astype(BF16).astype(F32)
        rows_ref[2 * spectra : 2 * spectra + 1, :] = high
        rows_ref[2 * spectra + 1 : 2 * spectra + 2, :] = norm - high

    def weight(turn, k, p):
        return model_ref[p] if turn == 0 else weights[k, p].astype(F32)

    def down(turn, k, c, j):
        w_re, w_im = weight(turn, k, 0), weight(turn, k, 1)
        for t in range(spectra):
            q_re, q_im = sample(k, 0, t), sample(k, 1, t)
            rows_ref[t : t + 1, :] = jnp.sum(q_re * w_re + q_im * w_im, axis=0, keepdims=True)
            rows_ref[spectra + t : spectra + t + 1, :] = jnp.sum(q_re * w_im - q_im * w_re, axis=0, keepdims=True)
        back_out = back_parts(turn)[0]
        if turn == 0:
            back_out[c, j] = rows_ref[: 2 * spectra, :]
        else:
            split_norm(jnp.sum(w_re * w_re + w_im * w_im, axis=0, keepdims=True))
            back_out[c, j] = rows_ref[...].astype(BF16)

    def up(turn, k, r, j):
        c, jj = lax.div(k, chunk), lax.rem(k, chunk)
        back = back_parts(turn)[2]
        rows_ref[: back.shape[2], :] = back[c, jj].astype(F32)
        h_re = jnp.zeros((inputs, LANES), F32)
        h_im = jnp.zeros((inputs, LANES), F32)
        for t in range(spectra):
            q_re, q_im = sample(k, 0, t), sample(k, 1, t)
            b_re, b_im = rows_ref[t : t + 1, :], rows_ref[spectra + t : spectra + t + 1, :]
            h_re = h_re + (q_re * b_re - q_im * b_im)
            h_im = h_im + (q_re * b_im + q_im * b_re)
        own_power = self_power[k]
        sum_out[r, j, 0] = (h_re - own_power * weight(turn, k, 0)).astype(BF16)
        sum_out[r, j, 1] = (h_im - own_power * weight(turn, k, 1)).astype(BF16)

    for turn in range(ITERS):
        def down_part(o, carry):
            r = order(turn, o, 0)[0]
            if turn > 0:

                @pl.when(o > 0)
                def _():
                    weight_copy(r, r).wait_recv()

            def one(n, carry):
                c = order(turn, o, n)[1]

                def each(j, carry):
                    if turn == 0:
                        quantize(c * chunk + j)
                    down(turn, c * chunk + j, c, j)
                    return carry

                lax.fori_loop(0, chunk, each, 0)

                @pl.when(c != stn)
                def _():
                    back_copy(turn, c, stn).start()

                return carry

            return lax.fori_loop(0, per, one, carry)

        lax.fori_loop(0, places, down_part, 0)

        def await_back(o, carry):
            c = peer_stn(o)
            back_copy(turn, c, c).wait_recv()
            return carry

        if chunk > 1:
            lax.fori_loop(1, stations, await_back, 0)

        def gather(j, carry):
            back_out, back_in, back_sum = back_parts(turn)
            total = back_out[stn, j].astype(F32)

            def more(o, total):
                if chunk == 1:
                    await_back(o, 0)
                return total + back_in[peer_stn(o), j].astype(F32)

            total = lax.fori_loop(1, stations, more, total)
            if turn > 0:
                rows_ref[...] = total
                split_norm(jnp.sum(rows_ref[2 * spectra : 2 * spectra + 2, :], axis=0, keepdims=True))
                total = rows_ref[...]
            back_sum[stn, j] = total.astype(back_sum.dtype)
            return carry

        lax.fori_loop(0, chunk, gather, 0)
        for c in far_first():
            total_copy(turn, c, stn).start()

        def up_part(o):
            r = peer_place(o)
            for n in range(per):
                c = r * per + n

                @pl.when(c != stn)
                def _():
                    total_copy(turn, c, c).wait_recv()

            def each(j, carry):
                up(turn, r * quad + j, r, j)
                return carry

            lax.fori_loop(0, quad, each, 0)
            if o > 0:
                sum_copy(r, place).start()

        for o in sorted(range(places), key=lambda o: -min(o, places - o)):
            up_part(o)

        def settle(o, carry):
            c = peer_stn(o)
            back_copy(turn, c, stn).wait_send()
            total_copy(turn, c, stn).wait_send()
            return carry

        lax.fori_loop(1, stations, settle, 0)

        def await_sum(o, carry):
            r = peer_place(o)
            sum_copy(r, r).wait_recv()
            if turn > 0:
                weight_copy(r, place).wait_send()
            return carry

        lax.fori_loop(1, places, await_sum, 0)

        for m in range(quad):
            k = place * quad + m
            total_re = sum_out[place, m, 0].astype(F32)
            total_im = sum_out[place, m, 1].astype(F32)

            def more(o, totals):
                r = peer_place(o)
                return totals[0] + sum_in[r, m, 0].astype(F32), totals[1] + sum_in[r, m, 1].astype(F32)

            total_re, total_im = lax.fori_loop(1, places, more, (total_re, total_im))
            m_re, m_im = model_ref[0], model_ref[1]
            g_re, g_im = gain[m, 0], gain[m, 1]
            w_re = g_re * m_re - g_im * m_im
            w_im = g_re * m_im + g_im * m_re
            if turn == 0:
                norm = first
            else:
                tail = back_narrow[2, lax.div(k, chunk), lax.rem(k, chunk), 2 * spectra :, :].astype(F32)
                norm = tail[0:1, :] + tail[1:2, :]
            denom = norm - (w_re * w_re + w_im * w_im) + EPS
            new_re = (m_re * total_re + m_im * total_im) / denom
            new_im = (m_re * total_im - m_im * total_re) / denom
            if turn % 2 == 1:
                new_re = (new_re + g_re) * 0.5
                new_im = (new_im + g_im) * 0.5
            gain[m, 0] = new_re
            gain[m, 1] = new_im
            if turn < ITERS - 1:
                w_re = new_re * m_re - new_im * m_im
                w_im = new_re * m_im + new_im * m_re
                weights[k, 0] = w_re.astype(BF16)
                weights[k, 1] = w_im.astype(BF16)

        if turn < ITERS - 1:
            for o in sorted(range(1, places), key=lambda o: -min(o, places - o)):
                weight_copy(peer_place(o), place).start()

        def sent(o, carry):
            sum_copy(peer_place(o), place).wait_send()
            return carry

        lax.fori_loop(1, places, sent, 0)

    def handed(k, carry):
        far_copy(k).wait_send()
        return carry

    lax.fori_loop(0, half, handed, 0)

    def final_copy(r, sender):
        return pltpu.make_async_remote_copy(
            src_ref=final_out.at[r], dst_ref=final_in.at[sender], send_sem=final_s.at[r], recv_sem=final_r.at[sender],
            device_id=(stn, r), device_id_type=MESH,
        )

    def last_copy(c, sender):
        return pltpu.make_async_remote_copy(
            src_ref=last_out.at[c], dst_ref=last_in.at[sender], send_sem=last_s.at[c], recv_sem=last_r.at[sender],
            device_id=(c, blk), device_id_type=MESH,
        )

    width = quad * 2 * inputs
    turned[...] = gain[...].reshape(width, LANES).T.reshape(stations, blocks, width)
    for r in range(blocks):
        final_out[r] = turned[:, r, :]
    for offset in sorted(range(1, blocks), key=lambda o: -min(o, blocks - o)):
        final_copy(peer_blk(offset), blk).start()
    final_in[blk] = final_out[blk]
    for offset in range(1, blocks):
        r = peer_blk(offset)
        final_copy(r, r).wait_recv()
    for c in range(stations):
        last_out[c] = final_in[:, c, :]

    for c in far_first():
        last_copy(c, stn).start()
    last_in[stn] = last_out[stn]

    def await_last(o, carry):
        c = peer_stn(o)
        last_copy(c, c).wait_recv()
        return carry

    lax.fori_loop(1, stations, await_last, 0)
    for m in range(quad):
        for p in range(2):
            at = (2 * m + p) * inputs
            for n in range(stations // span):
                block = jnp.concatenate(
                    [last_in[n * span + i, :, at : at + inputs] for i in range(span)], axis=1
                )
                for r in range(blocks):
                    k = (r % 2) * half + (r // 2) * quad + m
                    out_ref[p, k : k + 1, n * LANES : (n + 1) * LANES] = block[r : r + 1, :]

    for offset in range(1, blocks):
        final_copy(peer_blk(offset), blk).wait_send()

    def sent_last(o, carry):
        last_copy(peer_stn(o), stn).wait_send()
        return carry

    lax.fori_loop(1, stations, sent_last, 0)


def correlate(stations, blocks, voltages, high, low, taps, phases):
    inputs, channels = voltages.shape[1], taps.shape[1]
    here = voltages.shape[2] // channels
    groups = inputs // GROUP
    places, half = blocks // 2, RADIX // 2
    chunk, quad = half // stations, half // places
    rows = 4 * here + 16
    width = quad * 2 * inputs
    hbm = pl.BlockSpec(memory_space=pl.ANY)
    vmem = pl.BlockSpec(memory_space=pltpu.VMEM)
    dma = pltpu.SemaphoreType.DMA
    return pl.pallas_call(
        functools.partial(correlator_kernel, stations, blocks),
        in_specs=[hbm, hbm, hbm, vmem, vmem],
        out_specs=vmem,
        out_shape=jax.ShapeDtypeStruct((2, RADIX, stations * inputs), F32),
        scratch_shapes=[
            pltpu.VMEM((2, inputs, here * channels), BF16),
            pltpu.VMEM((2, inputs, BEFORE * channels), BF16),
            pltpu.VMEM((2, inputs, AFTER * channels), BF16),
            pltpu.VMEM((2, RADIX, here, inputs, LANES), F32),
            pltpu.VMEM(high.shape, BF16),
            pltpu.VMEM(low.shape, BF16),
            pltpu.VMEM((inputs, LANES), F32),
            pltpu.VMEM((blocks, inputs, LANES), F32),
            pltpu.VMEM((inputs, LANES), F32),
            pltpu.VMEM((2, inputs, LANES), F32),
            pltpu.VMEM((half, 2, here, inputs, LANES), BF16),
            pltpu.VMEM((half, 2, inputs, LANES), BF16),
            pltpu.VMEM((half, inputs, LANES), F32),
            pltpu.VMEM((3, stations, chunk, 4 * here, LANES), F32),
            pltpu.VMEM((3, stations, chunk, rows, LANES), BF16),
            pltpu.VMEM((places, quad, 2, inputs, LANES), BF16),
            pltpu.VMEM((places, quad, 2, inputs, LANES), BF16),
            pltpu.VMEM((quad, 2, inputs, LANES), F32),
            pltpu.VMEM((rows, LANES), F32),
            pltpu.VMEM((stations, blocks, width), F32),
            pltpu.VMEM((blocks, stations, width), F32),
            pltpu.VMEM((blocks, stations, width), F32),
            pltpu.VMEM((stations, blocks, width), F32),
            pltpu.VMEM((stations, blocks, width), F32),
            dma((groups,)),
            dma((2,)),
            dma((2, groups)),
            dma((2, groups)),
            dma((blocks,)),
            dma((blocks,)),
            dma((half,)),
            dma((half,)),
            dma((stations,)),
            dma((stations,)),
            dma((stations,)),
            dma((stations,)),
            dma((places,)),
            dma((places,)),
            dma((places,)),
            dma((places,)),
            dma((blocks,)),
            dma((blocks,)),
            dma((stations,)),
            dma((stations,)),
        ],
        compiler_params=pltpu.CompilerParams(
            collective_id=0, has_side_effects=True, vmem_limit_bytes=62 * 2**20
        ),
        name="correlator",
    )(voltages, high, low, taps, phases)


def on_device(stations, blocks, voltages, taps, model_phase):
    high, low = dft_tables(taps.shape[1])
    phases = model_phase.reshape(-1, LANES)
    return correlate(stations, blocks, voltages, jnp.asarray(high), jnp.asarray(low), taps, phases)


def solution(mesh):
    stations, blocks = mesh.shape["stn"], mesh.shape["blk"]
    in_specs = (P(None, "stn", "blk"), P(), P())
    out_specs = P(None, ("stn", "blk"), None)
    return jax.shard_map(
        functools.partial(on_device, stations, blocks),
        mesh=mesh, in_specs=in_specs, out_specs=out_specs, check_vma=False,
    )
```

```python
import functools
import math

import jax
import jax.numpy as jnp
import ml_dtypes
import numpy as np
from jax import lax
from jax.experimental import pallas as pl
from jax.experimental.pallas import tpu as pltpu
from jax.sharding import PartitionSpec as P

ITERS = 4
EPS = 1e-06
TAPS = 16
BEFORE = 7
AFTER = 8
LANES = 128
GROUP = 16
RADIX = 32
F32 = jnp.float32
BF16 = jnp.bfloat16
MESH = pl.DeviceIdType.MESH


def dft_tables(channels):
    b = np.arange(LANES)
    k = np.arange(RADIX)
    turns = (b[None, :, None] * (k[:, None, None] + RADIX * b[None, None, :])) % channels
    angle = -2.0 * np.pi * turns / channels
    cos, sin = np.cos(angle), np.sin(angle)
    table = np.concatenate(
        [np.concatenate([cos, sin], axis=2), np.concatenate([-sin, cos], axis=2)], axis=1
    ).astype(np.float32)
    high = table.astype(ml_dtypes.bfloat16)
    low = (table - high.astype(np.float32)).astype(ml_dtypes.bfloat16)
    return high, low


def times(z, w):
    re, im = z
    c, s = float(w.real), float(w.imag)
    if abs(s) < 1e-12:
        return (re, im) if c > 0 else (-re, -im)
    if abs(c) < 1e-12:
        return (-im, re) if s > 0 else (im, -re)
    if abs(abs(c) - abs(s)) < 1e-12:
        if c > 0 and s < 0:
            return ((re + im) * c, (im - re) * c)
        if c < 0 and s < 0:
            return ((im - re) * -c, (re + im) * c)
    return (re * c - im * s, re * s + im * c)


def add(x, y):
    return (x[0] + y[0], x[1] + y[1])


def sub(x, y):
    return (x[0] - y[0], x[1] - y[1])


def fft(points):
    size = len(points)
    if size == 1:
        return points
    if size == 2:
        return [add(points[0], points[1]), sub(points[0], points[1])]
    if size == 4:
        even = [add(points[0], points[2]), sub(points[0], points[2])]
        odd = [add(points[1], points[3]), sub(points[1], points[3])]
        turned = (odd[1][1], -odd[1][0])
        return [add(even[0], odd[0]), add(even[1], turned), sub(even[0], odd[0]), sub(even[1], turned)]
    if size == 8:
        even, odd = fft(points[0::2]), fft(points[1::2])
        odd = [times(z, np.exp(-2j * np.pi * i / 8)) for i, z in enumerate(odd)]
        return [add(e, o) for e, o in zip(even, odd)] + [sub(e, o) for e, o in zip(even, odd)]
    outer = size // 4
    result = [None] * size
    firsts = []
    for j in range(outer):
        first = fft([points[j + outer * r] for r in range(4)])
        firsts.append([times(z, np.exp(-2j * np.pi * j * u / size)) for u, z in enumerate(first)])
    for u in range(4):
        second = fft([firsts[j][u] for j in range(outer)])
        for v in range(outer):
            result[u + 4 * v] = second[v]
    return result


def correlator_kernel(
    stations, blocks,
    volt_ref, high_hbm, low_hbm, taps_ref, phases_ref,
    out_ref,
    own, prev, following, work, high_ref, low_ref, power_out, power_in, scale_ref, model_ref,
    near, weights, self_power, back_wide, back_narrow, sum_out, sum_in, norm_out, norm_in, gain, rows_ref,
    numer, turned, side_out, side_in, half_out, half_in, final, last_out, last_in,
    own_sem, table_sem, halo_s, halo_r, power_s, power_r, far_s, far_r, back_s, back_r, total_s, total_r,
    sum_s, sum_r, weight_s, weight_r, norm_s, norm_r, side_s, side_r, half_s, half_r, last_s, last_r,
):
    stn, blk = lax.axis_index("stn"), lax.axis_index("blk")
    channels = taps_ref.shape[1]
    inputs = volt_ref.shape[1]
    here = volt_ref.shape[2] // channels
    groups = inputs // GROUP
    core, place = lax.rem(blk, 2), lax.div(blk, 2)
    partner = blk + 1 - 2 * core
    places = blocks // 2
    half = RADIX // 2
    chunk = half // stations
    quad = half // places
    per = quad // chunk
    spectra = 2 * here
    keep = jnp.where(blk == blocks - 1, 0.0, 1.0)

    def peer_stn(offset):
        return lax.rem(stn + offset, stations)

    def peer_blk(offset):
        return lax.rem(blk + offset, blocks)

    def peer_place(offset):
        return lax.rem(place + offset, places)

    side = math.isqrt(stations)
    row_at, column_at = lax.div(stn, side), lax.rem(stn, side)
    ring = [min(d, side - d) for d in range(side)]
    others = sorted(
        ((dy, dz) for dy in range(side) for dz in range(side) if dy or dz), key=lambda d: -ring[d[0]] - ring[d[1]]
    )

    def far_first():
        for dy, dz in others:
            yield lax.rem(row_at + dy, side) * side + lax.rem(column_at + dz, side)

    def order(turn, q, n):
        offset = q + lax.div(q, 2) * (1 - 2 * lax.rem(q, 2)) if places == 4 else q
        if turn == 0:
            offset = offset + row_at
        r = lax.rem(place + offset, places)
        return r, r * per + lax.rem(n + column_at, per)

    barrier = pltpu.get_barrier_semaphore()
    for offset in range(1, stations):
        pl.semaphore_signal(barrier, inc=1, device_id=(peer_stn(offset), blk), device_id_type=MESH)
    for offset in range(1, blocks):
        pl.semaphore_signal(barrier, inc=1, device_id=(stn, peer_blk(offset)), device_id_type=MESH)

    def rows_of(g):
        return pl.ds(pl.multiple_of(g * GROUP, GROUP), GROUP)

    def own_copy(g):
        return pltpu.make_async_copy(volt_ref.at[:, rows_of(g), :], own.at[:, rows_of(g), :], own_sem.at[g])

    def table_copy(n):
        pair = ((high_hbm, high_ref), (low_hbm, low_ref))[n]
        return pltpu.make_async_copy(*pair, table_sem.at[n])

    def forward(g):
        return pltpu.make_async_remote_copy(
            src_ref=volt_ref.at[:, rows_of(g), pl.ds((here - BEFORE) * channels, BEFORE * channels)],
            dst_ref=prev.at[:, rows_of(g), :], send_sem=halo_s.at[0, g], recv_sem=halo_r.at[0, g],
            device_id=(stn, peer_blk(1)), device_id_type=MESH,
        )

    def backward(g):
        return pltpu.make_async_remote_copy(
            src_ref=volt_ref.at[:, rows_of(g), pl.ds(0, AFTER * channels)],
            dst_ref=following.at[:, rows_of(g), :], send_sem=halo_s.at[1, g], recv_sem=halo_r.at[1, g],
            device_id=(stn, peer_blk(blocks - 1)), device_id_type=MESH,
        )

    for g in range(groups):
        own_copy(g).start()
    for n in range(2):
        table_copy(n).start()
    pl.semaphore_wait(barrier, stations + blocks - 2)
    for g in range(groups):

        @pl.when(blk < blocks - 1)
        def _():
            forward(g).start()

        backward(g).start()

    @pl.when(blk == 0)
    def _():
        def clear(j, carry):
            at = pl.ds(pl.multiple_of(j * channels, channels), channels)
            for p in range(2):
                prev[p, :, at] = jnp.zeros((inputs, channels), BF16)
            return carry

        lax.fori_loop(0, BEFORE, clear, 0)

    def tap_rows(start):
        return [taps_ref[k : k + 1, pl.ds(start, LANES)] for k in range(TAPS)]

    def accumulate(sums, source, g, p, start, first, count, rows):
        for j in range(first, first + count):
            at = pl.multiple_of(start + (j - first) * channels, LANES)
            sample = source[p, rows_of(g), pl.ds(at, LANES)].astype(F32)
            for k in range(TAPS):
                u = j - k
                if 0 <= u < here:
                    term = sample * rows[k]
                    sums[u] = term if sums[u] is None else sums[u] + term

    def filter_own(g, carry):
        own_copy(g).wait()

        def part(a, carry):
            start = pl.multiple_of(a * LANES, LANES)
            rows = tap_rows(start)
            for p in range(2):
                sums = [None] * here
                accumulate(sums, own, g, p, start, BEFORE, here, rows)
                for u in range(here):
                    work[p, a, u, rows_of(g), :] = sums[u] if u < here - AFTER else sums[u] * keep
            return carry

        return lax.fori_loop(0, RADIX, part, carry)

    lax.fori_loop(0, groups, filter_own, 0)
    span = LANES // inputs
    row = phases_ref[pl.ds(lax.div(stn, span), 1), :]
    lane = lax.broadcasted_iota(jnp.int32, (inputs, LANES), 1)
    wanted = lax.broadcasted_iota(jnp.int32, (inputs, LANES), 0) + lax.rem(stn, span) * inputs
    phase = jnp.sum(jnp.where(lane == wanted, row, 0.0), axis=1, keepdims=True)
    phase = jnp.broadcast_to(phase, (inputs, LANES))
    model_ref[0] = jnp.cos(phase)
    model_ref[1] = jnp.sin(phase)
    all_re, all_im = jnp.cos(phases_ref[...]), jnp.sin(phases_ref[...])
    first = jnp.sum(all_re * all_re + all_im * all_im)
    rows_ref[...] = jnp.zeros(rows_ref.shape, F32)
    for n in range(2):
        table_copy(n).wait()

    def filter_rest(g, low_half, high_half):
        spots = [u for u in range(here) if (u < AFTER and low_half) or (u >= AFTER and high_half)]

        def part(a, total):
            start = pl.multiple_of(a * LANES, LANES)
            rows = tap_rows(start)
            for p in range(2):
                sums = [work[p, a, u, rows_of(g), :] if u in spots else None for u in range(here)]
                if low_half:
                    accumulate(sums, prev, g, p, start, 0, BEFORE, rows)
                if high_half:
                    accumulate(sums, following, g, p, start, BEFORE + here, AFTER, rows)
                for u in spots:
                    work[p, a, u, rows_of(g), :] = sums[u]
                    total = total + sums[u] * sums[u]
            return total

        return lax.fori_loop(0, RADIX, part, jnp.zeros((GROUP, LANES), F32))

    def transform(g, first_spot, count):
        def turn(s, carry):
            for part in range(GROUP // 8):
                rows = pl.ds(g * GROUP + 8 * part, 8)
                points = [(work[0, a, s, rows, :], work[1, a, s, rows, :]) for a in range(RADIX)]
                for k, (re, im) in enumerate(fft(points)):
                    work[0, k, s, rows, :] = re
                    work[1, k, s, rows, :] = im
            return carry

        lax.fori_loop(first_spot, first_spot + count, turn, 0)

        def second(k, carry):
            spots = pl.ds(first_spot, count)
            both = jnp.concatenate(
                [work[p, k, spots, rows_of(g), :].reshape(count * GROUP, LANES) for p in range(2)], axis=1
            )
            high = both.astype(BF16)
            low = (both - high.astype(F32)).astype(BF16)
            table = high_ref[k]
            out = jnp.dot(
                jnp.concatenate([high, low, high], axis=1),
                jnp.concatenate([table, table, low_ref[k]], axis=0),
                preferred_element_type=F32,
            )
            out = out.reshape(count, GROUP, 2 * LANES)
            work[0, k, spots, rows_of(g), :] = out[:, :, :LANES]
            work[1, k, spots, rows_of(g), :] = out[:, :, LANES:]
            return carry

        lax.fori_loop(0, RADIX, second, 0, unroll=4)

    def await_prev(g):
        @pl.when(blk > 0)
        def _():
            forward(g).wait_recv()

    def power_copy(r, sender):
        return pltpu.make_async_remote_copy(
            src_ref=power_out, dst_ref=power_in.at[sender], send_sem=power_s.at[r], recv_sem=power_r.at[sender],
            device_id=(stn, r), device_id_type=MESH,
        )

    for g in range(groups):
        await_prev(g)
        if g < groups - 1:
            backward(g).wait_recv()
            total = filter_rest(g, True, True)
        else:
            total = filter_rest(g, True, False)
            transform(g, 0, AFTER)
            backward(g).wait_recv()
            total = total + filter_rest(g, False, True)
        total = jnp.sum(total, axis=1, keepdims=True) * channels
        power_out[g * GROUP : (g + 1) * GROUP, :] = jnp.broadcast_to(total, (GROUP, LANES))
        if g < groups - 1:
            transform(g, 0, here)
        else:
            for offset in range(1, blocks):
                power_copy(peer_blk(offset), blk).start()
            transform(g, AFTER, here - AFTER)

    power = power_out[...]
    for offset in range(1, blocks):
        r = peer_blk(offset)
        power_copy(r, r).wait_recv()
        power = power + power_in[r]
    scale_ref[...] = 1.0 / jnp.sqrt(power / (here * blocks * channels) + EPS)
    for offset in range(1, blocks):
        power_copy(peer_blk(offset), blk).wait_send()
    for g in range(groups):

        @pl.when(blk < blocks - 1)
        def _():
            forward(g).wait_send()

        backward(g).wait_send()

    def far_rows(k, s):
        return pl.ds(pl.multiple_of((k * here + s) * LANES, LANES), LANES)

    def far_copy(k):
        part = pl.ds(pl.multiple_of(k * here * LANES, here * LANES), here * LANES)
        return pltpu.make_async_remote_copy(
            src_ref=own.at[:, :, part], dst_ref=following.at[:, :, part], send_sem=far_s.at[k], recv_sem=far_r.at[k],
            device_id=(stn, partner), device_id_type=MESH,
        )

    def hand_over(i, carry):
        c = order(0, lax.div(i, quad), lax.div(lax.rem(i, quad), chunk))[1]
        k = c * chunk + lax.rem(i, chunk)
        scale = scale_ref[...]
        for s in range(here):
            for p in range(2):
                own[p, :, far_rows(k, s)] = (work[p, (1 - core) * half + k, s] * scale).astype(BF16)
        far_copy(k).start()
        return carry

    lax.fori_loop(0, half, hand_over, 0)

    def quantize(k):
        far_copy(k).wait_recv()
        scale = scale_ref[...]
        total = jnp.zeros((inputs, LANES), F32)
        for s in range(here):
            for p in range(2):
                value = (work[p, core * half + k, s] * scale).astype(BF16)
                near[k, p, s] = value
                wide = value.astype(F32)
                wider = following[p, :, far_rows(k, s)].astype(F32)
                total = total + (wide * wide + wider * wider)
        self_power[k] = total

    def sample(k, p, t):
        return (near[k, p, t] if t < here else following[p, :, far_rows(k, t - here)]).astype(F32)

    def begin(m, carry):
        gain[m, 0] = jnp.ones((inputs, LANES), F32)
        gain[m, 1] = jnp.zeros((inputs, LANES), F32)
        return carry

    lax.fori_loop(0, quad, begin, 0)

    def back_parts(turn):
        return [(back_wide if turn == 0 else back_narrow).at[n] for n in range(3)]

    def back_copy(turn, c, sender):
        back_out, back_in, _ = back_parts(turn)
        return pltpu.make_async_remote_copy(
            src_ref=back_out.at[c], dst_ref=back_in.at[sender], send_sem=back_s.at[c], recv_sem=back_r.at[sender],
            device_id=(c, blk), device_id_type=MESH,
        )

    def total_copy(turn, c, owner):
        _, _, back_sum = back_parts(turn)
        return pltpu.make_async_remote_copy(
            src_ref=back_sum.at[owner], dst_ref=back_sum.at[owner], send_sem=total_s.at[c], recv_sem=total_r.at[owner],
            device_id=(c, blk), device_id_type=MESH,
        )

    def sum_copy(r, sender):
        return pltpu.make_async_remote_copy(
            src_ref=sum_out.at[r], dst_ref=sum_in.at[sender], send_sem=sum_s.at[r], recv_sem=sum_r.at[sender],
            device_id=(stn, 2 * r + core), device_id_type=MESH,
        )

    places_far_first = sorted(range(1, places), key=lambda o: -min(o, places - o))

    def weight_copy(r, owner, m):
        part = weights.at[owner * quad + m]
        return pltpu.make_async_remote_copy(
            src_ref=part, dst_ref=part, send_sem=weight_s.at[r, m], recv_sem=weight_r.at[owner, m],
            device_id=(stn, 2 * r + core), device_id_type=MESH,
        )

    def norm_copy(turn, c, sender):
        return pltpu.make_async_remote_copy(
            src_ref=norm_out.at[turn], dst_ref=norm_in.at[turn, sender],
            send_sem=norm_s.at[turn, c], recv_sem=norm_r.at[turn, sender],
            device_id=(c, blk), device_id_type=MESH,
        )

    def weight(turn, k, p):
        return model_ref[p] if turn == 0 else weights[k, p].astype(F32)

    def down(turn, k, c, j):
        w_re, w_im = weight(turn, k, 0), weight(turn, k, 1)
        for t in range(spectra):
            q_re, q_im = sample(k, 0, t), sample(k, 1, t)
            rows_ref[t : t + 1, :] = jnp.sum(q_re * w_re + q_im * w_im, axis=0, keepdims=True)
            rows_ref[spectra + t : spectra + t + 1, :] = jnp.sum(q_re * w_im - q_im * w_re, axis=0, keepdims=True)
        back_out = back_parts(turn)[0]
        back_out[c, j] = rows_ref[...].astype(back_out.dtype)

    def up(turn, k, r, j):
        c, jj = lax.div(k, chunk), lax.rem(k, chunk)
        back = back_parts(turn)[2]
        rows_ref[...] = back[c, jj].astype(F32)
        h_re = jnp.zeros((inputs, LANES), F32)
        h_im = jnp.zeros((inputs, LANES), F32)
        for t in range(spectra):
            q_re, q_im = sample(k, 0, t), sample(k, 1, t)
            b_re, b_im = rows_ref[t : t + 1, :], rows_ref[spectra + t : spectra + t + 1, :]
            h_re = h_re + (q_re * b_re - q_im * b_im)
            h_im = h_im + (q_re * b_im + q_im * b_re)
        own_power = self_power[k]
        h_re = h_re - own_power * weight(turn, k, 0)
        h_im = h_im - own_power * weight(turn, k, 1)
        if turn < ITERS - 1:
            sum_out[r, j, 0] = h_re.astype(BF16)
            sum_out[r, j, 1] = h_im.astype(BF16)
        else:
            m_re, m_im = model_ref[0], model_ref[1]
            numer[0, j] = m_re * h_re + m_im * h_im
            numer[1, j] = m_re * h_im - m_im * h_re

    def side_copy(r, sender):
        return pltpu.make_async_remote_copy(
            src_ref=side_out.at[r], dst_ref=side_in.at[sender], send_sem=side_s.at[r], recv_sem=side_r.at[sender],
            device_id=(stn, r), device_id_type=MESH,
        )

    def half_copy(r, sender, q):
        return pltpu.make_async_remote_copy(
            src_ref=half_out.at[r, q], dst_ref=half_in.at[sender, q],
            send_sem=half_s.at[r, q], recv_sem=half_r.at[sender, q],
            device_id=(stn, r), device_id_type=MESH,
        )

    def last_copy(c, sender):
        return pltpu.make_async_remote_copy(
            src_ref=last_out.at[c], dst_ref=last_in.at[sender], send_sem=last_s.at[c], recv_sem=last_r.at[sender],
            device_id=(c, blk), device_id_type=MESH,
        )

    blocks_far_first = sorted(range(1, blocks), key=lambda o: -min(o, blocks - o))

    def by_block(value, n):
        turned[n] = value.reshape(quad * inputs, LANES).T.reshape(stations, blocks, quad * inputs)
        return [turned[n, :, r, :] for r in range(blocks)]

    def add_norms(turn):
        def norms(o, total):
            c = peer_stn(o)
            norm_copy(turn - 1, c, c).wait_recv()
            return total + norm_in[turn - 1, c]

        rows_ref[0:8, :] = lax.fori_loop(1, stations, norms, norm_out[turn - 1])

    def denominator(norm, w_re, w_im):
        return norm - (w_re * w_re + w_im * w_im) + EPS

    def last_side():
        add_norms(ITERS - 1)
        m_re, m_im = model_ref[0], model_ref[1]
        for m in range(quad):
            g_re, g_im = gain[m, 0], gain[m, 1]
            w_re = g_re * m_re - g_im * m_im
            w_im = g_re * m_im + g_im * m_re
            numer[0, m] = 1.0 / denominator(rows_ref[m : m + 1, :], w_re, w_im)
        for n, value in enumerate((gain[:, 0], gain[:, 1], numer[0])):
            for r, part in enumerate(by_block(value, n)):
                side_out[r, n] = part
        for offset in blocks_far_first:
            side_copy(peer_blk(offset), blk).start()
        side_in[blk] = side_out[blk]

    def send_half(q):
        for p in range(2):
            for r, part in enumerate(by_block(numer[p], p)):
                half_out[r, q, p] = part.astype(BF16)
        for offset in blocks_far_first:
            half_copy(peer_blk(offset), blk, q).start()
        half_in[blk, q] = half_out[blk, q]

    for turn in range(ITERS):
        def down_part(o, carry):
            r = order(turn, o, 0)[0]
            def one(n, carry):
                c = order(turn, o, n)[1]

                def each(j, carry):
                    if turn > 0:

                        @pl.when(o > 0)
                        def _():
                            weight_copy(r, r, lax.rem(c * chunk + j, quad)).wait_recv()

                    if turn == 0:
                        quantize(c * chunk + j)
                    down(turn, c * chunk + j, c, j)
                    return carry

                lax.fori_loop(0, chunk, each, 0)

                @pl.when(c != stn)
                def _():
                    back_copy(turn, c, stn).start()

                return carry

            return lax.fori_loop(0, per, one, carry)

        lax.fori_loop(0, places, down_part, 0)

        def await_back(o, carry):
            c = peer_stn(o)
            back_copy(turn, c, c).wait_recv()
            return carry

        if chunk > 1:
            lax.fori_loop(1, stations, await_back, 0)

        def gather(j, carry):
            back_out, back_in, back_sum = back_parts(turn)
            total = back_out[stn, j].astype(F32)

            def more(o, total):
                if chunk == 1:
                    await_back(o, 0)
                return total + back_in[peer_stn(o), j].astype(F32)

            total = lax.fori_loop(1, stations, more, total)
            back_sum[stn, j] = total.astype(back_sum.dtype)
            return carry

        lax.fori_loop(0, chunk, gather, 0)
        for c in far_first():
            total_copy(turn, c, stn).start()
        if turn == ITERS - 1:
            last_side()

        def up_part(o):
            r = peer_place(o)
            for n in range(per):
                c = r * per + n

                @pl.when(c != stn)
                def _():
                    total_copy(turn, c, c).wait_recv()

            def each(j, carry):
                up(turn, r * quad + j, r, j)
                return carry

            lax.fori_loop(0, quad, each, 0)
            if turn == ITERS - 1:
                send_half(r)
            elif o > 0:
                sum_copy(r, place).start()

        for o in sorted(range(places), key=lambda o: -min(o, places - o)):
            up_part(o)

        def settle(o, carry):
            c = peer_stn(o)
            back_copy(turn, c, stn).wait_send()
            total_copy(turn, c, stn).wait_send()
            return carry

        lax.fori_loop(1, stations, settle, 0)

        def await_sum(o, carry):
            r = peer_place(o)
            if turn < ITERS - 1:
                sum_copy(r, r).wait_recv()
            if turn > 0:
                for m in range(quad):
                    weight_copy(r, place, m).wait_send()
            return carry

        lax.fori_loop(1, places, await_sum, 0)

        if turn == ITERS - 1:
            break
        if turn > 0:
            add_norms(turn)

        for m in range(quad):
            k = place * quad + m
            total_re = sum_out[place, m, 0].astype(F32)
            total_im = sum_out[place, m, 1].astype(F32)

            def more(o, totals):
                r = peer_place(o)
                return totals[0] + sum_in[r, m, 0].astype(F32), totals[1] + sum_in[r, m, 1].astype(F32)

            total_re, total_im = lax.fori_loop(1, places, more, (total_re, total_im))
            m_re, m_im = model_ref[0], model_ref[1]
            g_re, g_im = gain[m, 0], gain[m, 1]
            w_re = g_re * m_re - g_im * m_im
            w_im = g_re * m_im + g_im * m_re
            if turn == 0:
                norm = first
            else:
                norm = rows_ref[m : m + 1, :]
            denom = denominator(norm, w_re, w_im)
            new_re = (m_re * total_re + m_im * total_im) / denom
            new_im = (m_re * total_im - m_im * total_re) / denom
            if turn % 2 == 1:
                new_re = (new_re + g_re) * 0.5
                new_im = (new_im + g_im) * 0.5
            gain[m, 0] = new_re
            gain[m, 1] = new_im
            w_re = new_re * m_re - new_im * m_im
            w_im = new_re * m_im + new_im * m_re
            weights[k, 0] = w_re.astype(BF16)
            weights[k, 1] = w_im.astype(BF16)
            for o in places_far_first:
                weight_copy(peer_place(o), place, m).start()
            norm_out[turn, m : m + 1, :] = jnp.sum(w_re * w_re + w_im * w_im, axis=0, keepdims=True)

        for m in range(quad, 8):
            norm_out[turn, m : m + 1, :] = jnp.zeros((1, LANES), F32)
        for c in far_first():
            norm_copy(turn, c, stn).start()

        def sent(o, carry):
            sum_copy(peer_place(o), place).wait_send()
            return carry

        lax.fori_loop(1, places, sent, 0)

    def handed(k, carry):
        far_copy(k).wait_send()
        return carry

    lax.fori_loop(0, half, handed, 0)

    def normed(o, carry):
        for turn in range(ITERS - 1):
            norm_copy(turn, peer_stn(o), stn).wait_send()
        return carry

    lax.fori_loop(1, stations, normed, 0)

    for offset in blocks_far_first:
        r = peer_blk(offset)
        side_copy(r, r).wait_recv()
        for q in range(places):
            half_copy(r, r, q).wait_recv()
    for half_core in range(2):
        for q in range(places):
            owner = 2 * q + half_core
            for p in range(2):
                total = half_in[half_core, q, p].astype(F32)
                for n in range(1, places):
                    total = total + half_in[2 * n + half_core, q, p].astype(F32)
                total = total * side_in[owner, 2]
                if ITERS % 2 == 0:
                    total = (total + side_in[owner, p]) * 0.5
                final[(half_core * places + q) * 2 + p] = total
    for c in range(stations):
        last_out[c] = final[:, c, :]
    for c in far_first():
        last_copy(c, stn).start()
    last_in[stn] = last_out[stn]

    def await_last(o, carry):
        c = peer_stn(o)
        last_copy(c, c).wait_recv()
        return carry

    lax.fori_loop(1, stations, await_last, 0)
    for m in range(quad):
        for n in range(stations // span):
            block = jnp.concatenate(
                [last_in[n * span + i, :, m * inputs : (m + 1) * inputs] for i in range(span)], axis=1
            )
            for half_core in range(2):
                for q in range(places):
                    for p in range(2):
                        k = half_core * half + q * quad + m
                        at = (half_core * places + q) * 2 + p
                        out_ref[p, k : k + 1, n * LANES : (n + 1) * LANES] = block[at : at + 1, :]

    for offset in blocks_far_first:
        r = peer_blk(offset)
        side_copy(r, blk).wait_send()
        for q in range(places):
            half_copy(r, blk, q).wait_send()

    def sent_last(o, carry):
        last_copy(peer_stn(o), stn).wait_send()
        return carry

    lax.fori_loop(1, stations, sent_last, 0)


def correlate(stations, blocks, voltages, high, low, taps, phases):
    inputs, channels = voltages.shape[1], taps.shape[1]
    here = voltages.shape[2] // channels
    groups = inputs // GROUP
    places, half = blocks // 2, RADIX // 2
    chunk, quad = half // stations, half // places
    rows = 4 * here
    hbm = pl.BlockSpec(memory_space=pl.ANY)
    vmem = pl.BlockSpec(memory_space=pltpu.VMEM)
    dma = pltpu.SemaphoreType.DMA
    return pl.pallas_call(
        functools.partial(correlator_kernel, stations, blocks),
        in_specs=[hbm, hbm, hbm, vmem, vmem],
        out_specs=vmem,
        out_shape=jax.ShapeDtypeStruct((2, RADIX, stations * inputs), F32),
        scratch_shapes=[
            pltpu.VMEM((2, inputs, here * channels), BF16),
            pltpu.VMEM((2, inputs, BEFORE * channels), BF16),
            pltpu.VMEM((2, inputs, AFTER * channels), BF16),
            pltpu.VMEM((2, RADIX, here, inputs, LANES), F32),
            pltpu.VMEM(high.shape, BF16),
            pltpu.VMEM(low.shape, BF16),
            pltpu.VMEM((inputs, LANES), F32),
            pltpu.VMEM((blocks, inputs, LANES), F32),
            pltpu.VMEM((inputs, LANES), F32),
            pltpu.VMEM((2, inputs, LANES), F32),
            pltpu.VMEM((half, 2, here, inputs, LANES), BF16),
            pltpu.VMEM((half, 2, inputs, LANES), BF16),
            pltpu.VMEM((half, inputs, LANES), F32),
            pltpu.VMEM((3, stations, chunk, 4 * here, LANES), F32),
            pltpu.VMEM((3, stations, chunk, rows, LANES), BF16),
            pltpu.VMEM((places, quad, 2, inputs, LANES), BF16),
            pltpu.VMEM((places, quad, 2, inputs, LANES), BF16),
            pltpu.VMEM((ITERS - 1, 8, LANES), F32),
            pltpu.VMEM((ITERS - 1, stations, 8, LANES), F32),
            pltpu.VMEM((quad, 2, inputs, LANES), F32),
            pltpu.VMEM((rows, LANES), F32),
            pltpu.VMEM((2, quad, inputs, LANES), F32),
            pltpu.VMEM((3, stations, blocks, quad * inputs), F32),
            pltpu.VMEM((blocks, 3, stations, quad * inputs), F32),
            pltpu.VMEM((blocks, 3, stations, quad * inputs), F32),
            pltpu.VMEM((blocks, places, 2, stations, quad * inputs), BF16),
            pltpu.VMEM((blocks, places, 2, stations, quad * inputs), BF16),
            pltpu.VMEM((4 * places, stations, quad * inputs), F32),
            pltpu.VMEM((stations, 4 * places, quad * inputs), F32),
            pltpu.VMEM((stations, 4 * places, quad * inputs), F32),
            dma((groups,)),
            dma((2,)),
            dma((2, groups)),
            dma((2, groups)),
            dma((blocks,)),
            dma((blocks,)),
            dma((half,)),
            dma((half,)),
            dma((stations,)),
            dma((stations,)),
            dma((stations,)),
            dma((stations,)),
            dma((places,)),
            dma((places,)),
            dma((places, quad)),
            dma((places, quad)),
            dma((ITERS - 1, stations)),
            dma((ITERS - 1, stations)),
            dma((blocks,)),
            dma((blocks,)),
            dma((blocks, places)),
            dma((blocks, places)),
            dma((stations,)),
            dma((stations,)),
        ],
        compiler_params=pltpu.CompilerParams(
            collective_id=0, has_side_effects=True, vmem_limit_bytes=62 * 2**20
        ),
        name="correlator",
    )(voltages, high, low, taps, phases)


def on_device(stations, blocks, voltages, taps, model_phase):
    high, low = dft_tables(taps.shape[1])
    phases = model_phase.reshape(-1, LANES)
    return correlate(stations, blocks, voltages, jnp.asarray(high), jnp.asarray(low), taps, phases)


def solution(mesh):
    stations, blocks = mesh.shape["stn"], mesh.shape["blk"]
    in_specs = (P(None, "stn", "blk"), P(), P())
    out_specs = P(None, ("stn", "blk"), None)
    return jax.shard_map(
        functools.partial(on_device, stations, blocks),
        mesh=mesh, in_specs=in_specs, out_specs=out_specs, check_vma=False,
    )
```

```python
import functools
import math

import jax
import jax.numpy as jnp
import ml_dtypes
import numpy as np
from jax import lax
from jax.experimental import pallas as pl
from jax.experimental.pallas import tpu as pltpu
from jax.sharding import PartitionSpec as P

ITERS = 4
EPS = 1e-06
TAPS = 16
BEFORE = 7
AFTER = 8
LANES = 128
GROUP = 16
RADIX = 32
F32 = jnp.float32
BF16 = jnp.bfloat16
MESH = pl.DeviceIdType.MESH


def dft_tables(channels):
    b = np.arange(LANES)
    k = np.arange(RADIX)
    turns = (b[None, :, None] * (k[:, None, None] + RADIX * b[None, None, :])) % channels
    angle = -2.0 * np.pi * turns / channels
    cos, sin = np.cos(angle), np.sin(angle)
    table = np.concatenate(
        [np.concatenate([cos, sin], axis=2), np.concatenate([-sin, cos], axis=2)], axis=1
    ).astype(np.float32)
    high = table.astype(ml_dtypes.bfloat16)
    low = (table - high.astype(np.float32)).astype(ml_dtypes.bfloat16)
    return high, low


def times(z, w):
    re, im = z
    c, s = float(w.real), float(w.imag)
    if abs(s) < 1e-12:
        return (re, im) if c > 0 else (-re, -im)
    if abs(c) < 1e-12:
        return (-im, re) if s > 0 else (im, -re)
    if abs(abs(c) - abs(s)) < 1e-12:
        if c > 0 and s < 0:
            return ((re + im) * c, (im - re) * c)
        if c < 0 and s < 0:
            return ((im - re) * -c, (re + im) * c)
    return (re * c - im * s, re * s + im * c)


def add(x, y):
    return (x[0] + y[0], x[1] + y[1])


def sub(x, y):
    return (x[0] - y[0], x[1] - y[1])


def fft(points):
    size = len(points)
    if size == 1:
        return points
    if size == 2:
        return [add(points[0], points[1]), sub(points[0], points[1])]
    if size == 4:
        even = [add(points[0], points[2]), sub(points[0], points[2])]
        odd = [add(points[1], points[3]), sub(points[1], points[3])]
        turned = (odd[1][1], -odd[1][0])
        return [add(even[0], odd[0]), add(even[1], turned), sub(even[0], odd[0]), sub(even[1], turned)]
    if size == 8:
        even, odd = fft(points[0::2]), fft(points[1::2])
        odd = [times(z, np.exp(-2j * np.pi * i / 8)) for i, z in enumerate(odd)]
        return [add(e, o) for e, o in zip(even, odd)] + [sub(e, o) for e, o in zip(even, odd)]
    outer = size // 4
    result = [None] * size
    firsts = []
    for j in range(outer):
        first = fft([points[j + outer * r] for r in range(4)])
        firsts.append([times(z, np.exp(-2j * np.pi * j * u / size)) for u, z in enumerate(first)])
    for u in range(4):
        second = fft([firsts[j][u] for j in range(outer)])
        for v in range(outer):
            result[u + 4 * v] = second[v]
    return result


def correlator_kernel(
    stations, blocks,
    volt_ref, high_hbm, low_hbm, taps_ref, phases_ref,
    out_ref,
    own, prev, following, work, high_ref, low_ref, power_out, power_in, scale_ref, model_ref,
    near, weights, self_power, back_wide, back_narrow, sum_out, sum_in, norm_out, norm_in, gain, rows_ref,
    numer, turned, side_out, side_in, half_out, half_in, final, last_out, last_in,
    own_sem, table_sem, halo_s, halo_r, power_s, power_r, far_s, far_r, back_s, back_r, total_s, total_r,
    sum_s, sum_r, weight_s, weight_r, norm_s, norm_r, side_s, side_r, half_s, half_r, last_s, last_r,
):
    stn, blk = lax.axis_index("stn"), lax.axis_index("blk")
    channels = taps_ref.shape[1]
    inputs = volt_ref.shape[1]
    here = volt_ref.shape[2] // channels
    groups = inputs // GROUP
    core, place = lax.rem(blk, 2), lax.div(blk, 2)
    partner = blk + 1 - 2 * core
    places = blocks // 2
    half = RADIX // 2
    chunk = half // stations
    quad = half // places
    per = quad // chunk
    spectra = 2 * here
    keep = jnp.where(blk == blocks - 1, 0.0, 1.0)

    def peer_stn(offset):
        return lax.rem(stn + offset, stations)

    def peer_blk(offset):
        return lax.rem(blk + offset, blocks)

    def peer_place(offset):
        return lax.rem(place + offset, places)

    side = math.isqrt(stations)
    row_at, column_at = lax.div(stn, side), lax.rem(stn, side)
    ring = [min(d, side - d) for d in range(side)]
    others = sorted(
        ((dy, dz) for dy in range(side) for dz in range(side) if dy or dz), key=lambda d: -ring[d[0]] - ring[d[1]]
    )

    def far_first():
        for dy, dz in others:
            yield lax.rem(row_at + dy, side) * side + lax.rem(column_at + dz, side)

    def order(turn, q, n):
        offset = q + lax.div(q, 2) * (1 - 2 * lax.rem(q, 2)) if places == 4 else q
        if turn == 0:
            offset = offset + row_at
        r = lax.rem(place + offset, places)
        return r, r * per + lax.rem(n + column_at, per)

    barrier = pltpu.get_barrier_semaphore()
    for offset in range(1, stations):
        pl.semaphore_signal(barrier, inc=1, device_id=(peer_stn(offset), blk), device_id_type=MESH)
    for offset in range(1, blocks):
        pl.semaphore_signal(barrier, inc=1, device_id=(stn, peer_blk(offset)), device_id_type=MESH)

    def rows_of(g):
        return pl.ds(pl.multiple_of(g * GROUP, GROUP), GROUP)

    def own_copy(g):
        return pltpu.make_async_copy(volt_ref.at[:, rows_of(g), :], own.at[:, rows_of(g), :], own_sem.at[g])

    def table_copy(n):
        pair = ((high_hbm, high_ref), (low_hbm, low_ref))[n]
        return pltpu.make_async_copy(*pair, table_sem.at[n])

    def forward(g):
        return pltpu.make_async_remote_copy(
            src_ref=volt_ref.at[:, rows_of(g), pl.ds((here - BEFORE) * channels, BEFORE * channels)],
            dst_ref=prev.at[:, rows_of(g), :], send_sem=halo_s.at[0, g], recv_sem=halo_r.at[0, g],
            device_id=(stn, peer_blk(1)), device_id_type=MESH,
        )

    def backward(g):
        return pltpu.make_async_remote_copy(
            src_ref=volt_ref.at[:, rows_of(g), pl.ds(0, AFTER * channels)],
            dst_ref=following.at[:, rows_of(g), :], send_sem=halo_s.at[1, g], recv_sem=halo_r.at[1, g],
            device_id=(stn, peer_blk(blocks - 1)), device_id_type=MESH,
        )

    for g in range(groups):
        own_copy(g).start()
    for n in range(2):
        table_copy(n).start()
    pl.semaphore_wait(barrier, stations + blocks - 2)
    for g in range(groups):

        @pl.when(blk < blocks - 1)
        def _():
            forward(g).start()

        backward(g).start()

    @pl.when(blk == 0)
    def _():
        def clear(j, carry):
            at = pl.ds(pl.multiple_of(j * channels, channels), channels)
            for p in range(2):
                prev[p, :, at] = jnp.zeros((inputs, channels), BF16)
            return carry

        lax.fori_loop(0, BEFORE, clear, 0)

    def tap_rows(start):
        return [taps_ref[k : k + 1, pl.ds(start, LANES)] for k in range(TAPS)]

    def accumulate(sums, source, g, p, start, first, count, rows):
        for j in range(first, first + count):
            at = pl.multiple_of(start + (j - first) * channels, LANES)
            sample = source[p, rows_of(g), pl.ds(at, LANES)].astype(F32)
            for k in range(TAPS):
                u = j - k
                if 0 <= u < here:
                    term = sample * rows[k]
                    sums[u] = term if sums[u] is None else sums[u] + term

    def filter_own(g, carry):
        own_copy(g).wait()

        def part(a, carry):
            start = pl.multiple_of(a * LANES, LANES)
            rows = tap_rows(start)
            for p in range(2):
                sums = [None] * here
                accumulate(sums, own, g, p, start, BEFORE, here, rows)
                for u in range(here):
                    work[p, a, u, rows_of(g), :] = sums[u] if u < here - AFTER else sums[u] * keep
            return carry

        return lax.fori_loop(0, RADIX, part, carry)

    lax.fori_loop(0, groups, filter_own, 0)
    span = LANES // inputs
    row = phases_ref[pl.ds(lax.div(stn, span), 1), :]
    lane = lax.broadcasted_iota(jnp.int32, (inputs, LANES), 1)
    wanted = lax.broadcasted_iota(jnp.int32, (inputs, LANES), 0) + lax.rem(stn, span) * inputs
    phase = jnp.sum(jnp.where(lane == wanted, row, 0.0), axis=1, keepdims=True)
    phase = jnp.broadcast_to(phase, (inputs, LANES))
    model_ref[0] = jnp.cos(phase)
    model_ref[1] = jnp.sin(phase)
    all_re, all_im = jnp.cos(phases_ref[...]), jnp.sin(phases_ref[...])
    first = jnp.sum(all_re * all_re + all_im * all_im)
    rows_ref[...] = jnp.zeros(rows_ref.shape, F32)
    for n in range(2):
        table_copy(n).wait()

    def filter_rest(g, low_half, high_half):
        spots = [u for u in range(here) if (u < AFTER and low_half) or (u >= AFTER and high_half)]

        def part(a, total):
            start = pl.multiple_of(a * LANES, LANES)
            rows = tap_rows(start)
            for p in range(2):
                sums = [work[p, a, u, rows_of(g), :] if u in spots else None for u in range(here)]
                if low_half:
                    accumulate(sums, prev, g, p, start, 0, BEFORE, rows)
                if high_half:
                    accumulate(sums, following, g, p, start, BEFORE + here, AFTER, rows)
                for u in spots:
                    work[p, a, u, rows_of(g), :] = sums[u]
                    total = total + sums[u] * sums[u]
            return total

        return lax.fori_loop(0, RADIX, part, jnp.zeros((GROUP, LANES), F32))

    def transform(g, first_spot, count):
        def turn(s, carry):
            for part in range(GROUP // 8):
                rows = pl.ds(g * GROUP + 8 * part, 8)
                points = [(work[0, a, s, rows, :], work[1, a, s, rows, :]) for a in range(RADIX)]
                for k, (re, im) in enumerate(fft(points)):
                    work[0, k, s, rows, :] = re
                    work[1, k, s, rows, :] = im
            return carry

        lax.fori_loop(first_spot, first_spot + count, turn, 0)

        def second(k, carry):
            spots = pl.ds(first_spot, count)
            both = jnp.concatenate(
                [work[p, k, spots, rows_of(g), :].reshape(count * GROUP, LANES) for p in range(2)], axis=1
            )
            high = both.astype(BF16)
            low = (both - high.astype(F32)).astype(BF16)
            table = high_ref[k]
            out = jnp.dot(
                jnp.concatenate([high, low, high], axis=1),
                jnp.concatenate([table, table, low_ref[k]], axis=0),
                preferred_element_type=F32,
            )
            out = out.reshape(count, GROUP, 2 * LANES)
            work[0, k, spots, rows_of(g), :] = out[:, :, :LANES]
            work[1, k, spots, rows_of(g), :] = out[:, :, LANES:]
            return carry

        lax.fori_loop(0, RADIX, second, 0, unroll=8)

    def await_prev(g):
        @pl.when(blk > 0)
        def _():
            forward(g).wait_recv()

    def power_copy(r, sender):
        return pltpu.make_async_remote_copy(
            src_ref=power_out, dst_ref=power_in.at[sender], send_sem=power_s.at[r], recv_sem=power_r.at[sender],
            device_id=(stn, r), device_id_type=MESH,
        )

    for g in range(groups):
        await_prev(g)
        if g < groups - 1:
            backward(g).wait_recv()
            total = filter_rest(g, True, True)
        else:
            total = filter_rest(g, True, False)
            transform(g, 0, AFTER)
            backward(g).wait_recv()
            total = total + filter_rest(g, False, True)
        total = jnp.sum(total, axis=1, keepdims=True) * channels
        power_out[g * GROUP : (g + 1) * GROUP, :] = jnp.broadcast_to(total, (GROUP, LANES))
        if g < groups - 1:
            transform(g, 0, here)
        else:
            for offset in range(1, blocks):
                power_copy(peer_blk(offset), blk).start()
            transform(g, AFTER, here - AFTER)

    power = power_out[...]
    for offset in range(1, blocks):
        r = peer_blk(offset)
        power_copy(r, r).wait_recv()
        power = power + power_in[r]
    scale_ref[...] = 1.0 / jnp.sqrt(power / (here * blocks * channels) + EPS)
    for offset in range(1, blocks):
        power_copy(peer_blk(offset), blk).wait_send()
    for g in range(groups):

        @pl.when(blk < blocks - 1)
        def _():
            forward(g).wait_send()

        backward(g).wait_send()

    def far_rows(k, s):
        return pl.ds(pl.multiple_of((k * here + s) * LANES, LANES), LANES)

    def far_copy(k):
        part = pl.ds(pl.multiple_of(k * here * LANES, here * LANES), here * LANES)
        return pltpu.make_async_remote_copy(
            src_ref=own.at[:, :, part], dst_ref=following.at[:, :, part], send_sem=far_s.at[k], recv_sem=far_r.at[k],
            device_id=(stn, partner), device_id_type=MESH,
        )

    def hand_over(i, carry):
        c = order(0, lax.div(i, quad), lax.div(lax.rem(i, quad), chunk))[1]
        k = c * chunk + lax.rem(i, chunk)
        scale = scale_ref[...]
        for s in range(here):
            for p in range(2):
                own[p, :, far_rows(k, s)] = (work[p, (1 - core) * half + k, s] * scale).astype(BF16)
        far_copy(k).start()
        return carry

    lax.fori_loop(0, half, hand_over, 0)

    def quantize(k):
        far_copy(k).wait_recv()
        scale = scale_ref[...]
        total = jnp.zeros((inputs, LANES), F32)
        for s in range(here):
            for p in range(2):
                value = (work[p, core * half + k, s] * scale).astype(BF16)
                near[k, p, s] = value
                wide = value.astype(F32)
                wider = following[p, :, far_rows(k, s)].astype(F32)
                total = total + (wide * wide + wider * wider)
        self_power[k] = total

    def sample(k, p, t):
        return (near[k, p, t] if t < here else following[p, :, far_rows(k, t - here)]).astype(F32)

    def begin(m, carry):
        gain[m, 0] = jnp.ones((inputs, LANES), F32)
        gain[m, 1] = jnp.zeros((inputs, LANES), F32)
        return carry

    lax.fori_loop(0, quad, begin, 0)

    def back_parts(turn):
        return [(back_wide if turn == 0 else back_narrow).at[n] for n in range(3)]

    def back_copy(turn, c, sender):
        back_out, back_in, _ = back_parts(turn)
        return pltpu.make_async_remote_copy(
            src_ref=back_out.at[c], dst_ref=back_in.at[sender], send_sem=back_s.at[c], recv_sem=back_r.at[sender],
            device_id=(c, blk), device_id_type=MESH,
        )

    def total_copy(turn, c, owner):
        _, _, back_sum = back_parts(turn)
        return pltpu.make_async_remote_copy(
            src_ref=back_sum.at[owner], dst_ref=back_sum.at[owner], send_sem=total_s.at[c], recv_sem=total_r.at[owner],
            device_id=(c, blk), device_id_type=MESH,
        )

    def sum_copy(r, sender, j):
        return pltpu.make_async_remote_copy(
            src_ref=sum_out.at[r, j], dst_ref=sum_in.at[sender, j],
            send_sem=sum_s.at[r, j], recv_sem=sum_r.at[sender, j],
            device_id=(stn, 2 * r + core), device_id_type=MESH,
        )

    places_far_first = sorted(range(1, places), key=lambda o: -min(o, places - o))

    def weight_copy(r, owner, m):
        part = weights.at[owner * quad + m]
        return pltpu.make_async_remote_copy(
            src_ref=part, dst_ref=part, send_sem=weight_s.at[r, m], recv_sem=weight_r.at[owner, m],
            device_id=(stn, 2 * r + core), device_id_type=MESH,
        )

    def norm_copy(turn, c, sender):
        return pltpu.make_async_remote_copy(
            src_ref=norm_out.at[turn], dst_ref=norm_in.at[turn, sender],
            send_sem=norm_s.at[turn, c], recv_sem=norm_r.at[turn, sender],
            device_id=(c, blk), device_id_type=MESH,
        )

    def weight(turn, k, p):
        return model_ref[p] if turn == 0 else weights[k, p].astype(F32)

    def down(turn, k, c, j):
        w_re, w_im = weight(turn, k, 0), weight(turn, k, 1)
        for t in range(spectra):
            q_re, q_im = sample(k, 0, t), sample(k, 1, t)
            rows_ref[t : t + 1, :] = jnp.sum(q_re * w_re + q_im * w_im, axis=0, keepdims=True)
            rows_ref[spectra + t : spectra + t + 1, :] = jnp.sum(q_re * w_im - q_im * w_re, axis=0, keepdims=True)
        back_out = back_parts(turn)[0]
        back_out[c, j] = rows_ref[...].astype(back_out.dtype)

    def up(turn, k, r, j):
        c, jj = lax.div(k, chunk), lax.rem(k, chunk)
        back = back_parts(turn)[2]
        rows_ref[...] = back[c, jj].astype(F32)
        h_re = jnp.zeros((inputs, LANES), F32)
        h_im = jnp.zeros((inputs, LANES), F32)
        for t in range(spectra):
            q_re, q_im = sample(k, 0, t), sample(k, 1, t)
            b_re, b_im = rows_ref[t : t + 1, :], rows_ref[spectra + t : spectra + t + 1, :]
            h_re = h_re + (q_re * b_re - q_im * b_im)
            h_im = h_im + (q_re * b_im + q_im * b_re)
        own_power = self_power[k]
        h_re = h_re - own_power * weight(turn, k, 0)
        h_im = h_im - own_power * weight(turn, k, 1)
        if turn < ITERS - 1:
            sum_out[r, j, 0] = h_re.astype(BF16)
            sum_out[r, j, 1] = h_im.astype(BF16)
        else:
            m_re, m_im = model_ref[0], model_ref[1]
            numer[0, j] = m_re * h_re + m_im * h_im
            numer[1, j] = m_re * h_im - m_im * h_re

    def side_copy(r, sender):
        return pltpu.make_async_remote_copy(
            src_ref=side_out.at[r], dst_ref=side_in.at[sender], send_sem=side_s.at[r], recv_sem=side_r.at[sender],
            device_id=(stn, r), device_id_type=MESH,
        )

    def half_copy(r, sender, q):
        return pltpu.make_async_remote_copy(
            src_ref=half_out.at[r, q], dst_ref=half_in.at[sender, q],
            send_sem=half_s.at[r, q], recv_sem=half_r.at[sender, q],
            device_id=(stn, r), device_id_type=MESH,
        )

    def last_copy(c, sender):
        return pltpu.make_async_remote_copy(
            src_ref=last_out.at[c], dst_ref=last_in.at[sender], send_sem=last_s.at[c], recv_sem=last_r.at[sender],
            device_id=(c, blk), device_id_type=MESH,
        )

    blocks_far_first = sorted(range(1, blocks), key=lambda o: -min(o, blocks - o))

    def by_block(value, n):
        turned[n] = value.reshape(quad * inputs, LANES).T.reshape(stations, blocks, quad * inputs)
        return [turned[n, :, r, :] for r in range(blocks)]

    def add_norms(turn):
        def norms(o, total):
            c = peer_stn(o)
            norm_copy(turn - 1, c, c).wait_recv()
            return total + norm_in[turn - 1, c]

        rows_ref[0:8, :] = lax.fori_loop(1, stations, norms, norm_out[turn - 1])

    def denominator(norm, w_re, w_im):
        return norm - (w_re * w_re + w_im * w_im) + EPS

    def last_side():
        add_norms(ITERS - 1)
        m_re, m_im = model_ref[0], model_ref[1]
        for m in range(quad):
            g_re, g_im = gain[m, 0], gain[m, 1]
            w_re = g_re * m_re - g_im * m_im
            w_im = g_re * m_im + g_im * m_re
            numer[0, m] = 1.0 / denominator(rows_ref[m : m + 1, :], w_re, w_im)
        for n, value in enumerate((gain[:, 0], gain[:, 1], numer[0])):
            for r, part in enumerate(by_block(value, n)):
                side_out[r, n] = part
        for offset in blocks_far_first:
            side_copy(peer_blk(offset), blk).start()
        side_in[blk] = side_out[blk]

    def send_half(q):
        for p in range(2):
            for r, part in enumerate(by_block(numer[p], p)):
                half_out[r, q, p] = part.astype(BF16)
        for offset in blocks_far_first:
            half_copy(peer_blk(offset), blk, q).start()
        half_in[blk, q] = half_out[blk, q]

    for turn in range(ITERS):
        def down_part(o, carry):
            r = order(turn, o, 0)[0]
            def one(n, carry):
                c = order(turn, o, n)[1]

                def each(j, carry):
                    if turn > 0:

                        @pl.when(o > 0)
                        def _():
                            weight_copy(r, r, lax.rem(c * chunk + j, quad)).wait_recv()

                    if turn == 0:
                        quantize(c * chunk + j)
                    down(turn, c * chunk + j, c, j)
                    return carry

                lax.fori_loop(0, chunk, each, 0)

                @pl.when(c != stn)
                def _():
                    back_copy(turn, c, stn).start()

                return carry

            return lax.fori_loop(0, per, one, carry)

        lax.fori_loop(0, places, down_part, 0)

        def await_back(o, carry):
            c = peer_stn(o)
            back_copy(turn, c, c).wait_recv()
            return carry

        if chunk > 1:
            lax.fori_loop(1, stations, await_back, 0)

        def gather(j, carry):
            back_out, back_in, back_sum = back_parts(turn)
            total = back_out[stn, j].astype(F32)

            def more(o, total):
                if chunk == 1:
                    await_back(o, 0)
                return total + back_in[peer_stn(o), j].astype(F32)

            total = lax.fori_loop(1, stations, more, total)
            back_sum[stn, j] = total.astype(back_sum.dtype)
            return carry

        lax.fori_loop(0, chunk, gather, 0)
        for c in far_first():
            total_copy(turn, c, stn).start()
        if turn == ITERS - 1:
            last_side()

        def up_part(o):
            r = peer_place(o)
            for n in range(per):
                c = r * per + n

                @pl.when(c != stn)
                def _():
                    total_copy(turn, c, c).wait_recv()

            def each(j, carry):
                up(turn, r * quad + j, r, j)
                if o > 0 and turn < ITERS - 1:
                    sum_copy(r, place, j).start()
                return carry

            lax.fori_loop(0, quad, each, 0)
            if turn == ITERS - 1:
                send_half(r)

        for o in sorted(range(places), key=lambda o: -min(o, places - o)):
            up_part(o)

        def settle(o, carry):
            c = peer_stn(o)
            back_copy(turn, c, stn).wait_send()
            total_copy(turn, c, stn).wait_send()
            return carry

        lax.fori_loop(1, stations, settle, 0)

        def await_sum(o, carry):
            r = peer_place(o)
            if turn < ITERS - 1:
                for m in range(quad):
                    sum_copy(r, r, m).wait_recv()
            if turn > 0:
                for m in range(quad):
                    weight_copy(r, place, m).wait_send()
            return carry

        lax.fori_loop(1, places, await_sum, 0)

        if turn == ITERS - 1:
            break
        if turn > 0:
            add_norms(turn)

        for m in range(quad):
            k = place * quad + m
            total_re = sum_out[place, m, 0].astype(F32)
            total_im = sum_out[place, m, 1].astype(F32)

            def more(o, totals):
                r = peer_place(o)
                return totals[0] + sum_in[r, m, 0].astype(F32), totals[1] + sum_in[r, m, 1].astype(F32)

            total_re, total_im = lax.fori_loop(1, places, more, (total_re, total_im))
            m_re, m_im = model_ref[0], model_ref[1]
            g_re, g_im = gain[m, 0], gain[m, 1]
            w_re = g_re * m_re - g_im * m_im
            w_im = g_re * m_im + g_im * m_re
            if turn == 0:
                norm = first
            else:
                norm = rows_ref[m : m + 1, :]
            denom = denominator(norm, w_re, w_im)
            new_re = (m_re * total_re + m_im * total_im) / denom
            new_im = (m_re * total_im - m_im * total_re) / denom
            if turn % 2 == 1:
                new_re = (new_re + g_re) * 0.5
                new_im = (new_im + g_im) * 0.5
            gain[m, 0] = new_re
            gain[m, 1] = new_im
            w_re = new_re * m_re - new_im * m_im
            w_im = new_re * m_im + new_im * m_re
            weights[k, 0] = w_re.astype(BF16)
            weights[k, 1] = w_im.astype(BF16)
            for o in places_far_first:
                weight_copy(peer_place(o), place, m).start()
            norm_out[turn, m : m + 1, :] = jnp.sum(w_re * w_re + w_im * w_im, axis=0, keepdims=True)

        for m in range(quad, 8):
            norm_out[turn, m : m + 1, :] = jnp.zeros((1, LANES), F32)
        for c in far_first():
            norm_copy(turn, c, stn).start()

        def sent(o, carry):
            for m in range(quad):
                sum_copy(peer_place(o), place, m).wait_send()
            return carry

        lax.fori_loop(1, places, sent, 0)

    def handed(k, carry):
        far_copy(k).wait_send()
        return carry

    lax.fori_loop(0, half, handed, 0)

    def normed(o, carry):
        for turn in range(ITERS - 1):
            norm_copy(turn, peer_stn(o), stn).wait_send()
        return carry

    lax.fori_loop(1, stations, normed, 0)

    for offset in blocks_far_first:
        r = peer_blk(offset)
        side_copy(r, r).wait_recv()
        for q in range(places):
            half_copy(r, r, q).wait_recv()
    for half_core in range(2):
        for q in range(places):
            owner = 2 * q + half_core
            for p in range(2):
                total = half_in[half_core, q, p].astype(F32)
                for n in range(1, places):
                    total = total + half_in[2 * n + half_core, q, p].astype(F32)
                total = total * side_in[owner, 2]
                if ITERS % 2 == 0:
                    total = (total + side_in[owner, p]) * 0.5
                final[(half_core * places + q) * 2 + p] = total
    for c in range(stations):
        last_out[c] = final[:, c, :]
    for c in far_first():
        last_copy(c, stn).start()
    last_in[stn] = last_out[stn]

    def await_last(o, carry):
        c = peer_stn(o)
        last_copy(c, c).wait_recv()
        return carry

    lax.fori_loop(1, stations, await_last, 0)
    for m in range(quad):
        for n in range(stations // span):
            block = jnp.concatenate(
                [last_in[n * span + i, :, m * inputs : (m + 1) * inputs] for i in range(span)], axis=1
            )
            for half_core in range(2):
                for q in range(places):
                    for p in range(2):
                        k = half_core * half + q * quad + m
                        at = (half_core * places + q) * 2 + p
                        out_ref[p, k : k + 1, n * LANES : (n + 1) * LANES] = block[at : at + 1, :]

    for offset in blocks_far_first:
        r = peer_blk(offset)
        side_copy(r, blk).wait_send()
        for q in range(places):
            half_copy(r, blk, q).wait_send()

    def sent_last(o, carry):
        last_copy(peer_stn(o), stn).wait_send()
        return carry

    lax.fori_loop(1, stations, sent_last, 0)


def correlate(stations, blocks, voltages, high, low, taps, phases):
    inputs, channels = voltages.shape[1], taps.shape[1]
    here = voltages.shape[2] // channels
    groups = inputs // GROUP
    places, half = blocks // 2, RADIX // 2
    chunk, quad = half // stations, half // places
    rows = 4 * here
    hbm = pl.BlockSpec(memory_space=pl.ANY)
    vmem = pl.BlockSpec(memory_space=pltpu.VMEM)
    dma = pltpu.SemaphoreType.DMA
    return pl.pallas_call(
        functools.partial(correlator_kernel, stations, blocks),
        in_specs=[hbm, hbm, hbm, vmem, vmem],
        out_specs=vmem,
        out_shape=jax.ShapeDtypeStruct((2, RADIX, stations * inputs), F32),
        scratch_shapes=[
            pltpu.VMEM((2, inputs, here * channels), BF16),
            pltpu.VMEM((2, inputs, BEFORE * channels), BF16),
            pltpu.VMEM((2, inputs, AFTER * channels), BF16),
            pltpu.VMEM((2, RADIX, here, inputs, LANES), F32),
            pltpu.VMEM(high.shape, BF16),
            pltpu.VMEM(low.shape, BF16),
            pltpu.VMEM((inputs, LANES), F32),
            pltpu.VMEM((blocks, inputs, LANES), F32),
            pltpu.VMEM((inputs, LANES), F32),
            pltpu.VMEM((2, inputs, LANES), F32),
            pltpu.VMEM((half, 2, here, inputs, LANES), BF16),
            pltpu.VMEM((half, 2, inputs, LANES), BF16),
            pltpu.VMEM((half, inputs, LANES), F32),
            pltpu.VMEM((3, stations, chunk, 4 * here, LANES), F32),
            pltpu.VMEM((3, stations, chunk, rows, LANES), BF16),
            pltpu.VMEM((places, quad, 2, inputs, LANES), BF16),
            pltpu.VMEM((places, quad, 2, inputs, LANES), BF16),
            pltpu.VMEM((ITERS - 1, 8, LANES), F32),
            pltpu.VMEM((ITERS - 1, stations, 8, LANES), F32),
            pltpu.VMEM((quad, 2, inputs, LANES), F32),
            pltpu.VMEM((rows, LANES), F32),
            pltpu.VMEM((2, quad, inputs, LANES), F32),
            pltpu.VMEM((3, stations, blocks, quad * inputs), F32),
            pltpu.VMEM((blocks, 3, stations, quad * inputs), F32),
            pltpu.VMEM((blocks, 3, stations, quad * inputs), F32),
            pltpu.VMEM((blocks, places, 2, stations, quad * inputs), BF16),
            pltpu.VMEM((blocks, places, 2, stations, quad * inputs), BF16),
            pltpu.VMEM((4 * places, stations, quad * inputs), F32),
            pltpu.VMEM((stations, 4 * places, quad * inputs), F32),
            pltpu.VMEM((stations, 4 * places, quad * inputs), F32),
            dma((groups,)),
            dma((2,)),
            dma((2, groups)),
            dma((2, groups)),
            dma((blocks,)),
            dma((blocks,)),
            dma((half,)),
            dma((half,)),
            dma((stations,)),
            dma((stations,)),
            dma((stations,)),
            dma((stations,)),
            dma((places, quad)),
            dma((places, quad)),
            dma((places, quad)),
            dma((places, quad)),
            dma((ITERS - 1, stations)),
            dma((ITERS - 1, stations)),
            dma((blocks,)),
            dma((blocks,)),
            dma((blocks, places)),
            dma((blocks, places)),
            dma((stations,)),
            dma((stations,)),
        ],
        compiler_params=pltpu.CompilerParams(
            collective_id=0, has_side_effects=True, vmem_limit_bytes=62 * 2**20
        ),
        name="correlator",
    )(voltages, high, low, taps, phases)


def on_device(stations, blocks, voltages, taps, model_phase):
    high, low = dft_tables(taps.shape[1])
    phases = model_phase.reshape(-1, LANES)
    return correlate(stations, blocks, voltages, jnp.asarray(high), jnp.asarray(low), taps, phases)


def solution(mesh):
    stations, blocks = mesh.shape["stn"], mesh.shape["blk"]
    in_specs = (P(None, "stn", "blk"), P(), P())
    out_specs = P(None, ("stn", "blk"), None)
    return jax.shard_map(
        functools.partial(on_device, stations, blocks),
        mesh=mesh, in_specs=in_specs, out_specs=out_specs, check_vma=False,
    )
```

```python
import functools
import math

import jax
import jax.numpy as jnp
import ml_dtypes
import numpy as np
from jax import lax
from jax.experimental import pallas as pl
from jax.experimental.pallas import tpu as pltpu
from jax.sharding import PartitionSpec as P

ITERS = 4
EPS = 1e-06
TAPS = 16
BEFORE = 7
AFTER = 8
LANES = 128
GROUP = 16
RADIX = 32
F32 = jnp.float32
BF16 = jnp.bfloat16
MESH = pl.DeviceIdType.MESH


def dft_tables(channels):
    b = np.arange(LANES)
    k = np.arange(RADIX)
    turns = (b[None, :, None] * (k[:, None, None] + RADIX * b[None, None, :])) % channels
    angle = -2.0 * np.pi * turns / channels
    cos, sin = np.cos(angle), np.sin(angle)
    table = np.concatenate(
        [np.concatenate([cos, sin], axis=2), np.concatenate([-sin, cos], axis=2)], axis=1
    ).astype(np.float32)
    high = table.astype(ml_dtypes.bfloat16)
    low = (table - high.astype(np.float32)).astype(ml_dtypes.bfloat16)
    return high, low


def times(z, w):
    re, im = z
    c, s = float(w.real), float(w.imag)
    if abs(s) < 1e-12:
        return (re, im) if c > 0 else (-re, -im)
    if abs(c) < 1e-12:
        return (-im, re) if s > 0 else (im, -re)
    if abs(abs(c) - abs(s)) < 1e-12:
        if c > 0 and s < 0:
            return ((re + im) * c, (im - re) * c)
        if c < 0 and s < 0:
            return ((im - re) * -c, (re + im) * c)
    return (re * c - im * s, re * s + im * c)


def add(x, y):
    return (x[0] + y[0], x[1] + y[1])


def sub(x, y):
    return (x[0] - y[0], x[1] - y[1])


def fft(points):
    size = len(points)
    if size == 1:
        return points
    if size == 2:
        return [add(points[0], points[1]), sub(points[0], points[1])]
    if size == 4:
        even = [add(points[0], points[2]), sub(points[0], points[2])]
        odd = [add(points[1], points[3]), sub(points[1], points[3])]
        turned = (odd[1][1], -odd[1][0])
        return [add(even[0], odd[0]), add(even[1], turned), sub(even[0], odd[0]), sub(even[1], turned)]
    if size == 8:
        even, odd = fft(points[0::2]), fft(points[1::2])
        odd = [times(z, np.exp(-2j * np.pi * i / 8)) for i, z in enumerate(odd)]
        return [add(e, o) for e, o in zip(even, odd)] + [sub(e, o) for e, o in zip(even, odd)]
    outer = size // 4
    result = [None] * size
    firsts = []
    for j in range(outer):
        first = fft([points[j + outer * r] for r in range(4)])
        firsts.append([times(z, np.exp(-2j * np.pi * j * u / size)) for u, z in enumerate(first)])
    for u in range(4):
        second = fft([firsts[j][u] for j in range(outer)])
        for v in range(outer):
            result[u + 4 * v] = second[v]
    return result


def correlator_kernel(
    stations, blocks,
    volt_ref, high_hbm, low_hbm, taps_ref, phases_ref,
    out_ref,
    own, prev, following, work, high_ref, low_ref, power_out, power_in, scale_ref, model_ref,
    near, weights, self_power, back_wide, back_narrow, sum_out, sum_in, norm_out, norm_in, gain, rows_ref,
    numer, turned, side_out, side_in, half_out, half_in, final, last_out, last_in,
    own_sem, table_sem, halo_s, halo_r, power_s, power_r, far_s, far_r, back_s, back_r, total_s, total_r,
    sum_s, sum_r, weight_s, weight_r, norm_s, norm_r, side_s, side_r, half_s, half_r, last_s, last_r,
):
    stn, blk = lax.axis_index("stn"), lax.axis_index("blk")
    channels = taps_ref.shape[1]
    inputs = volt_ref.shape[1]
    here = volt_ref.shape[2] // channels
    groups = inputs // GROUP
    core, place = lax.rem(blk, 2), lax.div(blk, 2)
    partner = blk + 1 - 2 * core
    places = blocks // 2
    half = RADIX // 2
    chunk = half // stations
    quad = half // places
    per = quad // chunk
    spectra = 2 * here
    keep = jnp.where(blk == blocks - 1, 0.0, 1.0)

    def peer_stn(offset):
        return lax.rem(stn + offset, stations)

    def peer_blk(offset):
        return lax.rem(blk + offset, blocks)

    def peer_place(offset):
        return lax.rem(place + offset, places)

    side = math.isqrt(stations)
    row_at, column_at = lax.div(stn, side), lax.rem(stn, side)
    ring = [min(d, side - d) for d in range(side)]
    others = sorted(
        ((dy, dz) for dy in range(side) for dz in range(side) if dy or dz), key=lambda d: -ring[d[0]] - ring[d[1]]
    )

    def far_first():
        for dy, dz in others:
            yield lax.rem(row_at + dy, side) * side + lax.rem(column_at + dz, side)

    def order(turn, q, n):
        offset = q + lax.div(q, 2) * (1 - 2 * lax.rem(q, 2)) if places == 4 else q
        if turn == 0:
            offset = offset + row_at
        r = lax.rem(place + offset, places)
        return r, r * per + lax.rem(n + column_at, per)

    barrier = pltpu.get_barrier_semaphore()
    for offset in range(1, stations):
        pl.semaphore_signal(barrier, inc=1, device_id=(peer_stn(offset), blk), device_id_type=MESH)
    for offset in range(1, blocks):
        pl.semaphore_signal(barrier, inc=1, device_id=(stn, peer_blk(offset)), device_id_type=MESH)

    def rows_of(g):
        return pl.ds(pl.multiple_of(g * GROUP, GROUP), GROUP)

    def own_copy(g):
        return pltpu.make_async_copy(volt_ref.at[:, rows_of(g), :], own.at[:, rows_of(g), :], own_sem.at[g])

    def table_copy(n):
        pair = ((high_hbm, high_ref), (low_hbm, low_ref))[n]
        return pltpu.make_async_copy(*pair, table_sem.at[n])

    def forward(g):
        return pltpu.make_async_remote_copy(
            src_ref=volt_ref.at[:, rows_of(g), pl.ds((here - BEFORE) * channels, BEFORE * channels)],
            dst_ref=prev.at[:, rows_of(g), :], send_sem=halo_s.at[0, g], recv_sem=halo_r.at[0, g],
            device_id=(stn, peer_blk(1)), device_id_type=MESH,
        )

    def backward(g):
        return pltpu.make_async_remote_copy(
            src_ref=volt_ref.at[:, rows_of(g), pl.ds(0, AFTER * channels)],
            dst_ref=following.at[:, rows_of(g), :], send_sem=halo_s.at[1, g], recv_sem=halo_r.at[1, g],
            device_id=(stn, peer_blk(blocks - 1)), device_id_type=MESH,
        )

    for g in range(groups):
        own_copy(g).start()
    for n in range(2):
        table_copy(n).start()
    pl.semaphore_wait(barrier, stations + blocks - 2)
    for g in range(groups):

        @pl.when(blk < blocks - 1)
        def _():
            forward(g).start()

        backward(g).start()

    @pl.when(blk == 0)
    def _():
        def clear(j, carry):
            at = pl.ds(pl.multiple_of(j * channels, channels), channels)
            for p in range(2):
                prev[p, :, at] = jnp.zeros((inputs, channels), BF16)
            return carry

        lax.fori_loop(0, BEFORE, clear, 0)

    def tap_rows(start):
        return [taps_ref[k : k + 1, pl.ds(start, LANES)] for k in range(TAPS)]

    def accumulate(sums, source, g, p, start, first, count, rows):
        for j in range(first, first + count):
            at = pl.multiple_of(start + (j - first) * channels, LANES)
            sample = source[p, rows_of(g), pl.ds(at, LANES)].astype(F32)
            for k in range(TAPS):
                u = j - k
                if 0 <= u < here:
                    term = sample * rows[k]
                    sums[u] = term if sums[u] is None else sums[u] + term

    def filter_own(g, carry):
        own_copy(g).wait()

        def part(a, carry):
            start = pl.multiple_of(a * LANES, LANES)
            rows = tap_rows(start)
            for p in range(2):
                sums = [None] * here
                accumulate(sums, own, g, p, start, BEFORE, here, rows)
                for u in range(here):
                    work[p, a, u, rows_of(g), :] = sums[u] if u < here - AFTER else sums[u] * keep
            return carry

        return lax.fori_loop(0, RADIX, part, carry)

    lax.fori_loop(0, groups, filter_own, 0)
    span = LANES // inputs
    row = phases_ref[pl.ds(lax.div(stn, span), 1), :]
    lane = lax.broadcasted_iota(jnp.int32, (inputs, LANES), 1)
    wanted = lax.broadcasted_iota(jnp.int32, (inputs, LANES), 0) + lax.rem(stn, span) * inputs
    phase = jnp.sum(jnp.where(lane == wanted, row, 0.0), axis=1, keepdims=True)
    phase = jnp.broadcast_to(phase, (inputs, LANES))
    model_ref[0] = jnp.cos(phase)
    model_ref[1] = jnp.sin(phase)
    all_re, all_im = jnp.cos(phases_ref[...]), jnp.sin(phases_ref[...])
    first = jnp.sum(all_re * all_re + all_im * all_im)
    rows_ref[...] = jnp.zeros(rows_ref.shape, F32)
    for n in range(2):
        table_copy(n).wait()

    def filter_rest(g, low_half, high_half):
        spots = [u for u in range(here) if (u < AFTER and low_half) or (u >= AFTER and high_half)]

        def part(a, total):
            start = pl.multiple_of(a * LANES, LANES)
            rows = tap_rows(start)
            for p in range(2):
                sums = [work[p, a, u, rows_of(g), :] if u in spots else None for u in range(here)]
                if low_half:
                    accumulate(sums, prev, g, p, start, 0, BEFORE, rows)
                if high_half:
                    accumulate(sums, following, g, p, start, BEFORE + here, AFTER, rows)
                for u in spots:
                    work[p, a, u, rows_of(g), :] = sums[u]
                    total = total + sums[u] * sums[u]
            return total

        return lax.fori_loop(0, RADIX, part, jnp.zeros((GROUP, LANES), F32))

    def transform(g, first_spot, count):
        def turn(s, carry):
            for part in range(GROUP // 8):
                rows = pl.ds(g * GROUP + 8 * part, 8)
                points = [(work[0, a, s, rows, :], work[1, a, s, rows, :]) for a in range(RADIX)]
                for k, (re, im) in enumerate(fft(points)):
                    work[0, k, s, rows, :] = re
                    work[1, k, s, rows, :] = im
            return carry

        lax.fori_loop(first_spot, first_spot + count, turn, 0)

        def second(k, carry):
            spots = pl.ds(first_spot, count)
            both = jnp.concatenate(
                [work[p, k, spots, rows_of(g), :].reshape(count * GROUP, LANES) for p in range(2)], axis=1
            )
            high = both.astype(BF16)
            low = (both - high.astype(F32)).astype(BF16)
            table = high_ref[k]
            out = jnp.dot(
                jnp.concatenate([high, low, high], axis=1),
                jnp.concatenate([table, table, low_ref[k]], axis=0),
                preferred_element_type=F32,
            )
            out = out.reshape(count, GROUP, 2 * LANES)
            work[0, k, spots, rows_of(g), :] = out[:, :, :LANES]
            work[1, k, spots, rows_of(g), :] = out[:, :, LANES:]
            return carry

        lax.fori_loop(0, RADIX, second, 0, unroll=16)

    def await_prev(g):
        @pl.when(blk > 0)
        def _():
            forward(g).wait_recv()

    def power_copy(r, sender):
        return pltpu.make_async_remote_copy(
            src_ref=power_out, dst_ref=power_in.at[sender], send_sem=power_s.at[r], recv_sem=power_r.at[sender],
            device_id=(stn, r), device_id_type=MESH,
        )

    for g in range(groups):
        await_prev(g)
        if g < groups - 1:
            backward(g).wait_recv()
            total = filter_rest(g, True, True)
        else:
            total = filter_rest(g, True, False)
            transform(g, 0, AFTER)
            backward(g).wait_recv()
            total = total + filter_rest(g, False, True)
        total = jnp.sum(total, axis=1, keepdims=True) * channels
        power_out[g * GROUP : (g + 1) * GROUP, :] = jnp.broadcast_to(total, (GROUP, LANES))
        if g < groups - 1:
            transform(g, 0, here)
        else:
            for offset in range(1, blocks):
                power_copy(peer_blk(offset), blk).start()
            transform(g, AFTER, here - AFTER)

    power = power_out[...]
    for offset in range(1, blocks):
        r = peer_blk(offset)
        power_copy(r, r).wait_recv()
        power = power + power_in[r]
    scale_ref[...] = 1.0 / jnp.sqrt(power / (here * blocks * channels) + EPS)
    for offset in range(1, blocks):
        power_copy(peer_blk(offset), blk).wait_send()
    for g in range(groups):

        @pl.when(blk < blocks - 1)
        def _():
            forward(g).wait_send()

        backward(g).wait_send()

    def far_rows(k, s):
        return pl.ds(pl.multiple_of((k * here + s) * LANES, LANES), LANES)

    def far_copy(k):
        part = pl.ds(pl.multiple_of(k * here * LANES, here * LANES), here * LANES)
        return pltpu.make_async_remote_copy(
            src_ref=own.at[:, :, part], dst_ref=following.at[:, :, part], send_sem=far_s.at[k], recv_sem=far_r.at[k],
            device_id=(stn, partner), device_id_type=MESH,
        )

    def hand_over(i, carry):
        c = order(0, lax.div(i, quad), lax.div(lax.rem(i, quad), chunk))[1]
        k = c * chunk + lax.rem(i, chunk)
        scale = scale_ref[...]
        for s in range(here):
            for p in range(2):
                own[p, :, far_rows(k, s)] = (work[p, (1 - core) * half + k, s] * scale).astype(BF16)
        far_copy(k).start()
        return carry

    lax.fori_loop(0, half, hand_over, 0)

    def quantize(k):
        far_copy(k).wait_recv()
        scale = scale_ref[...]
        total = jnp.zeros((inputs, LANES), F32)
        for s in range(here):
            for p in range(2):
                value = (work[p, core * half + k, s] * scale).astype(BF16)
                near[k, p, s] = value
                wide = value.astype(F32)
                wider = following[p, :, far_rows(k, s)].astype(F32)
                total = total + (wide * wide + wider * wider)
        self_power[k] = total

    def sample(k, p, t):
        return (near[k, p, t] if t < here else following[p, :, far_rows(k, t - here)]).astype(F32)

    def begin(m, carry):
        gain[m, 0] = jnp.ones((inputs, LANES), F32)
        gain[m, 1] = jnp.zeros((inputs, LANES), F32)
        return carry

    lax.fori_loop(0, quad, begin, 0)

    def back_parts(turn):
        return [(back_wide if turn == 0 else back_narrow).at[n] for n in range(3)]

    def back_copy(turn, c, sender):
        back_out, back_in, _ = back_parts(turn)
        return pltpu.make_async_remote_copy(
            src_ref=back_out.at[c], dst_ref=back_in.at[sender], send_sem=back_s.at[c], recv_sem=back_r.at[sender],
            device_id=(c, blk), device_id_type=MESH,
        )

    def total_copy(turn, c, owner):
        _, _, back_sum = back_parts(turn)
        return pltpu.make_async_remote_copy(
            src_ref=back_sum.at[owner], dst_ref=back_sum.at[owner], send_sem=total_s.at[c], recv_sem=total_r.at[owner],
            device_id=(c, blk), device_id_type=MESH,
        )

    def sum_copy(r, sender, j):
        return pltpu.make_async_remote_copy(
            src_ref=sum_out.at[r, j], dst_ref=sum_in.at[sender, j],
            send_sem=sum_s.at[r, j], recv_sem=sum_r.at[sender, j],
            device_id=(stn, 2 * r + core), device_id_type=MESH,
        )

    places_far_first = sorted(range(1, places), key=lambda o: -min(o, places - o))

    def weight_copy(r, owner, m):
        part = weights.at[owner * quad + m]
        return pltpu.make_async_remote_copy(
            src_ref=part, dst_ref=part, send_sem=weight_s.at[r, m], recv_sem=weight_r.at[owner, m],
            device_id=(stn, 2 * r + core), device_id_type=MESH,
        )

    def norm_copy(turn, c, sender):
        return pltpu.make_async_remote_copy(
            src_ref=norm_out.at[turn], dst_ref=norm_in.at[turn, sender],
            send_sem=norm_s.at[turn, c], recv_sem=norm_r.at[turn, sender],
            device_id=(c, blk), device_id_type=MESH,
        )

    def weight(turn, k, p):
        return model_ref[p] if turn == 0 else weights[k, p].astype(F32)

    def down(turn, k, c, j):
        w_re, w_im = weight(turn, k, 0), weight(turn, k, 1)
        for t in range(spectra):
            q_re, q_im = sample(k, 0, t), sample(k, 1, t)
            rows_ref[t : t + 1, :] = jnp.sum(q_re * w_re + q_im * w_im, axis=0, keepdims=True)
            rows_ref[spectra + t : spectra + t + 1, :] = jnp.sum(q_re * w_im - q_im * w_re, axis=0, keepdims=True)
        back_out = back_parts(turn)[0]
        back_out[c, j] = rows_ref[...].astype(back_out.dtype)

    def up(turn, k, r, j):
        c, jj = lax.div(k, chunk), lax.rem(k, chunk)
        back = back_parts(turn)[2]
        rows_ref[...] = back[c, jj].astype(F32)
        h_re = jnp.zeros((inputs, LANES), F32)
        h_im = jnp.zeros((inputs, LANES), F32)
        for t in range(spectra):
            q_re, q_im = sample(k, 0, t), sample(k, 1, t)
            b_re, b_im = rows_ref[t : t + 1, :], rows_ref[spectra + t : spectra + t + 1, :]
            h_re = h_re + (q_re * b_re - q_im * b_im)
            h_im = h_im + (q_re * b_im + q_im * b_re)
        own_power = self_power[k]
        h_re = h_re - own_power * weight(turn, k, 0)
        h_im = h_im - own_power * weight(turn, k, 1)
        if turn < ITERS - 1:
            sum_out[r, j, 0] = h_re.astype(BF16)
            sum_out[r, j, 1] = h_im.astype(BF16)
        else:
            m_re, m_im = model_ref[0], model_ref[1]
            numer[0, j] = m_re * h_re + m_im * h_im
            numer[1, j] = m_re * h_im - m_im * h_re

    def side_copy(r, sender):
        return pltpu.make_async_remote_copy(
            src_ref=side_out.at[r], dst_ref=side_in.at[sender], send_sem=side_s.at[r], recv_sem=side_r.at[sender],
            device_id=(stn, r), device_id_type=MESH,
        )

    def half_copy(r, sender, q):
        return pltpu.make_async_remote_copy(
            src_ref=half_out.at[r, q], dst_ref=half_in.at[sender, q],
            send_sem=half_s.at[r, q], recv_sem=half_r.at[sender, q],
            device_id=(stn, r), device_id_type=MESH,
        )

    def last_copy(c, sender):
        return pltpu.make_async_remote_copy(
            src_ref=last_out.at[c], dst_ref=last_in.at[sender], send_sem=last_s.at[c], recv_sem=last_r.at[sender],
            device_id=(c, blk), device_id_type=MESH,
        )

    blocks_far_first = sorted(range(1, blocks), key=lambda o: -min(o, blocks - o))

    def by_block(value, n):
        turned[n] = value.reshape(quad * inputs, LANES).T.reshape(stations, blocks, quad * inputs)
        return [turned[n, :, r, :] for r in range(blocks)]

    def add_norms(turn):
        def norms(o, total):
            c = peer_stn(o)
            norm_copy(turn - 1, c, c).wait_recv()
            return total + norm_in[turn - 1, c]

        rows_ref[0:8, :] = lax.fori_loop(1, stations, norms, norm_out[turn - 1])

    def denominator(norm, w_re, w_im):
        return norm - (w_re * w_re + w_im * w_im) + EPS

    def last_side():
        add_norms(ITERS - 1)
        m_re, m_im = model_ref[0], model_ref[1]
        for m in range(quad):
            g_re, g_im = gain[m, 0], gain[m, 1]
            w_re = g_re * m_re - g_im * m_im
            w_im = g_re * m_im + g_im * m_re
            numer[0, m] = 1.0 / denominator(rows_ref[m : m + 1, :], w_re, w_im)
        for n, value in enumerate((gain[:, 0], gain[:, 1], numer[0])):
            for r, part in enumerate(by_block(value, n)):
                side_out[r, n] = part
        for offset in blocks_far_first:
            side_copy(peer_blk(offset), blk).start()
        side_in[blk] = side_out[blk]

    def send_half(q):
        for p in range(2):
            for r, part in enumerate(by_block(numer[p], p)):
                half_out[r, q, p] = part.astype(BF16)
        for offset in blocks_far_first:
            half_copy(peer_blk(offset), blk, q).start()
        half_in[blk, q] = half_out[blk, q]

    for turn in range(ITERS):
        def down_part(o, carry):
            r = order(turn, o, 0)[0]
            def one(n, carry):
                c = order(turn, o, n)[1]

                def each(j, carry):
                    if turn > 0:

                        @pl.when(o > 0)
                        def _():
                            weight_copy(r, r, lax.rem(c * chunk + j, quad)).wait_recv()

                    if turn == 0:
                        quantize(c * chunk + j)
                    down(turn, c * chunk + j, c, j)
                    return carry

                lax.fori_loop(0, chunk, each, 0)

                @pl.when(c != stn)
                def _():
                    back_copy(turn, c, stn).start()

                return carry

            return lax.fori_loop(0, per, one, carry)

        lax.fori_loop(0, places, down_part, 0)

        def await_back(o, carry):
            c = peer_stn(o)
            back_copy(turn, c, c).wait_recv()
            return carry

        if chunk > 1:
            lax.fori_loop(1, stations, await_back, 0)

        def gather(j, carry):
            back_out, back_in, back_sum = back_parts(turn)
            total = back_out[stn, j].astype(F32)

            def more(o, total):
                if chunk == 1:
                    await_back(o, 0)
                return total + back_in[peer_stn(o), j].astype(F32)

            total = lax.fori_loop(1, stations, more, total)
            back_sum[stn, j] = total.astype(back_sum.dtype)
            return carry

        lax.fori_loop(0, chunk, gather, 0)
        for c in far_first():
            total_copy(turn, c, stn).start()
        if turn == ITERS - 1:
            last_side()

        def up_part(o):
            r = peer_place(o)
            for n in range(per):
                c = r * per + n

                @pl.when(c != stn)
                def _():
                    total_copy(turn, c, c).wait_recv()

            def each(j, carry):
                up(turn, r * quad + j, r, j)
                if o > 0 and turn < ITERS - 1:
                    sum_copy(r, place, j).start()
                return carry

            lax.fori_loop(0, quad, each, 0)
            if turn == ITERS - 1:
                send_half(r)

        for o in sorted(range(places), key=lambda o: -min(o, places - o)):
            up_part(o)

        def settle(o, carry):
            c = peer_stn(o)
            back_copy(turn, c, stn).wait_send()
            total_copy(turn, c, stn).wait_send()
            return carry

        lax.fori_loop(1, stations, settle, 0)

        def await_sum(o, carry):
            r = peer_place(o)
            if turn < ITERS - 1:
                for m in range(quad):
                    sum_copy(r, r, m).wait_recv()
            if turn > 0:
                for m in range(quad):
                    weight_copy(r, place, m).wait_send()
            return carry

        lax.fori_loop(1, places, await_sum, 0)

        if turn == ITERS - 1:
            break
        if turn > 0:
            add_norms(turn)

        for m in range(quad):
            k = place * quad + m
            total_re = sum_out[place, m, 0].astype(F32)
            total_im = sum_out[place, m, 1].astype(F32)

            def more(o, totals):
                r = peer_place(o)
                return totals[0] + sum_in[r, m, 0].astype(F32), totals[1] + sum_in[r, m, 1].astype(F32)

            total_re, total_im = lax.fori_loop(1, places, more, (total_re, total_im))
            m_re, m_im = model_ref[0], model_ref[1]
            g_re, g_im = gain[m, 0], gain[m, 1]
            w_re = g_re * m_re - g_im * m_im
            w_im = g_re * m_im + g_im * m_re
            if turn == 0:
                norm = first
            else:
                norm = rows_ref[m : m + 1, :]
            denom = denominator(norm, w_re, w_im)
            new_re = (m_re * total_re + m_im * total_im) / denom
            new_im = (m_re * total_im - m_im * total_re) / denom
            if turn % 2 == 1:
                new_re = (new_re + g_re) * 0.5
                new_im = (new_im + g_im) * 0.5
            gain[m, 0] = new_re
            gain[m, 1] = new_im
            w_re = new_re * m_re - new_im * m_im
            w_im = new_re * m_im + new_im * m_re
            weights[k, 0] = w_re.astype(BF16)
            weights[k, 1] = w_im.astype(BF16)
            for o in places_far_first:
                weight_copy(peer_place(o), place, m).start()
            norm_out[turn, m : m + 1, :] = jnp.sum(w_re * w_re + w_im * w_im, axis=0, keepdims=True)

        for m in range(quad, 8):
            norm_out[turn, m : m + 1, :] = jnp.zeros((1, LANES), F32)
        for c in far_first():
            norm_copy(turn, c, stn).start()

        def sent(o, carry):
            for m in range(quad):
                sum_copy(peer_place(o), place, m).wait_send()
            return carry

        lax.fori_loop(1, places, sent, 0)

    def handed(k, carry):
        far_copy(k).wait_send()
        return carry

    lax.fori_loop(0, half, handed, 0)

    def normed(o, carry):
        for turn in range(ITERS - 1):
            norm_copy(turn, peer_stn(o), stn).wait_send()
        return carry

    lax.fori_loop(1, stations, normed, 0)

    for offset in blocks_far_first:
        r = peer_blk(offset)
        side_copy(r, r).wait_recv()
        for q in range(places):
            half_copy(r, r, q).wait_recv()
    for half_core in range(2):
        for q in range(places):
            owner = 2 * q + half_core
            for p in range(2):
                total = half_in[half_core, q, p].astype(F32)
                for n in range(1, places):
                    total = total + half_in[2 * n + half_core, q, p].astype(F32)
                total = total * side_in[owner, 2]
                if ITERS % 2 == 0:
                    total = (total + side_in[owner, p]) * 0.5
                final[(half_core * places + q) * 2 + p] = total
    for c in range(stations):
        last_out[c] = final[:, c, :]
    for c in far_first():
        last_copy(c, stn).start()
    last_in[stn] = last_out[stn]

    def await_last(o, carry):
        c = peer_stn(o)
        last_copy(c, c).wait_recv()
        return carry

    lax.fori_loop(1, stations, await_last, 0)
    for m in range(quad):
        for n in range(stations // span):
            block = jnp.concatenate(
                [last_in[n * span + i, :, m * inputs : (m + 1) * inputs] for i in range(span)], axis=1
            )
            for half_core in range(2):
                for q in range(places):
                    for p in range(2):
                        k = half_core * half + q * quad + m
                        at = (half_core * places + q) * 2 + p
                        out_ref[p, k : k + 1, n * LANES : (n + 1) * LANES] = block[at : at + 1, :]

    for offset in blocks_far_first:
        r = peer_blk(offset)
        side_copy(r, blk).wait_send()
        for q in range(places):
            half_copy(r, blk, q).wait_send()

    def sent_last(o, carry):
        last_copy(peer_stn(o), stn).wait_send()
        return carry

    lax.fori_loop(1, stations, sent_last, 0)


def correlate(stations, blocks, voltages, high, low, taps, phases):
    inputs, channels = voltages.shape[1], taps.shape[1]
    here = voltages.shape[2] // channels
    groups = inputs // GROUP
    places, half = blocks // 2, RADIX // 2
    chunk, quad = half // stations, half // places
    rows = 4 * here
    hbm = pl.BlockSpec(memory_space=pl.ANY)
    vmem = pl.BlockSpec(memory_space=pltpu.VMEM)
    dma = pltpu.SemaphoreType.DMA
    return pl.pallas_call(
        functools.partial(correlator_kernel, stations, blocks),
        in_specs=[hbm, hbm, hbm, vmem, vmem],
        out_specs=vmem,
        out_shape=jax.ShapeDtypeStruct((2, RADIX, stations * inputs), F32),
        scratch_shapes=[
            pltpu.VMEM((2, inputs, here * channels), BF16),
            pltpu.VMEM((2, inputs, BEFORE * channels), BF16),
            pltpu.VMEM((2, inputs, AFTER * channels), BF16),
            pltpu.VMEM((2, RADIX, here, inputs, LANES), F32),
            pltpu.VMEM(high.shape, BF16),
            pltpu.VMEM(low.shape, BF16),
            pltpu.VMEM((inputs, LANES), F32),
            pltpu.VMEM((blocks, inputs, LANES), F32),
            pltpu.VMEM((inputs, LANES), F32),
            pltpu.VMEM((2, inputs, LANES), F32),
            pltpu.VMEM((half, 2, here, inputs, LANES), BF16),
            pltpu.VMEM((half, 2, inputs, LANES), BF16),
            pltpu.VMEM((half, inputs, LANES), F32),
            pltpu.VMEM((3, stations, chunk, 4 * here, LANES), F32),
            pltpu.VMEM((3, stations, chunk, rows, LANES), BF16),
            pltpu.VMEM((places, quad, 2, inputs, LANES), BF16),
            pltpu.VMEM((places, quad, 2, inputs, LANES), BF16),
            pltpu.VMEM((ITERS - 1, 8, LANES), F32),
            pltpu.VMEM((ITERS - 1, stations, 8, LANES), F32),
            pltpu.VMEM((quad, 2, inputs, LANES), F32),
            pltpu.VMEM((rows, LANES), F32),
            pltpu.VMEM((2, quad, inputs, LANES), F32),
            pltpu.VMEM((3, stations, blocks, quad * inputs), F32),
            pltpu.VMEM((blocks, 3, stations, quad * inputs), F32),
            pltpu.VMEM((blocks, 3, stations, quad * inputs), F32),
            pltpu.VMEM((blocks, places, 2, stations, quad * inputs), BF16),
            pltpu.VMEM((blocks, places, 2, stations, quad * inputs), BF16),
            pltpu.VMEM((4 * places, stations, quad * inputs), F32),
            pltpu.VMEM((stations, 4 * places, quad * inputs), F32),
            pltpu.VMEM((stations, 4 * places, quad * inputs), F32),
            dma((groups,)),
            dma((2,)),
            dma((2, groups)),
            dma((2, groups)),
            dma((blocks,)),
            dma((blocks,)),
            dma((half,)),
            dma((half,)),
            dma((stations,)),
            dma((stations,)),
            dma((stations,)),
            dma((stations,)),
            dma((places, quad)),
            dma((places, quad)),
            dma((places, quad)),
            dma((places, quad)),
            dma((ITERS - 1, stations)),
            dma((ITERS - 1, stations)),
            dma((blocks,)),
            dma((blocks,)),
            dma((blocks, places)),
            dma((blocks, places)),
            dma((stations,)),
            dma((stations,)),
        ],
        compiler_params=pltpu.CompilerParams(
            collective_id=0, has_side_effects=True, vmem_limit_bytes=62 * 2**20
        ),
        name="correlator",
    )(voltages, high, low, taps, phases)


def on_device(stations, blocks, voltages, taps, model_phase):
    high, low = dft_tables(taps.shape[1])
    phases = model_phase.reshape(-1, LANES)
    return correlate(stations, blocks, voltages, jnp.asarray(high), jnp.asarray(low), taps, phases)


def solution(mesh):
    stations, blocks = mesh.shape["stn"], mesh.shape["blk"]
    in_specs = (P(None, "stn", "blk"), P(), P())
    out_specs = P(None, ("stn", "blk"), None)
    return jax.shard_map(
        functools.partial(on_device, stations, blocks),
        mesh=mesh, in_specs=in_specs, out_specs=out_specs, check_vma=False,
    )
```
